32 devices in a mesh: pairs: 16 (over z, y, x), heads: 2 (over core).
Axes of the slice: x: 2, y: 2, z: 4, core: 2. Of those that a mesh axis runs over, the one named last changes fastest.
Arguments:
- tokens: bfloat16 [64, 280, 768], P(('pairs', 'heads')), may hold values from -6 to 6
- cotangent: bfloat16 [64, 280, 768], P(('pairs', 'heads')), may hold values from -6 to 6
- text_len: int32 [64], P('pairs'), may hold values from 6 to 40, as said below
- word_mask: int32 [64, 40], P(('pairs', 'heads')), may hold values from 0 to 1, as said below
- attn_gain: float32 [768], replicated, may hold values from 0.1 to 1.9
- attn_shift: float32 [768], replicated, may hold values from -1.5 to 1.5
- w_qkv: bfloat16 [3, 768, 768], P(None, None, 'heads'), may hold values from -0.21875 to 0.21875
- qv_bias: float32 [2, 768], P(None, 'heads'), may hold values from -2.5 to 2.5
- w_out: bfloat16 [768, 768], replicated, may hold values from -0.875 to 0.875
- out_bias: float32 [768], replicated, may hold values from -1.5 to 1.5
- mlp_gain: float32 [768], replicated, may hold values from 0.1 to 1.9
- mlp_shift: float32 [768], replicated, may hold values from -1.5 to 1.5
- w_up: bfloat16 [768, 3072], P(None, 'heads'), may hold values from -0.21875 to 0.21875
- up_bias: bfloat16 [3072], P('heads'), may hold values from -2.5 to 2.5
- w_down: bfloat16 [3072, 768], P('heads'), may hold values from -0.109375 to 0.109375
- down_bias: float32 [768], replicated, may hold values from -1.5 to 1.5
Outputs:
- layer_out: bfloat16 [64, 280, 768], P(('pairs', 'heads'))
- grad_tokens: float32 [64, 280, 768], P(('pairs', 'heads'))
- grad_attn_gain: float32 [768], P(('pairs', 'heads'))
- grad_attn_shift: float32 [768], P(('pairs', 'heads'))
- grad_w_qkv: float32 [3, 768, 768], P(None, 'pairs', 'heads')
- grad_qv_bias: float32 [2, 768], P(None, ('pairs', 'heads'))
- grad_w_out: float32 [768, 768], P(('pairs', 'heads'))
- grad_out_bias: float32 [768], P(('pairs', 'heads'))
- grad_mlp_gain: float32 [768], P(('pairs', 'heads'))
- grad_mlp_shift: float32 [768], P(('pairs', 'heads'))
- grad_w_up: float32 [768, 3072], P('pairs', 'heads')
- grad_up_bias: float32 [3072], P(('pairs', 'heads'))
- grad_w_down: float32 [3072, 768], P('heads', 'pairs')
- grad_down_bias: float32 [768], P(('pairs', 'heads'))
The draws below stay inside these ranges and needn't reach their ends.
Inputs may be any that keep to these rules, and one draw needn't show every extreme that they name: `text_len`: every caption has 6 to 40 live word slots; some caption has 40. `word_mask`: 1 only at word slots below the caption's text_len; the number of masked slots varies widely from caption to caption.
All inputs are finite; a program needn't handle non-finite values.
Results may differ from the reference program's by a relative error of at most 0.014.
Values may be sent and summed in bfloat16 or wider, within the bound.
No kernel may reach another device: no remote copies, remote signals or barrier semaphores. Data moves between devices by JAX's collectives and lax.ppermute only.
A program may use at most 192 MiB of HBM per device.

```python
import math
import jax
import jax.numpy as jnp
from jax import lax

D = 768
HEAD_COUNT = 12
HEAD_DIM = 64
FF = 3072
WORDS = 40
SEQ = 280
BATCH = 64


def make_lengths(key):
    lengths = jax.random.randint(jax.random.fold_in(key, 7), (BATCH,), 6, WORDS + 1)
    return lengths.at[0].set(WORDS).at[1].set(6)


def draw_text_len(key, part):
    return make_lengths(key).astype(jnp.int32)


def draw_word_mask(key, part):
    lengths = make_lengths(key)
    level = jax.random.randint(jax.random.fold_in(key, 11), (BATCH,), 0, 4)
    upper = jnp.left_shift(jnp.ones((BATCH,), jnp.int32), level + 1)
    counts = jax.random.randint(jax.random.fold_in(key, 13), (BATCH,), 0, upper + 1)
    counts = jnp.minimum(counts, lengths)
    position = jnp.arange(WORDS, dtype=jnp.int32)
    ranking = jax.random.randint(jax.random.fold_in(key, 17), (BATCH, WORDS), 0, 1048576) * 64 + position[None, :]
    ranking = ranking + (position[None, :] >= lengths[:, None]).astype(jnp.int32) * 134217728
    order = jnp.argsort(jnp.argsort(ranking, axis=1), axis=1)
    return (order < counts[:, None]).astype(jnp.int32)


def steps_of(stream_key, shape, split, smallest, top_value):
    factor_of, own = 1.0, jax.random.fold_in(stream_key, 6)
    for axis_at, blocks in split:
        heights = jnp.exp(jax.random.uniform(jax.random.fold_in(own, axis_at), (blocks,), jnp.float32, smallest / len(split), top_value / len(split)))
        factor_of = factor_of * jnp.repeat(heights, shape[axis_at] // blocks).reshape([-1 if axis == axis_at else 1 for axis in range(len(shape))])
    return factor_of


def scatter_about(rng, extent, spread, bound, pieces=(), held_as=jnp.bfloat16):
    values = jax.random.normal(rng, extent, jnp.float32) * spread
    if len(pieces) > 0:
        values = steps_of(rng, extent, pieces, -0.22, 0.18) * values
    return jnp.clip(values, min=-bound, max=bound).astype(held_as)


def setup_inputs(seed: int = 0) -> dict:
    splits = jax.random.split(jax.random.key(seed), 17)
    tokens = scatter_about(splits[0], (BATCH, SEQ, D), 1.0, 6.0, ((0, 32),))
    cotangent = scatter_about(splits[1], (BATCH, SEQ, D), 1.0, 6.0, ((0, 32),))
    text_len = draw_text_len(jax.random.fold_in(splits[16], 71), 0)
    word_mask = draw_word_mask(jax.random.fold_in(splits[16], 71), 0)
    attn_gain = jnp.clip(1.0 + 0.18 * jax.random.normal(splits[4], (D,), jnp.float32), 0.1, 1.9)
    attn_shift = scatter_about(splits[5], (D,), 0.3, 1.5, (), jnp.float32)
    w_qkv = scatter_about(splits[6], (3, D, D), D ** -0.5, 0.21875, ((2, 2),))
    qv_bias = scatter_about(splits[7], (2, D), 0.5, 2.5, ((1, 2),), jnp.float32)
    w_out = scatter_about(splits[8], (D, D), (D // 16) ** -0.5, 0.875)
    out_bias = scatter_about(splits[9], (D,), 0.3, 1.5, (), jnp.float32)
    mlp_gain = jnp.clip(1.0 + 0.18 * jax.random.normal(splits[10], (D,), jnp.float32), 0.1, 1.9)
    mlp_shift = scatter_about(splits[11], (D,), 0.3, 1.5, (), jnp.float32)
    w_up = scatter_about(splits[12], (D, FF), D ** -0.5, 0.21875, ((1, 2),))
    up_bias = scatter_about(splits[13], (FF,), 0.5, 2.5, ((0, 2),))
    w_down = scatter_about(splits[14], (FF, D), FF ** -0.5, 0.109375, ((0, 2),))
    down_bias = scatter_about(splits[15], (D,), 0.3, 1.5, (), jnp.float32)
    return dict(tokens=tokens, cotangent=cotangent, text_len=text_len, word_mask=word_mask, attn_gain=attn_gain, attn_shift=attn_shift, w_qkv=w_qkv, qv_bias=qv_bias, w_out=w_out, out_bias=out_bias, mlp_gain=mlp_gain, mlp_shift=mlp_shift, w_up=w_up, up_bias=up_bias, w_down=w_down, down_bias=down_bias)


@jax.custom_vjp
def low(v):
    return lax.optimization_barrier(v.astype(jnp.bfloat16)).astype(jnp.float32)

@jax.custom_vjp
def low_back(v):
    return v

def low_keep(v):
    return (low(v), None)

def low_pass(kept, grad):
    return (grad,)

def back_keep(v):
    return (v, None)

def back_low(kept, grad):
    return (low(grad),)
low.defvjp(low_keep, low_pass)
low_back.defvjp(back_keep, back_low)
highest = lax.Precision.HIGHEST
epsilon = 1e-06
masked_score = -1000000000.0

def layer_norm(rows, gain_vec, shift_vec):
    mean_val = lax.optimization_barrier(jnp.mean(rows, axis=-1, keepdims=True))
    centred = rows - mean_val
    inv_std = lax.rsqrt(lax.optimization_barrier(jnp.mean(centred * centred, axis=-1, keepdims=True)) + epsilon)
    return centred * inv_std * gain_vec + shift_vec

def forward(tok_rows, lengths, params):
    attn_gain, attn_shift, w_qkv, qv_bias, w_out, out_bias, mlp_gain, mlp_shift, w_up, up_bias, w_down, down_bias = params
    group, seq_len, width = tok_rows.shape
    head_shape = (group, seq_len, HEAD_COUNT, HEAD_DIM)
    normed = low(layer_norm(tok_rows, attn_gain, attn_shift))
    proj = jnp.einsum('nsd,tdc->tnsc', normed, w_qkv, precision=highest)
    queries = low(low_back(proj[0] + qv_bias[0])).reshape(head_shape)
    key_rows = low(low_back(proj[1])).reshape(head_shape)
    values = low(low_back(proj[2] + qv_bias[1])).reshape(head_shape)
    scale = 1.0 / math.sqrt(HEAD_DIM)
    scores = jnp.einsum('nqhe,nkhe->nhqk', queries, key_rows, precision=highest) * scale
    position = jnp.arange(seq_len, dtype=jnp.int32)
    key_ok = (position[None, :] >= WORDS) | (position[None, :] < lengths[:, None])
    scores = low_back(jnp.where(key_ok[:, None, None, :], scores, masked_score))
    probs = low(jax.nn.softmax(scores, axis=-1))
    context = jnp.einsum('nhqk,nkhe->nqhe', probs, values, precision=highest).reshape(group, seq_len, width)
    context = low(low_back(context))
    attn_out = low_back(jnp.einsum('nsc,cd->nsd', context, w_out, precision=highest) + out_bias)
    resid = tok_rows + attn_out
    mlp_in = low(layer_norm(resid, mlp_gain, mlp_shift))
    hidden_pre = low_back(jnp.einsum('nsd,df->nsf', mlp_in, w_up, precision=highest) + up_bias)
    activated = low(jax.nn.gelu(hidden_pre, approximate=False))
    mlp_out = low_back(jnp.einsum('nsf,fd->nsd', activated, w_down, precision=highest) + down_bias)
    return resid + mlp_out

def reference(tokens, cotangent, text_len, word_mask, attn_gain, attn_shift, w_qkv, qv_bias, w_out, out_bias, mlp_gain, mlp_shift, w_up, up_bias, w_down, down_bias):
    params = tuple((item.astype(jnp.float32) for item in (attn_gain, attn_shift, w_qkv, qv_bias, w_out, out_bias, mlp_gain, mlp_shift, w_up, up_bias, w_down, down_bias)))
    group = 8
    blocks = BATCH // group
    tok_blocks = tokens.astype(jnp.float32).reshape(blocks, group, SEQ, D)
    keep = jnp.concatenate([word_mask.astype(jnp.float32), jnp.ones((BATCH, SEQ - WORDS), jnp.float32)], axis=1)
    cot_blocks = (cotangent.astype(jnp.float32) * keep[:, :, None]).reshape(blocks, group, SEQ, D)
    len_blocks = text_len.reshape(blocks, group)
    zero_grads = tuple((jnp.zeros_like(item) for item in params))

    def one_block(carry, block):
        tok_rows, cot_rows, lengths = block

        def inner(rows, weights):
            return forward(rows, lengths, weights)
        result, pullback = jax.vjp(inner, tok_rows, params)
        grad_rows, grad_params = pullback(cot_rows)
        summed = tuple((total + grad for total, grad in zip(carry, grad_params)))
        return (summed, (result.astype(jnp.bfloat16), grad_rows))
    totals, stacked = lax.scan(one_block, zero_grads, (tok_blocks, cot_blocks, len_blocks))
    layer_out = stacked[0].reshape(BATCH, SEQ, D)
    grad_tokens = stacked[1].reshape(BATCH, SEQ, D)
    return (layer_out, grad_tokens, totals[0], totals[1], totals[2], totals[3], totals[4], totals[5], totals[6], totals[7], totals[8], totals[9], totals[10], totals[11])
```

```python
import math

import jax
import jax.numpy as jnp
from jax import lax
from jax.sharding import PartitionSpec as P

HEAD_DIM = 64
WORDS = 40


epsilon = 1e-06
masked_score = -1000000000.0


def norm_fwd(rows, gain_vec, shift_vec):
    mean_val = jnp.mean(rows, axis=-1, keepdims=True)
    centred = rows - mean_val
    inv_std = lax.rsqrt(jnp.mean(centred * centred, axis=-1, keepdims=True) + epsilon)
    unit_rows = centred * inv_std
    return (unit_rows * gain_vec + shift_vec, unit_rows, inv_std)


def norm_back(grad_rows, unit_rows, inv_std, gain_vec):
    scaled = grad_rows * gain_vec
    first = jnp.mean(scaled, axis=-1, keepdims=True)
    second = jnp.mean(scaled * unit_rows, axis=-1, keepdims=True)
    grad_in = inv_std * (scaled - first - unit_rows * second)
    return (grad_in, jnp.sum(grad_rows * unit_rows, axis=(0, 1)), jnp.sum(grad_rows, axis=(0, 1)))


def gelu_slope(values_in):
    cumulative = 0.5 * (1.0 + lax.erf(values_in * 0.7071067811865476))
    density = jnp.exp(-0.5 * values_in * values_in) * 0.3989422804014327
    return cumulative + values_in * density


def pair_sum(blocks, masks, held=jnp.bfloat16):
    count = blocks.shape[0]
    me = lax.axis_index("pairs")
    offsets = [0]
    for mask in reversed(masks):
        offsets = offsets + [o ^ mask for o in offsets]
    total = jnp.concatenate(
        [lax.dynamic_slice_in_dim(blocks, me ^ o, 1, axis=0) for o in offsets], axis=0
    )
    for mask in masks:
        half = total.shape[0] // 2
        send = total[half:].astype(held)
        got = lax.ppermute(send, "pairs", [(i, i ^ mask) for i in range(count)])
        total = total[:half].astype(jnp.float32) + got.astype(jnp.float32)
    return total[0]


def per_device(
    tokens,
    cotangent,
    text_len,
    word_mask,
    attn_gain,
    attn_shift,
    w_qkv,
    qv_bias,
    w_out,
    out_bias,
    mlp_gain,
    mlp_shift,
    w_up,
    up_bias,
    w_down,
    down_bias,
):
    local_pairs, seq_len, width = tokens.shape
    local_width = w_qkv.shape[2]
    local_heads = local_width // HEAD_DIM
    scale = 1.0 / math.sqrt(HEAD_DIM)
    zero_index = jnp.zeros((), jnp.int32)
    head_index = lax.axis_index("heads")
    tok_rows = tokens.astype(jnp.float32)
    normed, unit_one, inv_one = norm_fwd(tok_rows, attn_gain, attn_shift)
    normed_low = normed.astype(jnp.bfloat16)
    normed_all = lax.all_gather(normed_low, "heads", axis=0, tiled=True)
    group_pairs = normed_all.shape[0]
    proj = jnp.einsum("nsd,tdc->tnsc", normed_all, w_qkv, preferred_element_type=jnp.float32)
    head_shape = (group_pairs, seq_len, local_heads, HEAD_DIM)
    queries = (proj[0] + qv_bias[0]).astype(jnp.bfloat16).reshape(head_shape)
    key_rows = proj[1].astype(jnp.bfloat16).reshape(head_shape)
    values = (proj[2] + qv_bias[1]).astype(jnp.bfloat16).reshape(head_shape)
    position = jnp.arange(seq_len, dtype=jnp.int32)
    key_ok = (position[None, :] >= WORDS) | (position[None, :] < text_len[:, None])

    def score_rows():
        raw = (
            jnp.einsum("nqhe,nkhe->nhqk", queries, key_rows, preferred_element_type=jnp.float32)
            * scale
        )
        return jnp.where(key_ok[:, None, None, :], raw, masked_score)

    scores = score_rows()
    row_max = jnp.max(scores, axis=-1, keepdims=True)
    weights = jnp.exp(scores - row_max)
    total = jnp.sum(weights, axis=-1, keepdims=True)
    log_total = row_max + jnp.log(total)
    probs_low = (weights / total).astype(jnp.bfloat16)
    context = jnp.einsum("nhqk,nkhe->nqhe", probs_low, values, preferred_element_type=jnp.float32)
    context = context.reshape(group_pairs, seq_len, local_width).astype(jnp.bfloat16)
    context_tok = lax.all_to_all(context, "heads", split_axis=0, concat_axis=2, tiled=True)
    attn_out = (
        jnp.einsum("nsc,cd->nsd", context_tok, w_out, preferred_element_type=jnp.float32) + out_bias
    )
    resid = tok_rows + attn_out
    mlp_norm, unit_two, inv_two = norm_fwd(resid, mlp_gain, mlp_shift)
    mlp_low = mlp_norm.astype(jnp.bfloat16)
    keep = jnp.concatenate(
        [word_mask.astype(jnp.float32), jnp.ones((local_pairs, seq_len - WORDS), jnp.float32)],
        axis=1,
    )
    grad_final = cotangent.astype(jnp.float32) * keep[:, :, None]
    grad_mlp_low = grad_final.astype(jnp.bfloat16)
    grad_down_bias = jnp.sum(grad_mlp_low.astype(jnp.float32), axis=(0, 1))
    up_full, down_full, up_bias_full = (
        lax.all_gather(w_up, "heads", axis=1, tiled=True),
        lax.all_gather(w_down, "heads", axis=0, tiled=True),
        lax.all_gather(up_bias, "heads", axis=0, tiled=True),
    )
    hidden_pre = jnp.einsum(
        "nsd,df->nsf", mlp_low, up_full, preferred_element_type=jnp.float32
    ) + up_bias_full.astype(jnp.float32)
    act_low = jax.nn.gelu(hidden_pre, approximate=False).astype(jnp.bfloat16)
    mlp_out = (
        jnp.einsum("nsf,fd->nsd", act_low, down_full, preferred_element_type=jnp.float32)
        + down_bias
    )
    layer_out = (resid + mlp_out).astype(jnp.bfloat16)
    down_term_grad = jnp.einsum(
        "nsf,nsd->df", act_low, grad_mlp_low, preferred_element_type=jnp.float32
    )
    grad_act = jnp.einsum(
        "nsd,fd->nsf", grad_mlp_low, down_full, preferred_element_type=jnp.float32
    )
    grad_pre = (grad_act * gelu_slope(hidden_pre)).astype(jnp.bfloat16)
    up_term_grad = jnp.einsum("nsd,nsf->df", mlp_low, grad_pre, preferred_element_type=jnp.float32)
    up_bias_term = jnp.sum(grad_pre.astype(jnp.float32), axis=(0, 1))
    grad_mlp_in = jnp.einsum("nsf,df->nsd", grad_pre, up_full, preferred_element_type=jnp.float32)
    grad_resid_norm, grad_mlp_gain, grad_mlp_shift = norm_back(
        grad_mlp_in, unit_two, inv_two, mlp_gain
    )
    grad_resid = grad_final + grad_resid_norm
    grad_attn_low = grad_resid.astype(jnp.bfloat16)
    grad_w_out = jnp.einsum(
        "nsc,nsd->cd", context_tok, grad_attn_low, preferred_element_type=jnp.float32
    )
    grad_out_bias = jnp.sum(grad_attn_low.astype(jnp.float32), axis=(0, 1))
    grad_context = jnp.einsum(
        "nsd,cd->nsc", grad_attn_low, w_out, preferred_element_type=jnp.float32
    ).astype(jnp.bfloat16)
    grad_context_heads = lax.all_to_all(
        grad_context, "heads", split_axis=2, concat_axis=0, tiled=True
    ).reshape(head_shape)
    probs = jnp.exp(score_rows() - log_total)
    probs_again = probs.astype(jnp.bfloat16)
    grad_values = jnp.einsum(
        "nhqk,nqhe->nkhe", probs_again, grad_context_heads, preferred_element_type=jnp.float32
    ).astype(jnp.bfloat16)
    grad_probs = jnp.einsum(
        "nqhe,nkhe->nhqk", grad_context_heads, values, preferred_element_type=jnp.float32
    )
    inner_sum = jnp.sum(probs * grad_probs, axis=-1, keepdims=True)
    grad_scores = (probs * (grad_probs - inner_sum)).astype(jnp.bfloat16)
    grad_queries = (
        scale
        * jnp.einsum("nhqk,nkhe->nqhe", grad_scores, key_rows, preferred_element_type=jnp.float32)
    ).astype(jnp.bfloat16)
    grad_keys = (
        scale
        * jnp.einsum("nhqk,nqhe->nkhe", grad_scores, queries, preferred_element_type=jnp.float32)
    ).astype(jnp.bfloat16)
    flat_shape = (group_pairs, seq_len, local_width)
    grad_proj = jnp.stack(
        [
            grad_queries.reshape(flat_shape),
            grad_keys.reshape(flat_shape),
            grad_values.reshape(flat_shape),
        ],
        axis=1,
    )
    grad_qkv_local = jnp.einsum(
        "nsd,ntsc->tdc", normed_all, grad_proj, preferred_element_type=jnp.float32
    )
    bias_local = jnp.stack(
        [
            jnp.sum(grad_proj[:, 0].astype(jnp.float32), axis=(0, 1)),
            jnp.sum(grad_proj[:, 2].astype(jnp.float32), axis=(0, 1)),
        ],
        axis=0,
    )
    qv_term = lax.dynamic_update_slice(
        jnp.zeros((2, width), jnp.float32), bias_local, (zero_index, head_index * local_width)
    )
    grad_normed = lax.psum_scatter(
        jnp.einsum("ntsc,tdc->nsd", grad_proj, w_qkv, preferred_element_type=jnp.float32).astype(
            jnp.bfloat16
        ),
        "heads",
        scatter_dimension=0,
        tiled=True,
    ).astype(jnp.float32)
    grad_tok_norm, grad_attn_gain, grad_attn_shift = norm_back(
        grad_normed, unit_one, inv_one, attn_gain
    )
    grad_tokens = grad_resid + grad_tok_norm
    up_term_grad, down_term_grad = (
        lax.psum_scatter(
            up_term_grad.astype(jnp.bfloat16), "heads", scatter_dimension=1, tiled=True
        ),
        lax.psum_scatter(
            down_term_grad.astype(jnp.bfloat16), "heads", scatter_dimension=1, tiled=True
        ),
    )
    pair_count = lax.axis_size("pairs")
    rows = width // pair_count
    bits = pair_count.bit_length() - 1
    order_a = [1 << b for b in range(bits)]
    order_b = order_a[1::-1] + order_a[2:]
    out_blocks = lax.psum_scatter(
        grad_w_out.astype(jnp.bfloat16).reshape(pair_count, 2, rows // 2, width),
        "heads",
        scatter_dimension=1,
        tiled=True,
    ).reshape(pair_count, rows // 2, width)
    grad_w_up = pair_sum(up_term_grad.reshape(pair_count, rows, -1), order_a)
    grad_w_down = pair_sum(down_term_grad.reshape(pair_count, rows, -1), order_b).T
    qkv_blocks = jnp.moveaxis(grad_qkv_local, 0, 1).astype(jnp.bfloat16)
    grad_w_qkv = pair_sum(qkv_blocks.reshape(pair_count, rows * 3, -1), order_a)
    grad_w_qkv = jnp.moveaxis(grad_w_qkv.reshape(rows, 3, -1), 1, 0)
    grad_w_out_rows = pair_sum(out_blocks, order_b)
    small = jnp.concatenate(
        [
            vec.reshape(-1, pair_count, 2, vec.shape[-1] // pair_count // 2)
            .transpose(1, 2, 0, 3)
            .reshape(pair_count, 2, -1)
            for vec in (
                grad_attn_gain,
                grad_attn_shift,
                grad_out_bias,
                grad_mlp_gain,
                grad_mlp_shift,
                grad_down_bias,
                qv_term,
                up_bias_term,
            )
        ],
        axis=2,
    )
    mine = lax.dynamic_index_in_dim(small, head_index, 1, keepdims=False)
    theirs = lax.dynamic_index_in_dim(small, 1 - head_index, 1, keepdims=False)
    small = mine + lax.ppermute(theirs, "heads", [(0, 1), (1, 0)])
    small = pair_sum(small, order_a, jnp.float32)
    step = width // pair_count // 2
    vecs = [small[i * step : (i + 1) * step] for i in range(6)]
    qv_rows = small[6 * step : 8 * step].reshape(2, step)
    up_bias_rows = small[8 * step :]
    summed = (
        grad_w_out_rows,
        vecs[0],
        vecs[1],
        vecs[2],
        vecs[3],
        vecs[4],
        up_bias_rows,
        vecs[5],
        qv_rows,
    )
    return (
        layer_out,
        grad_tokens,
        summed[1],
        summed[2],
        grad_w_qkv,
        summed[8],
        summed[0],
        summed[3],
        summed[4],
        summed[5],
        grad_w_up,
        summed[6],
        grad_w_down,
        summed[7],
    )


def solution(mesh):
    in_specs = (
        P(("pairs", "heads"), None, None),
        P(("pairs", "heads"), None, None),
        P("pairs"),
        P(("pairs", "heads"), None),
        P(),
        P(),
        P(None, None, "heads"),
        P(None, "heads"),
        P(),
        P(),
        P(),
        P(),
        P(None, "heads"),
        P("heads"),
        P("heads", None),
        P(),
    )
    out_specs = (
        P(("pairs", "heads"), None, None),
        P(("pairs", "heads"), None, None),
        P(("pairs", "heads")),
        P(("pairs", "heads")),
        P(None, "pairs", "heads"),
        P(None, ("pairs", "heads")),
        P(("pairs", "heads"), None),
        P(("pairs", "heads")),
        P(("pairs", "heads")),
        P(("pairs", "heads")),
        P("pairs", "heads"),
        P(("pairs", "heads")),
        P("heads", "pairs"),
        P(("pairs", "heads")),
    )
    return jax.shard_map(
        per_device, mesh=mesh, in_specs=in_specs, out_specs=out_specs, check_vma=False
    )
```

```python
import functools
import math

import jax
import jax.numpy as jnp
from jax import lax
from jax.experimental import pallas as pl
from jax.experimental.pallas import tpu as pltpu
from jax.sharding import PartitionSpec as P

HEAD_DIM = 64
WORDS = 40
LANES = 128
EPSILON = 1e-06
MASKED = -1000000000.0
SWAP = [(0, 1), (1, 0)]
f32, bf16 = jnp.float32, jnp.bfloat16
VMEM_LIMIT = 58 * 1024 * 1024


def dot(a, b, ca=1, cb=0):
    return lax.dot_general(a, b, (((ca,), (cb,)), ((), ())), preferred_element_type=f32)


def centre(rows):
    mean_val = jnp.mean(rows, axis=-1, keepdims=True)
    centred = rows - mean_val
    inv_std = lax.rsqrt(jnp.mean(centred * centred, axis=-1, keepdims=True) + EPSILON)
    return centred * inv_std, inv_std


def norm_back(grad_rows, unit_rows, inv_std, gain):
    scaled = grad_rows * gain
    first = jnp.mean(scaled, axis=-1, keepdims=True)
    second = jnp.mean(scaled * unit_rows, axis=-1, keepdims=True)
    return inv_std * (scaled - first - unit_rows * second)


def col_sum(rows):
    return jnp.sum(rows, axis=0, keepdims=True)


def gelu_parts(v):
    u = jnp.abs(v) * 0.7071067811865476
    t = 1.0 / (1.0 + 0.39 * u)
    poly = 0.8866643918219983 - 0.22753713046899435 * t
    poly = -0.6354003145887568 + poly * t
    poly = 0.6495594277724073 + poly * t
    poly = 0.09138840279707615 + poly * t
    poly = 0.23532522096757497 + poly * t
    bell = jnp.exp(v * v * -0.5)
    tail = (0.5 * t) * poly * bell
    cdf = jnp.where(v < 0.0, tail, 1.0 - tail)
    return v * cdf, cdf + v * (bell * 0.3989422804014327)


def half_mask(value, lane, e):
    keep = (lane < HEAD_DIM) if e == 0 else (lane >= HEAD_DIM)
    return jnp.where(keep, value, jnp.zeros_like(value))


def attend(n, seq, half, len_ref, proj, ctx, lse_cols, lse_ref):
    scale = 1.0 / math.sqrt(HEAD_DIM)
    lane = lax.broadcasted_iota(jnp.int32, (seq, LANES), 1)
    key = lax.broadcasted_iota(jnp.int32, (1, seq), 1)
    lse_cols[...] = jnp.zeros_like(lse_cols)

    def step(hp, carry):
        off = pl.multiple_of(hp * LANES, LANES)
        for i in range(n):
            rows = pl.ds(i * seq, seq)
            q2 = proj[rows, pl.ds(off, LANES)] * scale
            k2 = proj[rows, pl.ds(half + off, LANES)].astype(bf16)
            v2 = proj[rows, pl.ds(2 * half + off, LANES)].astype(bf16)
            key_ok = (key >= WORDS) | (key < len_ref[i])
            outs = []
            for e in range(2):
                qm = half_mask(q2, lane, e).astype(bf16)
                s = jnp.where(key_ok, dot(qm, k2, 1, 1), MASKED)
                top = jnp.max(s, axis=-1, keepdims=True)
                w = jnp.exp(s - top)
                total = jnp.sum(w, axis=-1, keepdims=True)
                p = (w * (1.0 / total)).astype(bf16)
                outs.append(dot(p, v2))
                lse_cols[i] = jnp.where(lane == 2 * hp + e, top + jnp.log(total), lse_cols[i])
            ctx[rows, pl.ds(off, LANES)] = jnp.where(lane < HEAD_DIM, outs[0], outs[1])
        return carry

    lax.fori_loop(0, half // LANES, step, 0)
    for i in range(n):
        lse_ref[i] = lse_cols[i].T[: lse_ref.shape[1]]


def project(normed, w_ref, bias_ref, half, proj):
    for t in range(3):
        part = dot(normed, w_ref[t])
        if t != 1:
            part = part + bias_ref[t // 2 : t // 2 + 1]
        proj[:, t * half : (t + 1) * half] = part.astype(bf16).astype(f32)


def first_kernel(n, seq, half, len_ref, tok, gain, shift, w, bias, normed, qkv, ctx, lse, proj, ctx32, lse_cols):
    unit, _ = centre(tok[...].astype(f32))
    rows = (unit * gain[...] + shift[...]).astype(bf16)
    normed[...] = rows
    project(rows, w, bias, half, proj)
    for i in range(n):
        qkv[i] = proj[pl.ds(i * seq, seq)].astype(bf16)
    attend(n, seq, half, len_ref, proj, ctx32, lse_cols, lse)
    ctx[...] = ctx32[...].astype(bf16)


def second_kernel(
    n, seq, half, len_ref, head_ref, normed, w, bias, ctx_own, tok, w_out, out_bias, gain, shift,
    qkv, ctx, lse, resid, mlp_low, proj, ctx32, lse_cols,
):
    project(normed[...], w, bias, half, proj)
    for i in range(n):
        qkv[i] = proj[pl.ds(i * seq, seq)].astype(bf16)
    attend(n, seq, half, len_ref, proj, ctx32, lse_cols, lse)
    ctx[...] = ctx32[...].astype(bf16)
    own = pl.multiple_of(head_ref[0] * half, LANES)
    oth = pl.multiple_of((1 - head_ref[0]) * half, LANES)
    attn = dot(ctx_own[...], w_out[pl.ds(own, half)]) + dot(ctx[...], w_out[pl.ds(oth, half)])
    total = tok[...].astype(f32) + (attn + out_bias[...])
    resid[...] = total
    unit, _ = centre(total)
    mlp_low[...] = (unit * gain[...] + shift[...]).astype(bf16)


def mlp_kernel(
    steps, masks, block, me_ref, a_own, a_oth, g_own, g_oth, up, down, bias,
    out_own, out_oth, gmi_own, gmi_oth, d_up, d_down, d_bias, out_acc, gmi_acc, scr_up, scr_down,
):
    step = pl.program_id(0)
    rows = a_own.shape[0]

    @pl.when(step == 0)
    def _():
        out_acc[...] = jnp.zeros_like(out_acc)
        gmi_acc[...] = jnp.zeros_like(gmi_acc)

    sum_up = sum_down = sum_bias = None
    for part, (a, g) in enumerate(((a_own, g_own), (a_oth, g_oth))):
        at = pl.ds(part * rows, rows)
        act, slope = gelu_parts(dot(a[...], up[...]) + bias[...].astype(f32))
        act = act.astype(bf16)
        grad = (dot(g[...], down[...], 1, 1) * slope).astype(bf16)
        out_acc[at] += dot(act, down[...])
        gmi_acc[at] += dot(grad, up[...], 1, 1)
        u, d, b = dot(a[...], grad, 0, 0), dot(g[...], act, 0, 0), col_sum(grad.astype(f32))
        sum_up, sum_down, sum_bias = (
            (u, d, b) if part == 0 else (sum_up + u, sum_down + d, sum_bias + b)
        )
    d_bias[...] = sum_bias
    ordered(sum_up, scr_up, d_up, masks[0], block, me_ref)
    ordered(sum_down, scr_down, d_down, masks[1], block, me_ref)

    @pl.when(step == steps - 1)
    def _():
        out_own[...] = out_acc[:rows]
        out_oth[...] = out_acc[rows:].astype(bf16)
        gmi_own[...] = gmi_acc[:rows]
        gmi_oth[...] = gmi_acc[rows:].astype(bf16)


def ordered(value, scr, dest, offsets, block, me_ref):
    if block % 16:
        dest[...] = value.astype(dest.dtype)
        return
    scr[...] = value.astype(scr.dtype)
    for slot, offset in enumerate(offsets):
        at = pl.multiple_of((me_ref[0] ^ offset) * block, 16)
        dest[slot * block : (slot + 1) * block] = scr[pl.ds(at, block)].astype(dest.dtype)


def middle_kernel(
    n, seq, half, block, offsets, me_ref, head_ref, gmi_own, gmi_got, resid, g_low, gain, w_out, ctx_own, ctx_oth,
    grad_resid, gc_own, gc_oth, keep, send, sums, scr, cuts,
):
    unit, inv_std = centre(resid[...])
    gmi = gmi_own[...] + gmi_got[...].astype(f32)
    g_final = g_low[...].astype(f32)
    total = g_final + norm_back(gmi, unit, inv_std, gain[...])
    grad_resid[...] = total
    low = total.astype(bf16)
    sums[...] = jnp.zeros_like(sums)
    sums[0:1] = col_sum(gmi * unit)
    sums[1:2] = col_sum(gmi)
    sums[2:3] = col_sum(low.astype(f32))
    sums[3:4] = col_sum(g_final)
    own = pl.multiple_of(head_ref[0] * half, LANES)
    oth = pl.multiple_of((1 - head_ref[0]) * half, LANES)
    for dest, at in ((gc_own, own), (gc_oth, oth)):
        part = dot(low, w_out[pl.ds(at, half)], 1, 1)
        for i in range(n):
            dest[i] = part[i * seq : (i + 1) * seq].astype(bf16)
    scr[pl.ds(own, half)] = dot(ctx_own[...], low, 0, 0)
    scr[pl.ds(oth, half)] = dot(ctx_oth[...], low, 0, 0)
    if block % 16:
        keep[...] = scr[:half].astype(bf16)
        send[...] = scr[half:].astype(bf16)
        return
    part = block // 2
    for dest, core in ((keep, head_ref[0]), (send, 1 - head_ref[0])):
        for slot, offset in enumerate(offsets):
            at = pl.multiple_of((me_ref[0] ^ offset) * block + core * part, 8)
            cuts[slot * part : (slot + 1) * part] = scr[pl.ds(at, part)]
        dest[...] = cuts[...].astype(bf16)


def back_kernel(
    n, seq, half, block, offsets, len_ref, me_ref, qkv, gc, lse, normed, dqkv, d_w, sums, grads, scr
):
    scale = 1.0 / math.sqrt(HEAD_DIM)
    lane = lax.broadcasted_iota(jnp.int32, (seq, LANES), 1)
    key = lax.broadcasted_iota(jnp.int32, (seq, 1), 0)

    def step(hp, carry):
        off = pl.multiple_of(hp * LANES, LANES)
        for i in range(n):
            q2 = qkv[i, :, pl.ds(off, LANES)]
            k2 = qkv[i, :, pl.ds(half + off, LANES)]
            v2 = qkv[i, :, pl.ds(2 * half + off, LANES)]
            g2 = gc[i, :, pl.ds(off, LANES)]
            kt = k2.T
            key_ok = (key >= WORDS) | (key < len_ref[i])
            dq, dk, dv = [], [], []
            for e in range(2):
                qm = half_mask(q2, lane, e) * jnp.asarray(scale, bf16)
                s = jnp.where(key_ok, dot(k2, qm, 1, 1), MASKED)
                p = jnp.exp(s - lse[i, pl.ds(2 * hp + e, 1), :])
                dp = dot(v2, half_mask(g2, lane, e), 1, 1)
                inner = jnp.sum(p * dp, axis=0, keepdims=True)
                ds = (p * (dp - inner)).astype(bf16)
                dv.append(dot(p.astype(bf16), g2))
                dk.append(dot(ds, q2))
                dq.append(dot(kt[e * HEAD_DIM : (e + 1) * HEAD_DIM], ds))
            rows = pl.ds(i * seq, seq)
            grads[rows, pl.ds(off, LANES)] = jnp.concatenate(dq, axis=0).T * scale
            grads[rows, pl.ds(half + off, LANES)] = jnp.where(lane < HEAD_DIM, dk[0], dk[1]) * scale
            grads[rows, pl.ds(2 * half + off, LANES)] = jnp.where(lane < HEAD_DIM, dv[0], dv[1])
        return carry

    lax.fori_loop(0, half // LANES, step, 0)
    low = grads[...].astype(bf16)
    dqkv[...] = low
    sums[...] = jnp.zeros_like(sums)
    sums[0:1] = col_sum(low[:, :half].astype(f32))
    sums[1:2] = col_sum(low[:, 2 * half :].astype(f32))
    ordered(dot(normed[...], low, 0, 0), scr, d_w, offsets, block, me_ref)


def last_kernel(half, dq_own, dq_oth, w_own, w_oth, tok, gain, grad_resid, grad_tokens, sums):
    grad = None
    for dq, w in ((dq_own, w_own), (dq_oth, w_oth)):
        for t in range(3):
            part = dot(dq[:, t * half : (t + 1) * half], w[t], 1, 1)
            grad = part if grad is None else grad + part
    unit, inv_std = centre(tok[...].astype(f32))
    grad_tokens[...] = grad_resid[...] + norm_back(grad, unit, inv_std, gain[...])
    sums[...] = jnp.zeros_like(sums)
    sums[0:1] = col_sum(grad * unit)
    sums[1:2] = col_sum(grad)


SMEM = pl.BlockSpec(memory_space=pltpu.SMEM)


def call(body, name, outs, scratch, scalars, args, flops, trans=0):
    shapes = [jax.ShapeDtypeStruct(s, d) for s, d in outs]
    moved = sum(math.prod(s) * jnp.dtype(d).itemsize for s, d in outs)
    moved += sum(a.size * a.dtype.itemsize for a in args)
    return pl.pallas_call(
        body,
        name=name,
        out_shape=shapes,
        in_specs=[SMEM] * len(scalars) + [pl.BlockSpec(memory_space=pltpu.VMEM)] * len(args),
        out_specs=[pl.BlockSpec(memory_space=pltpu.VMEM)] * len(outs),
        scratch_shapes=[pltpu.VMEM(s, d) for s, d in scratch],
        compiler_params=pltpu.CompilerParams(vmem_limit_bytes=VMEM_LIMIT),
        cost_estimate=pl.CostEstimate(flops=flops, bytes_accessed=moved, transcendentals=trans),
    )(*scalars, *args)


def slots(masks):
    offsets = [0]
    for mask in reversed(masks):
        offsets = offsets + [o ^ mask for o in offsets]
    return offsets


def arrange(blocks, offsets, me):
    return jnp.concatenate([lax.dynamic_slice_in_dim(blocks, me ^ o, 1, axis=0) for o in offsets], axis=0)


def exchange(send, mask, count):
    return lax.ppermute(send, "pairs", [(i, i ^ mask) for i in range(count)])


def pair_sum(total, masks, count, held=bf16):
    for mask in masks:
        half = total.shape[0] // 2
        got = exchange(total[half:].astype(held), mask, count)
        total = total[:half].astype(f32) + got.astype(f32)
    return total[0].astype(f32)


def per_device(
    tokens, cotangent, text_len, word_mask, attn_gain, attn_shift, w_qkv, qv_bias, w_out, out_bias,
    mlp_gain, mlp_shift, w_up, up_bias, w_down, down_bias,
):
    n, seq, width = tokens.shape
    half = w_qkv.shape[2]
    hidden = w_up.shape[1]
    rows = n * seq
    count = lax.axis_size("pairs")
    block = width // count
    head = lax.axis_index("heads")
    me = lax.axis_index("pairs")
    head_s, me_s = head.reshape(1), me.reshape(1)
    lens = lax.dynamic_slice_in_dim(text_len, head * n, n)
    bits = count.bit_length() - 1
    order_a = [1 << b for b in range(bits)]
    order_b = order_a[1::-1] + order_a[2:]
    slots_a, slots_b = slots(order_a), slots(order_b)
    row = lambda v: v.reshape(1, -1)
    tok = tokens.reshape(rows, width)

    w_oth = lax.ppermute(w_qkv, "heads", SWAP)
    bias_oth = lax.ppermute(qv_bias, "heads", SWAP)
    keep_rows = jnp.concatenate(
        [word_mask.astype(bf16), jnp.ones((n, seq - WORDS), bf16)], axis=1
    )
    g_own = (cotangent * keep_rows[:, :, None]).reshape(rows, width)
    g_oth = lax.ppermute(g_own, "heads", SWAP)

    qkv_shape = ((n, seq, 3 * half), bf16)
    lse_shape = ((n, 8, seq), f32)
    attn_scratch = [((rows, 3 * half), f32), ((rows, half), f32), ((n, seq, LANES), f32)]
    units = n * half // HEAD_DIM
    attn_flops = 4 * units * seq * seq * HEAD_DIM + 6 * rows * width * half
    normed, qkv_own, ctx_own, lse_own = call(
        functools.partial(first_kernel, n, seq, half),
        "attend_own",
        [((rows, width), bf16), qkv_shape, ((rows, half), bf16), lse_shape],
        attn_scratch,
        [lens],
        [tok, row(attn_gain), row(attn_shift), w_qkv, qv_bias],
        attn_flops,
        units * seq * seq,
    )
    qkv_oth, ctx_oth, lse_oth, resid, mlp_low = call(
        functools.partial(second_kernel, n, seq, half),
        "attend_other",
        [qkv_shape, ((rows, half), bf16), lse_shape, ((rows, width), f32), ((rows, width), bf16)],
        attn_scratch,
        [lens, head_s],
        [normed, w_oth, bias_oth, ctx_own, tok, w_out, row(out_bias), row(mlp_gain), row(mlp_shift)],
        attn_flops + 2 * rows * width * width,
        units * seq * seq,
    )
    mlp_oth = lax.ppermute(mlp_low, "heads", SWAP)

    cut = 256
    steps = hidden // cut
    whole = lambda shape: pl.BlockSpec(shape, lambda i: (0,) * len(shape))
    row_spec = whole((rows, width))
    out_own, out_send, gmi_own, gmi_send, d_up, d_down, d_up_bias = pl.pallas_call(
        functools.partial(mlp_kernel, steps, (slots_a, slots_b), block),
        name="mlp",
        grid=(steps,),
        out_shape=[
            jax.ShapeDtypeStruct((rows, width), f32),
            jax.ShapeDtypeStruct((rows, width), bf16),
            jax.ShapeDtypeStruct((rows, width), f32),
            jax.ShapeDtypeStruct((rows, width), bf16),
            jax.ShapeDtypeStruct((width, hidden), bf16),
            jax.ShapeDtypeStruct((width, hidden), bf16),
            jax.ShapeDtypeStruct((1, hidden), f32),
        ],
        in_specs=[SMEM]
        + [row_spec] * 4
        + [
            pl.BlockSpec((width, cut), lambda i: (0, i)),
            pl.BlockSpec((cut, width), lambda i: (i, 0)),
            pl.BlockSpec((1, cut), lambda i: (0, i)),
        ],
        out_specs=[row_spec] * 4
        + [pl.BlockSpec((width, cut), lambda i: (0, i))] * 2
        + [pl.BlockSpec((1, cut), lambda i: (0, i))],
        scratch_shapes=[pltpu.VMEM((2 * rows, width), f32)] * 2 + [pltpu.VMEM((width, cut), bf16)] * 2,
        compiler_params=pltpu.CompilerParams(vmem_limit_bytes=VMEM_LIMIT),
        cost_estimate=pl.CostEstimate(
            flops=24 * rows * width * hidden, bytes_accessed=20 << 20, transcendentals=4 * rows * hidden
        ),
    )(me_s, mlp_low, mlp_oth, g_own, g_oth, w_up, w_down, row(up_bias))
    gmi_got = lax.ppermute(gmi_send, "heads", SWAP)
    out_got = lax.ppermute(out_send, "heads", SWAP)
    layer_out = (resid + (out_own + out_got.astype(f32) + down_bias)).astype(bf16)

    grad_resid, gc_own, gc_oth, wo_keep, wo_send, sums_mid = call(
        functools.partial(middle_kernel, n, seq, half, block, slots_b),
        "middle",
        [
            ((rows, width), f32),
            ((n, seq, half), bf16),
            ((n, seq, half), bf16),
            ((half, width), bf16),
            ((half, width), bf16),
            ((8, width), f32),
        ],
        [((width, width), f32), ((half, width), f32)],
        [me_s, head_s],
        [gmi_own, gmi_got, resid, g_own, row(mlp_gain), w_out, ctx_own, ctx_oth],
        4 * rows * width * width,
    )

    back = lambda name, qkv, gc, lse, kind: call(
        functools.partial(back_kernel, n, seq, half, block, slots_a),
        name,
        [((rows, 3 * half), bf16), ((width, 3 * half), kind), ((8, half), f32)],
        [((rows, 3 * half), f32), ((width, 3 * half), kind)],
        [lens, me_s],
        [qkv, gc, lse, normed],
        10 * units * seq * seq * HEAD_DIM + 6 * rows * width * half,
        units * seq * seq,
    )
    dq_oth, dw_send, sums_oth = back("back_other", qkv_oth, gc_oth, lse_oth, bf16)
    dq_own, dw_keep, sums_own = back("back_own", qkv_own, gc_own, lse_own, f32)
    grad_tok, sums_last = call(
        functools.partial(last_kernel, half),
        "last",
        [((rows, width), f32), ((8, width), f32)],
        [],
        [],
        [dq_own, dq_oth, w_qkv, w_oth, tok, row(attn_gain), grad_resid],
        12 * rows * width * half,
    )

    blocks = lambda v, size: v.reshape(count, size, -1)
    place = lambda v, size, offsets: blocks(v, size) if block % 16 == 0 else arrange(blocks(v, size), offsets, me)
    grad_w_up = pair_sum(place(d_up, block, slots_a), order_a, count)
    grad_w_down = pair_sum(place(d_down, block, slots_b), order_b, count).T
    if block % 16:
        wo = jnp.concatenate([wo_keep, wo_send], axis=0).reshape(count, 2, block // 2, width)
        wo = arrange(wo, slots_b, me)
        wo_keep = lax.dynamic_index_in_dim(wo, head, 1, keepdims=False)
        wo_send = lax.dynamic_index_in_dim(wo, 1 - head, 1, keepdims=False)
    wo_got = lax.ppermute(wo_send, "heads", SWAP)
    wo = wo_keep.astype(f32) + wo_got.astype(f32)
    grad_w_out = pair_sum(wo.reshape(count, block // 2, width), order_b, count)
    dw_got = lax.ppermute(dw_send, "heads", SWAP)
    dw = place(dw_keep + dw_got.astype(f32), block, slots_a)
    cut_at = 2 * half
    grad_qk = pair_sum(dw[..., :cut_at], order_a, count)
    grad_v = grad_vpart = None
    if block % 16 == 0:
        quarter = count // 4
        v = dw[..., cut_at:].reshape(2, 2, quarter, block, half).swapaxes(0, 1)
        grad_v = pair_sum(v.reshape(count, block, half), order_b, count)
    else:
        grad_v = pair_sum(dw[..., cut_at:], order_a, count)
    grad_w_qkv = jnp.stack([grad_qk[:, :half], grad_qk[:, half:], grad_v], axis=0)

    halves = lambda own, oth: jnp.where(
        head == 0, jnp.concatenate([own, oth], -1), jnp.concatenate([oth, own], -1)
    )
    up_zero = jnp.zeros_like(d_up_bias)
    vecs = [
        sums_last[0:1], sums_last[1:2], sums_mid[0:1], sums_mid[1:2], sums_mid[2:3], sums_mid[3:4],
        halves(sums_own[0:1], sums_oth[0:1]), halves(sums_own[1:2], sums_oth[1:2]), halves(d_up_bias, up_zero),
    ]
    small = jnp.concatenate([v.reshape(count, 2, -1) for v in vecs], axis=2)
    mine = lax.dynamic_index_in_dim(small, head, 1, keepdims=False)
    theirs = lax.dynamic_index_in_dim(small, 1 - head, 1, keepdims=False)
    small = mine + lax.ppermute(theirs, "heads", SWAP)
    small = pair_sum(arrange(small, slots_a, me), order_a, count, f32)
    step = width // count // 2
    piece = [small[i * step : (i + 1) * step] for i in range(8)]
    return (
        layer_out.reshape(n, seq, width),
        grad_tok.reshape(n, seq, width),
        piece[0],
        piece[1],
        grad_w_qkv,
        jnp.stack([piece[6], piece[7]], axis=0),
        grad_w_out,
        piece[4],
        piece[2],
        piece[3],
        grad_w_up,
        small[8 * step :],
        grad_w_down,
        piece[5],
    )


def solution(mesh):
    in_specs = (
        P(("pairs", "heads"), None, None),
        P(("pairs", "heads"), None, None),
        P("pairs"),
        P(("pairs", "heads"), None),
        P(),
        P(),
        P(None, None, "heads"),
        P(None, "heads"),
        P(),
        P(),
        P(),
        P(),
        P(None, "heads"),
        P("heads"),
        P("heads", None),
        P(),
    )
    out_specs = (
        P(("pairs", "heads"), None, None),
        P(("pairs", "heads"), None, None),
        P(("pairs", "heads")),
        P(("pairs", "heads")),
        P(None, "pairs", "heads"),
        P(None, ("pairs", "heads")),
        P(("pairs", "heads"), None),
        P(("pairs", "heads")),
        P(("pairs", "heads")),
        P(("pairs", "heads")),
        P("pairs", "heads"),
        P(("pairs", "heads")),
        P("heads", "pairs"),
        P(("pairs", "heads")),
    )
    return jax.shard_map(
        per_device, mesh=mesh, in_specs=in_specs, out_specs=out_specs, check_vma=False
    )
```

```python
import functools
import math

import jax
import jax.numpy as jnp
from jax import lax
from jax.experimental import pallas as pl
from jax.experimental.pallas import tpu as pltpu
from jax.sharding import PartitionSpec as P

HEAD_DIM = 64
WORDS = 40
LANES = 128
EPSILON = 1e-06
MASKED = -1000000000.0
SWAP = [(0, 1), (1, 0)]
f32, bf16 = jnp.float32, jnp.bfloat16
MIB = 1024 * 1024


def dot(a, b, ca=1, cb=0):
    return lax.dot_general(a, b, (((ca,), (cb,)), ((), ())), preferred_element_type=f32)


def centre(rows):
    mean_val = jnp.mean(rows, axis=-1, keepdims=True)
    centred = rows - mean_val
    inv_std = lax.rsqrt(jnp.mean(centred * centred, axis=-1, keepdims=True) + EPSILON)
    return centred * inv_std, inv_std


def norm_back(grad_rows, unit_rows, inv_std, gain):
    scaled = grad_rows * gain
    first = jnp.mean(scaled, axis=-1, keepdims=True)
    second = jnp.mean(scaled * unit_rows, axis=-1, keepdims=True)
    return inv_std * (scaled - first - unit_rows * second)


def col_sum(rows):
    return jnp.sum(rows, axis=0, keepdims=True)


def gelu_parts(v):
    u = jnp.abs(v) * 0.7071067811865476
    t = 1.0 / (1.0 + 0.39 * u)
    poly = 0.8866643918219983 - 0.22753713046899435 * t
    poly = -0.6354003145887568 + poly * t
    poly = 0.6495594277724073 + poly * t
    poly = 0.09138840279707615 + poly * t
    poly = 0.23532522096757497 + poly * t
    bell = jnp.exp(v * v * -0.5)
    tail = (0.5 * t) * poly * bell
    cdf = jnp.where(v < 0.0, tail, 1.0 - tail)
    return v * cdf, cdf + v * (bell * 0.3989422804014327)


def as_row(ref):
    return ref[...].astype(f32).reshape(1, ref.shape[0])


def half_mask(value, lane, e):
    keep = (lane < HEAD_DIM) if e == 0 else (lane >= HEAD_DIM)
    return jnp.where(keep, value, jnp.zeros_like(value))


def attend(n, seq, half, len_ref, proj, ctx, lse_cols, lse_ref):
    scale = 1.0 / math.sqrt(HEAD_DIM)
    lane = lax.broadcasted_iota(jnp.int32, (seq, LANES), 1)
    key = lax.broadcasted_iota(jnp.int32, (1, seq), 1)
    lse_cols[...] = jnp.zeros_like(lse_cols)

    def step(hp, carry):
        off = pl.multiple_of(hp * LANES, LANES)
        for i in range(n):
            rows = pl.ds(i * seq, seq)
            q2 = proj[rows, pl.ds(off, LANES)] * scale
            k2 = proj[rows, pl.ds(half + off, LANES)].astype(bf16)
            v2 = proj[rows, pl.ds(2 * half + off, LANES)].astype(bf16)
            key_ok = (key >= WORDS) | (key < len_ref[i])
            outs = []
            for e in range(2):
                qm = half_mask(q2, lane, e).astype(bf16)
                s = jnp.where(key_ok, dot(qm, k2, 1, 1), MASKED)
                top = jnp.max(s, axis=-1, keepdims=True)
                w = jnp.exp(s - top)
                total = jnp.sum(w, axis=-1, keepdims=True)
                p = (w * (1.0 / total)).astype(bf16)
                outs.append(dot(p, v2))
                lse_cols[i] = jnp.where(lane == 2 * hp + e, top + jnp.log(total), lse_cols[i])
            ctx[rows, pl.ds(off, LANES)] = jnp.where(lane < HEAD_DIM, outs[0], outs[1])
        return carry

    lax.fori_loop(0, half // LANES, step, 0)
    for i in range(n):
        lse_ref[i] = lse_cols[i].T[: lse_ref.shape[1]]


def project(normed, w_ref, bias_ref, half, proj):
    for t in range(3):
        part = dot(normed, w_ref[t])
        if t != 1:
            part = part + bias_ref[t // 2 : t // 2 + 1]
        proj[:, t * half : (t + 1) * half] = part.astype(bf16).astype(f32)


def first_kernel(n, seq, half, len_ref, tok, gain, shift, w, bias, normed, qkv, ctx, lse, proj, ctx32, lse_cols):
    unit, _ = centre(tok[...].astype(f32))
    rows = (unit * as_row(gain) + as_row(shift)).astype(bf16)
    normed[...] = rows
    project(rows, w, bias, half, proj)
    for i in range(n):
        qkv[i] = proj[pl.ds(i * seq, seq)].astype(bf16)
    attend(n, seq, half, len_ref, proj, ctx32, lse_cols, lse)
    ctx[...] = ctx32[...].astype(bf16)


def second_kernel(
    n, seq, half, len_ref, head_ref, normed, w, bias, ctx_own, tok, w_out, out_bias, gain, shift,
    qkv, ctx, lse, resid, mlp_low, proj, ctx32, lse_cols,
):
    project(normed[...], w, bias, half, proj)
    for i in range(n):
        qkv[i] = proj[pl.ds(i * seq, seq)].astype(bf16)
    attend(n, seq, half, len_ref, proj, ctx32, lse_cols, lse)
    ctx[...] = ctx32[...].astype(bf16)
    own = pl.multiple_of(head_ref[0] * half, LANES)
    oth = pl.multiple_of((1 - head_ref[0]) * half, LANES)
    attn = dot(ctx_own[...], w_out[pl.ds(own, half)]) + dot(ctx[...], w_out[pl.ds(oth, half)])
    total = tok[...].astype(f32) + (attn + as_row(out_bias))
    resid[...] = total
    unit, _ = centre(total)
    mlp_low[...] = (unit * as_row(gain) + as_row(shift)).astype(bf16)


def mlp_kernel(
    steps, masks, block, me_ref, a_own, a_oth, g_own, g_oth, up, down, bias,
    out_own, out_oth, gmi_own, gmi_oth, up_keep, up_send, down_keep, down_send, d_bias,
    out_acc, gmi_acc, scr_up, scr_down, a, g,
):
    step = pl.program_id(0)
    rows = a_own.shape[0]

    @pl.when(step == 0)
    def _():
        out_acc[...] = jnp.zeros_like(out_acc)
        gmi_acc[...] = jnp.zeros_like(gmi_acc)
        a[:rows], a[rows:] = a_own[...], a_oth[...]
        g[:rows], g[rows:] = g_own[...], g_oth[...]

    act, slope = gelu_parts(dot(a[...], up[...]) + as_row(bias))
    act = act.astype(bf16)
    grad = (dot(g[...], down[...], 1, 1) * slope).astype(bf16)
    ordered(dot(a[...], grad, 0, 0), scr_up, up_keep, up_send, masks[0], block, me_ref)
    ordered(dot(g[...], act, 0, 0), scr_down, down_keep, down_send, masks[1], block, me_ref)
    out_acc[...] += dot(act, down[...])
    gmi_acc[...] += dot(grad, up[...], 1, 1)
    d_bias[...] = col_sum(grad.astype(f32)).reshape(d_bias.shape)

    @pl.when(step == steps - 1)
    def _():
        out_own[...] = out_acc[:rows]
        out_oth[...] = out_acc[rows:].astype(bf16)
        gmi_own[...] = gmi_acc[:rows]
        gmi_oth[...] = gmi_acc[rows:].astype(bf16)


def ordered(value, scr, keep, send, offsets, block, me_ref, got=()):
    half, cols = keep.shape[0], pl.ds(0, value.shape[1])
    if block % 16:
        keep[:, cols] = value[:half].astype(keep.dtype)
        send[:, cols] = value[half:].astype(send.dtype)
        return
    scr[...] = value.astype(scr.dtype)
    for slot, offset in enumerate(offsets):
        late = slot * block >= half
        dest, at = (send, pl.ds(slot * block - half, block)) if late else (keep, pl.ds(slot * block, block))
        part = scr[pl.ds(pl.multiple_of((me_ref[0] ^ offset) * block, 16), block)]
        if got:
            part = part + got[late][at].astype(f32)
        dest[at, cols] = part.astype(dest.dtype)


def middle_kernel(
    n, seq, half, block, offsets, me_ref, head_ref, gmi_own, gmi_got, resid, g_low, gain, w_out, ctx_own, ctx_oth,
    grad_resid, gc_own, gc_oth, keep, send, sums, scr, cuts,
):
    unit, inv_std = centre(resid[...])
    gmi = gmi_own[...] + gmi_got[...].astype(f32)
    g_final = g_low[...].astype(f32)
    total = g_final + norm_back(gmi, unit, inv_std, as_row(gain))
    grad_resid[...] = total
    low = total.astype(bf16)
    sums[...] = jnp.zeros_like(sums)
    sums[0:1] = col_sum(gmi * unit)
    sums[1:2] = col_sum(gmi)
    sums[2:3] = col_sum(low.astype(f32))
    sums[3:4] = col_sum(g_final)
    own = pl.multiple_of(head_ref[0] * half, LANES)
    oth = pl.multiple_of((1 - head_ref[0]) * half, LANES)
    for dest, at in ((gc_own, own), (gc_oth, oth)):
        part = dot(low, w_out[pl.ds(at, half)], 1, 1)
        for i in range(n):
            dest[i] = part[i * seq : (i + 1) * seq].astype(bf16)
    scr[pl.ds(own, half)] = dot(ctx_own[...], low, 0, 0)
    scr[pl.ds(oth, half)] = dot(ctx_oth[...], low, 0, 0)
    if block % 16:
        keep[...] = scr[:half].astype(bf16)
        send[...] = scr[half:].astype(bf16)
        return
    part = block // 2
    for dest, core in ((keep, head_ref[0]), (send, 1 - head_ref[0])):
        for slot, offset in enumerate(offsets):
            at = pl.multiple_of((me_ref[0] ^ offset) * block + core * part, 8)
            cuts[slot * block : slot * block + part] = scr[pl.ds(at, part), :half]
            cuts[slot * block + part : (slot + 1) * block] = scr[pl.ds(at, part), half:]
        dest[...] = cuts[...].astype(bf16)


def back_kernel(n, seq, half, block, masks, fused, len_ref, me_ref, qkv, gc, lse, normed, *rest):
    if fused:
        got_qk, got_v, (wo, wo_got), rest = rest[:2], rest[2:4], rest[4:6], rest[6:]
    else:
        got_qk = got_v = ()
    dqkv, qk_keep, qk_send, v_keep, v_send, sums, grads, scr_qk, scr_v = rest
    scale = 1.0 / math.sqrt(HEAD_DIM)
    lane = lax.broadcasted_iota(jnp.int32, (seq, LANES), 1)
    key = lax.broadcasted_iota(jnp.int32, (seq, 1), 0)

    def step(hp, carry):
        off = pl.multiple_of(hp * LANES, LANES)
        for i in range(n):
            q2 = qkv[i, :, pl.ds(off, LANES)]
            k2 = qkv[i, :, pl.ds(half + off, LANES)]
            v2 = qkv[i, :, pl.ds(2 * half + off, LANES)]
            g2 = gc[i, :, pl.ds(off, LANES)]
            kt = k2.T
            key_ok = (key >= WORDS) | (key < len_ref[i])
            dq, dk, dv = [], [], []
            for e in range(2):
                qm = half_mask(q2, lane, e) * jnp.asarray(scale, bf16)
                s = jnp.where(key_ok, dot(k2, qm, 1, 1), MASKED)
                p = jnp.exp(s - lse[i, pl.ds(2 * hp + e, 1), :])
                dp = dot(v2, half_mask(g2, lane, e), 1, 1)
                inner = jnp.sum(p * dp, axis=0, keepdims=True)
                ds = (p * (dp - inner)).astype(bf16)
                dv.append(dot(p.astype(bf16), g2))
                dk.append(dot(ds, q2))
                dq.append(dot(kt[e * HEAD_DIM : (e + 1) * HEAD_DIM], ds))
            rows = pl.ds(i * seq, seq)
            grads[rows, pl.ds(off, LANES)] = jnp.concatenate(dq, axis=0).T * scale
            grads[rows, pl.ds(half + off, LANES)] = jnp.where(lane < HEAD_DIM, dk[0], dk[1]) * scale
            grads[rows, pl.ds(2 * half + off, LANES)] = jnp.where(lane < HEAD_DIM, dv[0], dv[1])
        return carry

    lax.fori_loop(0, half // LANES, step, 0)
    low = grads[...].astype(bf16)
    dqkv[...] = low
    sums[...] = jnp.zeros_like(sums)
    sums[0:1] = col_sum(low[:, :half].astype(f32))
    sums[1:2] = col_sum(low[:, 2 * half :].astype(f32))
    rows = normed[...]
    ordered(dot(rows, low[:, : 2 * half], 0, 0), scr_qk, qk_keep, qk_send, masks[0], block, me_ref, got_qk)
    ordered(dot(rows, low[:, 2 * half :], 0, 0), scr_v, v_keep, v_send, masks[1], block, me_ref, got_v)
    if fused:
        at = v_keep.shape[0]
        both = wo[...].astype(f32) + wo_got[...].astype(f32)
        v_keep[:, half:] = both[:at]
        v_send[:, half:] = both[at:].astype(bf16)


def last_kernel(
    half, head_ref, dq_own, dq_oth, w_own, w_oth, tok, gain, grad_resid, sums_mid, sums_own, sums_oth, up_sums,
    grad_tokens, vecs,
):
    grad = None
    for dq, w in ((dq_own, w_own), (dq_oth, w_oth)):
        for t in range(3):
            part = dot(dq[:, t * half : (t + 1) * half], w[t], 1, 1)
            grad = part if grad is None else grad + part
    unit, inv_std = centre(tok[...].astype(f32))
    grad_tokens[...] = grad_resid[...] + norm_back(grad, unit, inv_std, as_row(gain))
    width = 2 * half
    vecs[...] = jnp.zeros_like(vecs)
    vecs[0:1, :width], vecs[0:1, width:] = col_sum(grad * unit), col_sum(grad)
    vecs[1:2, :width], vecs[1:2, width:] = sums_mid[0:1], sums_mid[1:2]
    vecs[2:3, :width], vecs[2:3, width:] = sums_mid[2:3], sums_mid[3:4]
    first = head_ref[0] == 0
    for i in range(2):
        own, oth = sums_own[i : i + 1], sums_oth[i : i + 1]
        vecs[3:4, i * width : i * width + half] = jnp.where(first, own, oth)
        vecs[3:4, i * width + half : (i + 1) * width] = jnp.where(first, oth, own)
    up = as_row(up_sums)
    for i in range(2):
        vecs[4 + i : 5 + i, : up.shape[1]] = jnp.where(head_ref[0] == i, up, jnp.zeros_like(up))


def spread_kernel(count, width, hidden, index_ref, vec, vec_got, *outs):
    index, lanes = index_ref[0], vec.shape[1]
    total = vec[...] + vec_got[...]
    part = width // count // 2
    rolled = pltpu.roll(total, lanes - index * part, 1)
    for i in range(6):
        at = (i % 2) * width
        outs[i][...] = rolled[i // 2 : i // 2 + 1, at : at + part].reshape(part)
    for i in range(2):
        outs[6][i : i + 1] = rolled[3:4, i * width : i * width + part]
    part = hidden // count
    up = jnp.where(index < count, total[4:5], total[5:6])
    up = pltpu.roll(jnp.concatenate([up] * 8, axis=0), lanes - (index % count) * part, 1)
    outs[7][...] = up[0:1, :part].reshape(part)


def combine_kernel(plan, adds, *refs):
    ins, outs = refs[: plan["ins"]], refs[plan["ins"] :]
    for keep, got, at, kept, send, place in plan["parts"]:
        rows = ins[keep].shape[0]
        half = rows // 2
        outs[kept][...] = ins[keep][:half].astype(f32) + ins[got][at : at + half].astype(f32)
        low = ins[keep][half:].astype(f32) + ins[got][at + half : at + rows].astype(f32)
        outs[send][place : place + half] = low.astype(bf16)
    for a, b, at, out, turned in adds:
        total = ins[a][...].astype(f32) + ins[b][at : at + ins[a].shape[0]].astype(f32)
        outs[out][...] = total.T if turned else total


def combine(name, parts, groups, adds=()):
    if any(keep.shape[0] % 32 for keep, _, _ in parts) or any(a.shape[0] % 8 for a, *_ in adds):
        total = [k.astype(f32) + g[at : at + k.shape[0]].astype(f32) for k, g, at in parts]
        keeps = [t[: t.shape[0] // 2] for t in total]
        sends = [jnp.concatenate([total[i][total[i].shape[0] // 2 :].astype(bf16) for i in g], 0) for g in groups]
        sums = [a.astype(f32) + b[at : at + a.shape[0]].astype(f32) for a, b, at, _ in adds]
        return keeps, sends, [v.T if turned else v for v, (*_, turned) in zip(sums, adds)]
    arrays, outs, plan, plan_adds = [], [], [], []

    def put(array):
        for i, have in enumerate(arrays):
            if have is array:
                return i
        arrays.append(array)
        return len(arrays) - 1

    for keep, _, _ in parts:
        outs.append(((keep.shape[0] // 2, keep.shape[1]), f32))
    for g in groups:
        outs.append(((sum(parts[i][0].shape[0] // 2 for i in g), parts[g[0]][0].shape[1]), bf16))
    for number, g in enumerate(groups):
        place = 0
        for i in g:
            keep, got, at = parts[i]
            plan.append((put(keep), put(got), at, i, len(parts) + number, place))
            place += keep.shape[0] // 2
    for a, b, at, turned in adds:
        plan_adds.append((put(a), put(b), at, len(outs), turned))
        outs.append((a.shape[::-1] if turned else a.shape, f32))
    got = call(
        functools.partial(combine_kernel, {"ins": len(arrays), "parts": plan}, plan_adds),
        name, outs, [], [], arrays, 24,
    )
    return got[: len(parts)], got[len(parts) : len(parts) + len(groups)], got[len(parts) + len(groups) :]


SMEM = pl.BlockSpec(memory_space=pltpu.SMEM)
VMEM = pl.BlockSpec(memory_space=pltpu.VMEM)


def params(limit):
    return dict(
        compiler_params=pltpu.CompilerParams(vmem_limit_bytes=limit * MIB),
        cost_estimate=pl.CostEstimate(flops=0, bytes_accessed=MIB, transcendentals=0),
    )


def call(body, name, outs, scratch, scalars, args, limit):
    return pl.pallas_call(
        body,
        name=name,
        out_shape=[jax.ShapeDtypeStruct(s, d) for s, d in outs],
        in_specs=[SMEM] * len(scalars) + [VMEM] * len(args),
        out_specs=[VMEM] * len(outs),
        scratch_shapes=[pltpu.VMEM(s, d) for s, d in scratch],
        **params(limit),
    )(*scalars, *args)


def slots(masks):
    offsets = [0]
    for mask in reversed(masks):
        offsets = offsets + [o ^ mask for o in offsets]
    return offsets


def arrange(blocks, offsets, me):
    return jnp.concatenate([lax.dynamic_slice_in_dim(blocks, me ^ o, 1, axis=0) for o in offsets], axis=0)


def exchange(send, mask, count):
    return lax.ppermute(send, "pairs", [(i, i ^ mask) for i in range(count)])


def per_device(
    tokens, cotangent, text_len, word_mask, attn_gain, attn_shift, w_qkv, qv_bias, w_out, out_bias,
    mlp_gain, mlp_shift, w_up, up_bias, w_down, down_bias,
):
    n, seq, width = tokens.shape
    half = w_qkv.shape[2]
    hidden = w_up.shape[1]
    rows = n * seq
    count = lax.axis_size("pairs")
    block = width // count
    head = lax.axis_index("heads")
    me = lax.axis_index("pairs")
    head_s, me_s = head.reshape(1), me.reshape(1)
    lens = lax.dynamic_slice_in_dim(text_len, head * n, n)
    bits = count.bit_length() - 1
    order_a = [1 << b for b in range(bits)]
    order_b = order_a[1::-1] + order_a[2:]
    slots_a, slots_b = slots(order_a), slots(order_b)
    tie = lax.optimization_barrier
    tok = tokens.reshape(rows, width)

    w_oth = lax.ppermute(w_qkv, "heads", SWAP)
    bias_oth = lax.ppermute(qv_bias, "heads", SWAP)
    keep_rows = jnp.concatenate(
        [word_mask.astype(bf16), jnp.ones((n, seq - WORDS), bf16)], axis=1
    )
    g_own = (cotangent * keep_rows[:, :, None]).reshape(rows, width)
    g_oth = lax.ppermute(g_own, "heads", SWAP)

    qkv_shape = ((n, seq, 3 * half), bf16)
    lse_shape = ((n, 8, seq), f32)
    attn_scratch = [((rows, 3 * half), f32), ((rows, half), f32), ((n, seq, LANES), f32)]
    normed, qkv_own, ctx_own, lse_own = call(
        functools.partial(first_kernel, n, seq, half),
        "attend_own",
        [((rows, width), bf16), qkv_shape, ((rows, half), bf16), lse_shape],
        attn_scratch,
        [lens],
        [tok, attn_gain, attn_shift, w_qkv, qv_bias],
        24,
    )
    qkv_oth, ctx_oth, lse_oth, resid, mlp_low = call(
        functools.partial(second_kernel, n, seq, half),
        "attend_other",
        [qkv_shape, ((rows, half), bf16), lse_shape, ((rows, width), f32), ((rows, width), bf16)],
        attn_scratch,
        [lens, head_s],
        [normed, w_oth, bias_oth, ctx_own, tok, w_out, out_bias, mlp_gain, mlp_shift],
        28,
    )
    mlp_oth = lax.ppermute(mlp_low, "heads", SWAP)

    cut = 512 if hidden % 512 == 0 else hidden
    steps = hidden // cut
    out_own, out_send, gmi_own, gmi_send, up_keep, up_send, down_keep, down_send, up_sums = pl.pallas_call(
        functools.partial(mlp_kernel, steps, (slots_a, slots_b), block),
        name="mlp",
        grid=(steps,),
        out_shape=[
            jax.ShapeDtypeStruct((rows, width), f32),
            jax.ShapeDtypeStruct((rows, width), bf16),
            jax.ShapeDtypeStruct((rows, width), f32),
            jax.ShapeDtypeStruct((rows, width), bf16),
            *[jax.ShapeDtypeStruct((width // 2, hidden), bf16)] * 4,
            jax.ShapeDtypeStruct((hidden,), f32),
        ],
        in_specs=[SMEM]
        + [VMEM] * 4
        + [
            pl.BlockSpec((width, cut), lambda i: (0, i)),
            pl.BlockSpec((cut, width), lambda i: (i, 0)),
            pl.BlockSpec((cut,), lambda i: (i,)),
        ],
        out_specs=[VMEM] * 4
        + [pl.BlockSpec((width // 2, cut), lambda i: (0, i))] * 4
        + [pl.BlockSpec((cut,), lambda i: (i,))],
        scratch_shapes=[pltpu.VMEM((2 * rows, width), f32)] * 2
        + [pltpu.VMEM((width, cut), bf16)] * 2
        + [pltpu.VMEM((2 * rows, width), bf16)] * 2,
        **params(48),
    )(me_s, mlp_low, mlp_oth, g_own, g_oth, w_up, w_down, up_bias)
    gmi_got = lax.ppermute(gmi_send, "heads", SWAP)

    def take(keep, send, offsets):
        if block % 16 == 0:
            return keep, send
        total = jnp.concatenate([keep, send], axis=0).reshape(count, block, -1)
        total = arrange(total, offsets, me).reshape(width, -1)
        return total[: width // 2], total[width // 2 :]

    up_keep, up_send = take(up_keep, up_send, slots_a)
    down_keep, down_send = take(down_keep, down_send, slots_b)
    up_got = exchange(up_send, order_a[0], count)
    down_got = exchange(down_send, order_b[0], count)

    grad_resid, gc_own, gc_oth, wo_keep, wo_send, sums_mid = call(
        functools.partial(middle_kernel, n, seq, half, block, slots_b),
        "middle",
        [
            ((rows, width), f32),
            ((n, seq, half), bf16),
            ((n, seq, half), bf16),
            *[((width, half) if block % 16 == 0 else (half, width), bf16)] * 2,
            ((8, width), f32),
        ],
        [((width, width), f32), ((width, half), f32)],
        [me_s, head_s],
        [gmi_own, gmi_got, resid, g_own, mlp_gain, w_out, ctx_own, ctx_oth],
        28,
    )
    if block % 16:
        wo = jnp.concatenate([wo_keep, wo_send], axis=0).reshape(count, 2, block // 2, 2, half)
        wo = arrange(wo, slots_b, me).swapaxes(2, 3)
        wo_keep = lax.dynamic_index_in_dim(wo, head, 1, keepdims=False).reshape(width, half)
        wo_send = lax.dynamic_index_in_dim(wo, 1 - head, 1, keepdims=False).reshape(width, half)
    wo_got = lax.ppermute(wo_send, "heads", SWAP)

    def back(name, qkv, gc, lse, fused, kinds, more):
        wide = width if fused else half
        return call(
            functools.partial(back_kernel, n, seq, half, block, (slots_a, slots_b), fused),
            name,
            [
                ((rows, 3 * half), bf16),
                *[((width // 2, 2 * half), k) for k in kinds],
                *[((width // 2, wide), k) for k in kinds],
                ((8, half), f32),
            ],
            [((rows, 3 * half), f32), ((width, 2 * half), kinds[0]), ((width, half), kinds[0])],
            [lens, me_s],
            [qkv, gc, lse, normed, *more],
            32,
        )

    dq_oth, *dw_oth, sums_oth = back("back_other", qkv_oth, gc_oth, lse_oth, False, (bf16, bf16), [])
    dw_got = [lax.ppermute(d, "heads", SWAP) for d in dw_oth]
    (up, down), (up_send, down_send), _ = combine(
        "add_first", [(up_keep, up_got, 0), (down_keep, down_got, 0)], [[0], [1]]
    )
    qkv_own, up_send, down_send = tie((qkv_own, up_send, down_send))
    up_got = exchange(up_send, order_a[1], count)
    down_got = exchange(down_send, order_b[1], count)
    if block % 16:
        dq_own, *dw_own, sums_own = back("back_own", qkv_own, gc_own, lse_own, False, (f32, f32), [])
        qk_keep, qk_send, v_keep, v_send = [d + o.astype(f32) for d, o in zip(dw_own, dw_got)]
        qk_keep, qk_send = take(qk_keep, qk_send, slots_a)
        v_keep, v_send = take(v_keep, v_send, slots_b)
        wo = wo_keep.astype(f32) + wo_got.astype(f32)
        vo_keep = jnp.concatenate([v_keep, wo[: width // 2]], axis=1)
        vo_send = jnp.concatenate([v_send, wo[width // 2 :]], axis=1).astype(bf16)
        qk_send = qk_send.astype(bf16)
    else:
        dq_own, qk_keep, qk_send, vo_keep, vo_send, sums_own = back(
            "back_own", qkv_own, gc_own, lse_own, True, (f32, bf16), [*dw_got, wo_keep, wo_got]
        )
    (up, down), (wide_send,), _ = combine("add_second", [(up, up_got, 0), (down, down_got, 0)], [[0, 1]])
    qk_send, vo_send, wide_send, dq_own = tie((qk_send, vo_send, wide_send, dq_own))
    qk_got = exchange(qk_send, order_a[0], count)
    vo_got = exchange(vo_send, order_b[0], count)
    wide_got = exchange(wide_send, order_a[2], count)
    grad_tok, vecs = call(
        functools.partial(last_kernel, half),
        "last",
        [((rows, width), f32), ((8, max(2 * width, hidden)), f32)],
        [],
        [head_s],
        [dq_own, dq_oth, w_qkv, w_oth, tok, attn_gain, grad_resid, sums_mid, sums_own, sums_oth, up_sums],
        24,
    )
    out_send, vecs = tie((out_send, vecs))
    out_got = lax.ppermute(out_send, "heads", SWAP)
    vecs = vecs + lax.ppermute(vecs, "heads", SWAP)
    vecs_got = exchange(vecs, order_a[0], count)
    layer_out = (resid + (out_own + out_got.astype(f32) + down_bias)).astype(bf16)
    qk_got, vo_got, wide_got, vecs_got = tie((qk_got, vo_got, wide_got, vecs_got))
    (qk, vo, up, down), (qk_send, vo_send, wide_send), (vecs,) = combine(
        "add_third",
        [(qk_keep, qk_got, 0), (vo_keep, vo_got, 0), (up, wide_got, 0), (down, wide_got, up.shape[0])],
        [[0], [1], [2, 3]],
        [(vecs, vecs_got, 0, False)],
    )
    qk_got = exchange(qk_send, order_a[1], count)
    vo_got = exchange(vo_send, order_b[1], count)
    wide_got = exchange(wide_send, order_a[3], count)
    vecs_got = exchange(vecs, order_a[1], count)
    qk_got, vo_got, wide_got, vecs_got = tie((qk_got, vo_got, wide_got, vecs_got))
    for mask in order_a[4:]:
        (up, down), (wide_send,), _ = combine(
            "add_more", [(up, wide_got, 0), (down, wide_got, up.shape[0])], [[0, 1]]
        )
        wide_got = exchange(wide_send, mask, count)
    (qk, vo), (pair_send,), (vecs,) = combine(
        "add_fourth", [(qk, qk_got, 0), (vo, vo_got, 0)], [[0, 1]], [(vecs, vecs_got, 0, False)]
    )
    for mask, later in zip(order_a[2:], order_a[3:]):
        pair_got, vecs_got = exchange(pair_send, mask, count), exchange(vecs, mask, count)
        if mask == order_a[2]:
            _, _, (grad_w_up, grad_w_down) = combine(
                "add_wide", [], [], [(up, wide_got, 0, False), (down, wide_got, up.shape[0], True)]
            )
        pair_got, vecs_got, grad_w_up = tie((pair_got, vecs_got, grad_w_up))
        (qk, vo), (pair_send,), (vecs,) = combine(
            "add_fifth",
            [(qk, pair_got, 0), (vo, pair_got, qk.shape[0])],
            [[0, 1]],
            [(vecs, vecs_got, 0, False)],
        )
    pair_got, vecs_got = exchange(pair_send, order_a[-1], count), exchange(vecs, order_a[-1], count)
    _, _, (qk, vo) = combine("add_last", [], [], [(qk, pair_got, 0, False), (vo, pair_got, qk.shape[0], False)])
    grad_w_qkv = jnp.stack([qk[:, :half], qk[:, half:], vo[:, :half]], axis=0)
    grad_w_out = jnp.concatenate([vo[: block // 2, half:], vo[block // 2 :, half:]], axis=1)
    part, up_part = width // count // 2, hidden // count
    piece = call(
        functools.partial(spread_kernel, count, width, hidden),
        "spread",
        [((part,), f32)] * 6 + [((2, part), f32), ((up_part,), f32)],
        [],
        [(me * 2 + head).reshape(1)],
        [vecs, vecs_got],
        8,
    )
    return (
        layer_out.reshape(n, seq, width),
        grad_tok.reshape(n, seq, width),
        piece[0],
        piece[1],
        grad_w_qkv,
        piece[6],
        grad_w_out,
        piece[4],
        piece[2],
        piece[3],
        grad_w_up,
        piece[7],
        grad_w_down,
        piece[5],
    )


def solution(mesh):
    in_specs = (
        P(("pairs", "heads"), None, None),
        P(("pairs", "heads"), None, None),
        P("pairs"),
        P(("pairs", "heads"), None),
        P(),
        P(),
        P(None, None, "heads"),
        P(None, "heads"),
        P(),
        P(),
        P(),
        P(),
        P(None, "heads"),
        P("heads"),
        P("heads", None),
        P(),
    )
    out_specs = (
        P(("pairs", "heads"), None, None),
        P(("pairs", "heads"), None, None),
        P(("pairs", "heads")),
        P(("pairs", "heads")),
        P(None, "pairs", "heads"),
        P(None, ("pairs", "heads")),
        P(("pairs", "heads"), None),
        P(("pairs", "heads")),
        P(("pairs", "heads")),
        P(("pairs", "heads")),
        P("pairs", "heads"),
        P(("pairs", "heads")),
        P("heads", "pairs"),
        P(("pairs", "heads")),
    )
    return jax.shard_map(
        per_device, mesh=mesh, in_specs=in_specs, out_specs=out_specs, check_vma=False
    )
```

```python
import functools
import math

import jax
import jax.numpy as jnp
from jax import lax
from jax.experimental import pallas as pl
from jax.experimental.pallas import tpu as pltpu
from jax.sharding import PartitionSpec as P

HEAD_DIM = 64
WORDS = 40
LANES = 128
EPSILON = 1e-06
MASKED = -1000000000.0
SWAP = [(0, 1), (1, 0)]
f32, bf16 = jnp.float32, jnp.bfloat16
MIB = 1024 * 1024


def dot(a, b, ca=1, cb=0):
    return lax.dot_general(a, b, (((ca,), (cb,)), ((), ())), preferred_element_type=f32)


def centre(rows):
    mean_val = jnp.mean(rows, axis=-1, keepdims=True)
    centred = rows - mean_val
    inv_std = lax.rsqrt(jnp.mean(centred * centred, axis=-1, keepdims=True) + EPSILON)
    return centred * inv_std, inv_std


def norm_back(grad_rows, unit_rows, inv_std, gain):
    scaled = grad_rows * gain
    first = jnp.mean(scaled, axis=-1, keepdims=True)
    second = jnp.mean(scaled * unit_rows, axis=-1, keepdims=True)
    return inv_std * (scaled - first - unit_rows * second)


def col_sum(rows):
    return jnp.sum(rows, axis=0, keepdims=True)


def gelu_parts(v):
    u = jnp.abs(v) * 0.7071067811865476
    t = 1.0 / (1.0 + 0.39 * u)
    poly = 0.8866643918219983 - 0.22753713046899435 * t
    poly = -0.6354003145887568 + poly * t
    poly = 0.6495594277724073 + poly * t
    poly = 0.09138840279707615 + poly * t
    poly = 0.23532522096757497 + poly * t
    bell = jnp.exp(v * v * -0.5)
    tail = (0.5 * t) * poly * bell
    cdf = jnp.where(v < 0.0, tail, 1.0 - tail)
    return v * cdf, cdf + v * (bell * 0.3989422804014327)


def as_row(ref):
    return ref[...].astype(f32).reshape(1, ref.shape[0])


def half_mask(value, lane, e):
    keep = (lane < HEAD_DIM) if e == 0 else (lane >= HEAD_DIM)
    return jnp.where(keep, value, jnp.zeros_like(value))


def attend(n, seq, half, len_ref, head_ref, proj, ctx, lse_cols, lse_ref):
    scale = 1.0 / math.sqrt(HEAD_DIM)
    lane = lax.broadcasted_iota(jnp.int32, (seq, LANES), 1)
    key = lax.broadcasted_iota(jnp.int32, (1, seq), 1)
    first = head_ref[0] * n
    lse_cols[...] = jnp.zeros_like(lse_cols)

    def step(hp, carry):
        off = pl.multiple_of(hp * LANES, LANES)
        for i in range(n):
            rows = pl.ds(i * seq, seq)
            q2 = proj[rows, pl.ds(off, LANES)] * scale
            k2 = proj[rows, pl.ds(half + off, LANES)].astype(bf16)
            v2 = proj[rows, pl.ds(2 * half + off, LANES)].astype(bf16)
            key_ok = (key >= WORDS) | (key < len_ref[first + i])
            outs = []
            for e in range(2):
                qm = half_mask(q2, lane, e).astype(bf16)
                s = jnp.where(key_ok, dot(qm, k2, 1, 1), MASKED)
                top = jnp.max(s, axis=-1, keepdims=True)
                w = jnp.exp(s - top)
                total = jnp.sum(w, axis=-1, keepdims=True)
                p = (w * (1.0 / total)).astype(bf16)
                outs.append(dot(p, v2))
                lse_cols[i] = jnp.where(lane == 2 * hp + e, top + jnp.log(total), lse_cols[i])
            ctx[rows, pl.ds(off, LANES)] = jnp.where(lane < HEAD_DIM, outs[0], outs[1])
        return carry

    lax.fori_loop(0, half // LANES, step, 0)
    for i in range(n):
        lse_ref[i] = lse_cols[i].T[: lse_ref.shape[1]]


def project(normed, w, ready, bias, half, proj):
    for t in range(3):
        ready[t].wait()
        part = dot(normed, w[t])
        if t != 1:
            at = t // 2 * half
            part = part + as_row(bias)[:, at : at + half]
        proj[:, t * half : (t + 1) * half] = part.astype(bf16).astype(f32)


def bring(pairs, sems):
    copies = [pltpu.make_async_copy(a, b, sems.at[i]) for i, (a, b) in enumerate(pairs)]
    for c in copies:
        c.start()
    return copies


def first_kernel(
    n, seq, half, len_ref, head_ref, tok_h, gain_h, shift_h, bias_h, w_h, normed, qkv_h, ctx, lse,
    tok, gain, shift, bias, w, qkv, proj, ctx32, lse_cols, sems,
):
    copies = bring(
        [(tok_h, tok), (gain_h, gain), (shift_h, shift), (bias_h, bias)] + [(w_h.at[t], w.at[t]) for t in range(3)],
        sems,
    )
    for c in copies[:4]:
        c.wait()
    unit, _ = centre(tok[...].astype(f32))
    rows = (unit * as_row(gain) + as_row(shift)).astype(bf16)
    normed[...] = rows
    project(rows, w, copies[4:], bias, half, proj)
    for i in range(n):
        qkv[i] = proj[pl.ds(i * seq, seq)].astype(bf16)
    leave = pltpu.make_async_copy(qkv, qkv_h, sems.at[7])
    leave.start()
    attend(n, seq, half, len_ref, head_ref, proj, ctx32, lse_cols, lse)
    ctx[...] = ctx32[...].astype(bf16)
    leave.wait()


def second_kernel(
    n, seq, half, len_ref, head_ref, normed, ctx_own, bias_h, w_h, tok_h, w_out_h, out_bias_h, gain_h, shift_h,
    up_h, down_h, qkv_h, ctx_h, lse, resid_h, mlp_low, up, down,
    bias, w, tok, w_out, out_bias, gain, shift, ctx, resid, qkv, proj, ctx32, lse_cols, sems,
):
    copies = bring(
        [(bias_h, bias)]
        + [(w_h.at[t], w.at[t]) for t in range(3)]
        + [(tok_h, tok), (w_out_h, w_out), (out_bias_h, out_bias), (gain_h, gain), (shift_h, shift)]
        + [(up_h, up), (down_h, down)],
        sems,
    )
    copies[0].wait()
    project(normed[...], w, copies[1:4], bias, half, proj)
    for i in range(n):
        qkv[i] = proj[pl.ds(i * seq, seq)].astype(bf16)
    leave = [pltpu.make_async_copy(qkv, qkv_h, sems.at[11])]
    leave[0].start()
    ctx[:, :half] = ctx_own[...]
    attend(n, seq, half, len_ref, head_ref, proj, ctx32, lse_cols, lse)
    ctx[:, half:] = ctx32[...].astype(bf16)
    leave.append(pltpu.make_async_copy(ctx, ctx_h, sems.at[12]))
    leave[1].start()
    for c in copies[4:9]:
        c.wait()
    own = pl.multiple_of(head_ref[0] * half, LANES)
    oth = pl.multiple_of((1 - head_ref[0]) * half, LANES)
    attn = dot(ctx[:, :half], w_out[pl.ds(own, half)]) + dot(ctx[:, half:], w_out[pl.ds(oth, half)])
    total = tok[...].astype(f32) + (attn + as_row(out_bias))
    resid[...] = total
    leave.append(pltpu.make_async_copy(resid, resid_h, sems.at[13]))
    leave[2].start()
    unit, _ = centre(total)
    mlp_low[...] = (unit * as_row(gain) + as_row(shift)).astype(bf16)
    for c in leave + copies[9:]:
        c.wait()


def mlp_kernel(start, masks, block, me_ref, *refs):
    count = 6 if start == 0 else 4
    ins, (up, down, bias), refs = refs[:count], refs[count : count + 3], refs[count + 3 :]
    a, g, out_acc, gmi_acc, up_keep, up_send, down_keep, down_send, d_bias, scr_up, scr_down = refs
    cut = d_bias.shape[0]
    if start == 0:
        rows = ins[0].shape[0]
        a[:rows], a[rows:] = ins[0][...], ins[1][...]
        at = 0
        for cot, words in (ins[2:4], ins[4:6]):
            keep = words[...].astype(f32).T
            for i in range(cot.shape[0]):
                seq, word = cot.shape[1], words.shape[1]
                rows_g = cot[i].astype(f32)
                gmi_acc[at : at + word] = rows_g[:word] * keep[:, i : i + 1]
                gmi_acc[at + word : at + seq] = rows_g[word:]
                at += seq
        g[...] = gmi_acc[...].astype(bf16)
        a_rows, g_rows = a, g
    else:
        a_rows, g_rows = ins[:2]
    units = pl.ds(start, cut)
    w_up, w_down = up[:, units], down[units]
    act, slope = gelu_parts(dot(a_rows[...], w_up) + bias[units].astype(f32).reshape(1, cut))
    act = act.astype(bf16)
    grad = (dot(g_rows[...], w_down, 1, 1) * slope).astype(bf16)
    ordered(dot(a_rows[...], grad, 0, 0), scr_up, up_keep, up_send, masks[0], block, me_ref)
    ordered(dot(g_rows[...], act, 0, 0), scr_down, down_keep, down_send, masks[1], block, me_ref)
    d_bias[...] = col_sum(grad.astype(f32)).reshape(cut)
    out, gmi = dot(act, w_down), dot(grad, w_up, 1, 1)
    if start == 0:
        out_acc[...], gmi_acc[...] = out, gmi
        return
    rows = out_acc.shape[0]
    out, gmi = ins[2][...] + out, ins[3][...] + gmi
    out_acc[...], gmi_acc[...] = out[:rows], gmi[:rows]
    a[...], g[...] = out[rows:].astype(bf16), gmi[rows:].astype(bf16)


def ordered(value, scr, keep, send, offsets, block, me_ref, got=()):
    half, cols = keep.shape[0], pl.ds(0, value.shape[1])
    if block % 16:
        keep[:, cols] = value[:half].astype(keep.dtype)
        send[:, cols] = value[half:].astype(send.dtype)
        return
    scr[...] = value.astype(scr.dtype)
    for slot, offset in enumerate(offsets):
        late = slot * block >= half
        dest, at = (send, pl.ds(slot * block - half, block)) if late else (keep, pl.ds(slot * block, block))
        part = scr[pl.ds(pl.multiple_of((me_ref[0] ^ offset) * block, 16), block)]
        if got:
            part = part + got[late][at].astype(f32)
        dest[at, cols] = part.astype(dest.dtype)


def middle_kernel(
    n, seq, half, block, offsets, me_ref, head_ref, gmi_own, gmi_got, resid, g_all, gain, w_out, ctx,
    grad_resid, gc_own, gc_oth, keep, send, sums, scr, cuts,
):
    unit, inv_std = centre(resid[...])
    gmi = gmi_own[...] + gmi_got[...].astype(f32)
    g_final = g_all[: gmi_own.shape[0]].astype(f32)
    total = g_final + norm_back(gmi, unit, inv_std, as_row(gain))
    grad_resid[...] = total
    low = total.astype(bf16)
    sums[...] = jnp.zeros_like(sums)
    sums[0:1] = col_sum(gmi * unit)
    sums[1:2] = col_sum(gmi)
    sums[2:3] = col_sum(low.astype(f32))
    sums[3:4] = col_sum(g_final)
    own = pl.multiple_of(head_ref[0] * half, LANES)
    oth = pl.multiple_of((1 - head_ref[0]) * half, LANES)
    for dest, at in ((gc_own, own), (gc_oth, oth)):
        part = dot(low, w_out[pl.ds(at, half)], 1, 1)
        for i in range(n):
            dest[i] = part[i * seq : (i + 1) * seq].astype(bf16)
    scr[pl.ds(own, half)] = dot(ctx[:, :half], low, 0, 0)
    scr[pl.ds(oth, half)] = dot(ctx[:, half:], low, 0, 0)
    if block % 16:
        keep[...] = scr[:half].astype(bf16)
        send[...] = scr[half:].astype(bf16)
        return
    part = block // 2
    for dest, core in ((keep, head_ref[0]), (send, 1 - head_ref[0])):
        for slot, offset in enumerate(offsets):
            at = pl.multiple_of((me_ref[0] ^ offset) * block + core * part, 8)
            cuts[slot * block : slot * block + part] = scr[pl.ds(at, part), :half]
            cuts[slot * block + part : (slot + 1) * block] = scr[pl.ds(at, part), half:]
        dest[...] = cuts[...].astype(bf16)


def back_kernel(n, seq, half, block, masks, fused, len_ref, head_ref, me_ref, qkv, gc, lse, normed, *rest):
    if fused:
        got_qk, got_v, (wo, wo_got), rest = rest[:2], rest[2:4], rest[4:6], rest[6:]
    else:
        got_qk = got_v = ()
    dqkv, qk_keep, qk_send, v_keep, v_send, sums, grads, scr_qk, scr_v = rest
    scale = 1.0 / math.sqrt(HEAD_DIM)
    lane = lax.broadcasted_iota(jnp.int32, (seq, LANES), 1)
    key = lax.broadcasted_iota(jnp.int32, (seq, 1), 0)
    first = head_ref[0] * n

    def step(hp, carry):
        off = pl.multiple_of(hp * LANES, LANES)
        for i in range(n):
            q2 = qkv[i, :, pl.ds(off, LANES)]
            k2 = qkv[i, :, pl.ds(half + off, LANES)]
            v2 = qkv[i, :, pl.ds(2 * half + off, LANES)]
            g2 = gc[i, :, pl.ds(off, LANES)]
            kt = k2.T
            key_ok = (key >= WORDS) | (key < len_ref[first + i])
            dq, dk, dv = [], [], []
            for e in range(2):
                qm = half_mask(q2, lane, e) * jnp.asarray(scale, bf16)
                s = jnp.where(key_ok, dot(k2, qm, 1, 1), MASKED)
                p = jnp.exp(s - lse[i, pl.ds(2 * hp + e, 1), :])
                dp = dot(v2, half_mask(g2, lane, e), 1, 1)
                inner = jnp.sum(p * dp, axis=0, keepdims=True)
                ds = (p * (dp - inner)).astype(bf16)
                dv.append(dot(p.astype(bf16), g2))
                dk.append(dot(ds, q2))
                dq.append(dot(kt[e * HEAD_DIM : (e + 1) * HEAD_DIM], ds))
            rows = pl.ds(i * seq, seq)
            grads[rows, pl.ds(off, LANES)] = jnp.concatenate(dq, axis=0).T * scale
            grads[rows, pl.ds(half + off, LANES)] = jnp.where(lane < HEAD_DIM, dk[0], dk[1]) * scale
            grads[rows, pl.ds(2 * half + off, LANES)] = jnp.where(lane < HEAD_DIM, dv[0], dv[1])
        return carry

    lax.fori_loop(0, half // LANES, step, 0)
    low = grads[...].astype(bf16)
    dqkv[...] = low
    sums[...] = jnp.zeros_like(sums)
    sums[0:1] = col_sum(low[:, :half].astype(f32))
    sums[1:2] = col_sum(low[:, 2 * half :].astype(f32))
    rows = normed[...]
    ordered(dot(rows, low[:, : 2 * half], 0, 0), scr_qk, qk_keep, qk_send, masks[0], block, me_ref, got_qk)
    ordered(dot(rows, low[:, 2 * half :], 0, 0), scr_v, v_keep, v_send, masks[1], block, me_ref, got_v)
    if fused:
        at = v_keep.shape[0]
        both = wo[...].astype(f32) + wo_got[...].astype(f32)
        v_keep[:, half:] = both[:at]
        v_send[:, half:] = both[at:].astype(bf16)


def last_kernel(
    half, head_ref, dq_own, dq_oth, w_own, w_oth, tok, gain, grad_resid, sums_mid, sums_own, sums_oth, up_first, up_second,
    resid, out_own, out_got, down_bias, grad_tokens, layer_out, vecs,
):
    grad = None
    for dq, w in ((dq_own, w_own), (dq_oth, w_oth)):
        for t in range(3):
            part = dot(dq[:, t * half : (t + 1) * half], w[t], 1, 1)
            grad = part if grad is None else grad + part
    unit, inv_std = centre(tok[...].astype(f32))
    layer_out[...] = (resid[...] + (out_own[...] + out_got[...].astype(f32) + as_row(down_bias))).astype(bf16)
    width = 2 * half
    grad_tokens[...] = grad_resid[...] + norm_back(grad, unit, inv_std, as_row(gain))
    width = 2 * half
    vecs[...] = jnp.zeros_like(vecs)
    vecs[0:1, :width], vecs[0:1, width:] = col_sum(grad * unit), col_sum(grad)
    vecs[1:2, :width], vecs[1:2, width:] = sums_mid[0:1], sums_mid[1:2]
    vecs[2:3, :width], vecs[2:3, width:] = sums_mid[2:3], sums_mid[3:4]
    first = head_ref[0] == 0
    for i in range(2):
        own, oth = sums_own[i : i + 1], sums_oth[i : i + 1]
        vecs[3:4, i * width : i * width + half] = jnp.where(first, own, oth)
        vecs[3:4, i * width + half : (i + 1) * width] = jnp.where(first, oth, own)
    for place, sums in enumerate((up_first, up_second)):
        up = as_row(sums)
        cut = up.shape[1]
        for i in range(2):
            at = place * cut
            vecs[4 + i : 5 + i, at : at + cut] = jnp.where(head_ref[0] == i, up, jnp.zeros_like(up))


def spread_vectors(count, width, hidden, index, total, outs):
    lanes = total.shape[1]
    part = width // count // 2
    rolled = pltpu.roll(total, lanes - index * part, 1)
    for i in range(6):
        at = (i % 2) * width
        outs[i][...] = rolled[i // 2 : i // 2 + 1, at : at + part].reshape(part)
    for i in range(2):
        outs[6][i : i + 1] = rolled[3:4, i * width : i * width + part]
    part = hidden // count
    up = jnp.where(index < count, total[4:5], total[5:6])
    up = pltpu.roll(jnp.concatenate([up] * 8, axis=0), lanes - (index % count) * part, 1)
    outs[7][...] = up[0:1, :part].reshape(part)


def spread_kernel(count, width, hidden, index_ref, vec, vec_got, *outs):
    spread_vectors(count, width, hidden, index_ref[0], vec[...] + vec_got[...], outs)


def fan_kernel(qk, qk_got, vo, vo_got, vec, *refs):
    vec_gots, (qk_keep, vo_keep, *sends, vec_out) = refs[:-6], refs[-6:]
    block = qk.shape[0] // 4
    for place, (have, got, keep) in enumerate(((qk, qk_got, qk_keep), (vo, vo_got, vo_keep))):
        keep[...] = have[:block] + got[:block].astype(f32)
        for i, send in enumerate(sends):
            at = pl.ds((i + 1) * block, block)
            send[place * block : (place + 1) * block] = (have[at] + got[at].astype(f32)).astype(bf16)
    vec_out[...] = vec[...] + sum(g[...] for g in vec_gots)


def finish_kernel(count, width, hidden, index_ref, qk, vo, vec, *refs):
    gots, vec_gots, (w_qkv, w_out, *outs) = refs[:3], refs[3:6], refs[6:]
    block, half = qk.shape[0], width // 2
    both = [have[...] + sum(g[i * block : (i + 1) * block].astype(f32) for g in gots) for i, have in enumerate((qk, vo))]
    w_qkv[0], w_qkv[1], w_qkv[2] = both[0][:, :half], both[0][:, half:], both[1][:, :half]
    part = block // 2
    w_out[:, :half], w_out[:, half:] = both[1][:part, half:], both[1][part:, half:]
    spread_vectors(count, width, hidden, index_ref[0], vec[...] + sum(g[...] for g in vec_gots), outs)


def wide_kernel(up1, down1, got1, up2, down2, got2, up, down):
    block = up1.shape[0]
    for place, (a, b, got) in enumerate(((up1, down1, got1), (up2, down2, got2))):
        at = pl.ds(place * a.shape[1], a.shape[1])
        up[:, at] = a[...] + got[:block].astype(f32)
        down[:, at] = b[...] + got[block:].astype(f32)


def combine_kernel(plan, adds, *refs):
    ins, outs = refs[: plan["ins"]], refs[plan["ins"] :]
    for keep, got, at, kept, send, place in plan["parts"]:
        rows = ins[keep].shape[0]
        half = rows // 2
        outs[kept][...] = ins[keep][:half].astype(f32) + ins[got][at : at + half].astype(f32)
        low = ins[keep][half:].astype(f32) + ins[got][at + half : at + rows].astype(f32)
        outs[send][place : place + half] = low.astype(bf16)
    for a, b, at, out, turned in adds:
        total = ins[a][...].astype(f32) + ins[b][at : at + ins[a].shape[0]].astype(f32)
        outs[out][...] = total.T if turned else total


def combine(name, parts, groups, adds=()):
    if any(keep.shape[0] % 32 for keep, _, _ in parts) or any(a.shape[0] % 8 for a, *_ in adds):
        total = [k.astype(f32) + g[at : at + k.shape[0]].astype(f32) for k, g, at in parts]
        keeps = [t[: t.shape[0] // 2] for t in total]
        sends = [jnp.concatenate([total[i][total[i].shape[0] // 2 :].astype(bf16) for i in g], 0) for g in groups]
        sums = [a.astype(f32) + b[at : at + a.shape[0]].astype(f32) for a, b, at, _ in adds]
        return keeps, sends, [v.T if turned else v for v, (*_, turned) in zip(sums, adds)]
    arrays, outs, plan, plan_adds = [], [], [], []

    def put(array):
        for i, have in enumerate(arrays):
            if have is array:
                return i
        arrays.append(array)
        return len(arrays) - 1

    for keep, _, _ in parts:
        outs.append(((keep.shape[0] // 2, keep.shape[1]), f32, VMEM))
    for g in groups:
        outs.append(((sum(parts[i][0].shape[0] // 2 for i in g), parts[g[0]][0].shape[1]), bf16, VMEM))
    for number, g in enumerate(groups):
        place = 0
        for i in g:
            keep, got, at = parts[i]
            plan.append((put(keep), put(got), at, i, len(parts) + number, place))
            place += keep.shape[0] // 2
    for a, b, at, turned in adds:
        plan_adds.append((put(a), put(b), at, len(outs), turned))
        outs.append((a.shape[::-1] if turned else a.shape, f32, VMEM))
    got = call(
        functools.partial(combine_kernel, {"ins": len(arrays), "parts": plan}, plan_adds),
        name, outs, [], [], arrays, 4,
    )
    return got[: len(parts)], got[len(parts) : len(parts) + len(groups)], got[len(parts) + len(groups) :]


SMEM = pl.BlockSpec(memory_space=pltpu.SMEM)
HBM, VMEM = pltpu.HBM, pltpu.VMEM


def params(limit):
    return dict(
        compiler_params=pltpu.CompilerParams(vmem_limit_bytes=limit * MIB),
        cost_estimate=pl.CostEstimate(flops=0, bytes_accessed=MIB, transcendentals=0),
    )


def call(body, name, outs, scratch, scalars, args, limit):
    place = lambda where: pl.BlockSpec(memory_space=pltpu.HBM if where is HBM else pltpu.VMEM)
    outs = [(*o, None)[:3] for o in outs]
    args = [a if isinstance(a, tuple) else (a, None) for a in args]
    arrays = [pltpu.with_memory_space_constraint(a, pltpu.HBM) if w is HBM else a for a, w in args]
    return pl.pallas_call(
        body,
        name=name,
        out_shape=[jax.ShapeDtypeStruct(s, d) if w is None else w(s, d) for s, d, w in outs],
        in_specs=[SMEM] * len(scalars) + [place(w) for _, w in args],
        out_specs=[place(w) for *_, w in outs],
        scratch_shapes=[pltpu.VMEM(*v) if isinstance(v, tuple) else pltpu.SemaphoreType.DMA((v,)) for v in scratch],
        **params(limit),
    )(*scalars, *arrays)


def slots(masks):
    offsets = [0]
    for mask in reversed(masks):
        offsets = offsets + [o ^ mask for o in offsets]
    return offsets


def arrange(blocks, offsets, me):
    return jnp.concatenate([lax.dynamic_slice_in_dim(blocks, me ^ o, 1, axis=0) for o in offsets], axis=0)


def exchange(send, mask, count):
    return lax.ppermute(send, "pairs", [(i, i ^ mask) for i in range(count)])


def per_device(
    tokens, cotangent, text_len, word_mask, attn_gain, attn_shift, w_qkv, qv_bias, w_out, out_bias,
    mlp_gain, mlp_shift, w_up, up_bias, w_down, down_bias,
):
    n, seq, width = tokens.shape
    half = w_qkv.shape[2]
    hidden = w_up.shape[1]
    rows = n * seq
    count = lax.axis_size("pairs")
    block = width // count
    head = lax.axis_index("heads")
    me = lax.axis_index("pairs")
    head_s, me_s = head.reshape(1), me.reshape(1)
    bits = count.bit_length() - 1
    order_a = [1 << b for b in range(bits)]
    order_b = order_a[1::-1] + order_a[2:]
    slots_a, slots_b = slots(order_a), slots(order_b)
    tie = lax.optimization_barrier
    tok = tokens.reshape(rows, width)

    w_oth = lax.ppermute(w_qkv, "heads", SWAP)
    bias_own = qv_bias.reshape(width)
    bias_oth = lax.ppermute(bias_own, "heads", SWAP)
    words_oth = lax.ppermute(word_mask, "heads", SWAP)
    cot_oth = lax.ppermute(cotangent, "heads", SWAP)

    qkv_shape = ((n, seq, 3 * half), bf16)
    lse_shape = ((n, 8, seq), f32, VMEM)
    low_rows, high_rows = ((rows, width), bf16), ((rows, width), f32)
    vector = ((width,), f32)
    weights = ((3, width, half), bf16)
    attn_scratch = [qkv_shape, ((rows, 3 * half), f32), ((rows, half), f32), ((n, seq, LANES), f32)]
    normed, qkv_own, ctx_own, lse_own = call(
        functools.partial(first_kernel, n, seq, half),
        "attend_own",
        [(*low_rows, VMEM), (*qkv_shape, HBM), ((rows, half), bf16, VMEM), lse_shape],
        [low_rows, vector, vector, vector, weights, *attn_scratch, 8],
        [text_len, head_s],
        [(tok, HBM), (attn_gain, HBM), (attn_shift, HBM), (bias_own, HBM), (w_qkv, HBM)],
        16,
    )
    qkv_oth, ctx, lse_oth, resid, mlp_low, w_up_here, w_down_here = call(
        functools.partial(second_kernel, n, seq, half),
        "attend_other",
        [
            (*qkv_shape, HBM),
            (*low_rows, HBM),
            lse_shape,
            (*high_rows, HBM),
            (*low_rows, VMEM),
            (w_up.shape, bf16, VMEM),
            (w_down.shape, bf16, VMEM),
        ],
        [
            vector, weights, low_rows, ((width, width), bf16), vector, vector, vector, low_rows, high_rows,
            *attn_scratch, 14,
        ],
        [text_len, head_s],
        [
            normed,
            ctx_own,
            *[
                (v, HBM)
                for v in (bias_oth, w_oth, tok, w_out, out_bias, mlp_gain, mlp_shift, w_up, w_down)
            ],
        ],
        20,
    )
    mlp_oth = lax.ppermute(mlp_low, "heads", SWAP)

    cut = hidden // 2

    def mlp(name, start, outs, args):
        return call(
            functools.partial(mlp_kernel, start, (slots_a, slots_b), block),
            name,
            outs + [((width // 2, cut), bf16, VMEM)] * 4 + [((cut,), f32, VMEM)],
            [((width, cut), bf16)] * 2,
            [me_s],
            args + [w_up_here, w_down_here, up_bias],
            18,
        )

    a_all, g_all, out_part, gmi_part, *first = mlp(
        "mlp_first",
        0,
        [((2 * rows, width), bf16, VMEM)] * 2 + [((2 * rows, width), f32, VMEM)] * 2,
        [mlp_low, mlp_oth, cotangent, word_mask, cot_oth, words_oth],
    )
    def take(keep, send, offsets):
        if block % 16 == 0:
            return keep, send
        total = jnp.concatenate([keep, send], axis=0).reshape(count, block, -1)
        total = arrange(total, offsets, me).reshape(width, -1)
        return total[: width // 2], total[width // 2 :]

    def first_exchange(up_keep, up_send, down_keep, down_send, up_sums):
        up_keep, up_send = take(up_keep, up_send, slots_a)
        down_keep, down_send = take(down_keep, down_send, slots_b)
        return up_keep, exchange(up_send, order_a[0], count), down_keep, exchange(down_send, order_b[0], count)

    def second_exchange(sends):
        return exchange(sends[0], order_a[1], count), exchange(sends[1], order_b[1], count)

    up1, up1_got, down1, down1_got = first_exchange(*first)
    out_send, gmi_send, out_own, gmi_own, *second = mlp(
        "mlp_second",
        cut,
        [((rows, width), bf16)] * 2 + [((rows, width), f32)] * 2,
        [a_all, g_all, out_part, gmi_part],
    )
    gmi_send, up1_got, down1_got, *second = tie((gmi_send, up1_got, down1_got, *second))
    gmi_got = lax.ppermute(gmi_send, "heads", SWAP)
    out_got = lax.ppermute(out_send, "heads", SWAP)
    up2, up2_got, down2, down2_got = first_exchange(*second)

    grad_resid, gc_own, gc_oth, wo_keep, wo_send, sums_mid = call(
        functools.partial(middle_kernel, n, seq, half, block, slots_b),
        "middle",
        [
            (*high_rows, VMEM),
            ((n, seq, half), bf16, VMEM),
            ((n, seq, half), bf16, VMEM),
            *[((width, half) if block % 16 == 0 else (half, width), bf16, VMEM)] * 2,
            ((8, width), f32, VMEM),
        ],
        [((width, width), f32), ((width, half), f32)],
        [me_s, head_s],
        [gmi_own, gmi_got, resid, g_all, mlp_gain, w_out, ctx],
        8,
    )
    if block % 16:
        wo = jnp.concatenate([wo_keep, wo_send], axis=0).reshape(count, 2, block // 2, 2, half)
        wo = arrange(wo, slots_b, me).swapaxes(2, 3)
        wo_keep = lax.dynamic_index_in_dim(wo, head, 1, keepdims=False).reshape(width, half)
        wo_send = lax.dynamic_index_in_dim(wo, 1 - head, 1, keepdims=False).reshape(width, half)
    wo_got = lax.ppermute(wo_send, "heads", SWAP)

    def back(name, qkv, gc, lse, fused, kinds, more):
        wide = width if fused else half
        return call(
            functools.partial(back_kernel, n, seq, half, block, (slots_a, slots_b), fused),
            name,
            [
                ((rows, 3 * half), bf16, VMEM),
                *[((width // 2, 2 * half), k, VMEM) for k in kinds],
                *[((width // 2, wide), k, VMEM) for k in kinds],
                ((8, half), f32, VMEM),
            ],
            [((rows, 3 * half), f32), ((width, 2 * half), kinds[0]), ((width, half), kinds[0])],
            [text_len, head_s, me_s],
            [qkv, gc, lse, normed, *more],
            10,
        )

    (up1, down1), sends1, _ = combine("add_1", [(up1, up1_got, 0), (down1, down1_got, 0)], [[0], [1]])
    qkv_oth, *sends1 = tie((qkv_oth, *sends1))
    up1_got, down1_got = second_exchange(sends1)
    dq_oth, *dw_oth, sums_oth = back("back_other", qkv_oth, gc_oth, lse_oth, False, (bf16, bf16), [])
    dw_got = [lax.ppermute(d, "heads", SWAP) for d in dw_oth]
    up1_got, down1_got, up2_got, down2_got, *dw_oth = tie((up1_got, down1_got, up2_got, down2_got, *dw_oth))
    (up2, down2, up1, down1), (*sends2, wide1), _ = combine(
        "add_2",
        [(up2, up2_got, 0), (down2, down2_got, 0), (up1, up1_got, 0), (down1, down1_got, 0)],
        [[0], [1], [2, 3]],
    )
    qkv_own, wide1, *sends2 = tie((qkv_own, wide1, *sends2))
    up2_got, down2_got = second_exchange(sends2)
    wide1_got = exchange(wide1, order_a[2], count)
    if block % 16:
        dq_own, *dw_own, sums_own = back("back_own", qkv_own, gc_own, lse_own, False, (f32, f32), [])
        qk_keep, qk_send, v_keep, v_send = [d + o.astype(f32) for d, o in zip(dw_own, dw_got)]
        qk_keep, qk_send = take(qk_keep, qk_send, slots_a)
        v_keep, v_send = take(v_keep, v_send, slots_b)
        wo = wo_keep.astype(f32) + wo_got.astype(f32)
        vo_keep = jnp.concatenate([v_keep, wo[: width // 2]], axis=1)
        vo_send = jnp.concatenate([v_send, wo[width // 2 :]], axis=1).astype(bf16)
        qk_send = qk_send.astype(bf16)
    else:
        dq_own, qk_keep, qk_send, vo_keep, vo_send, sums_own = back(
            "back_own", qkv_own, gc_own, lse_own, True, (f32, bf16), [*dw_got, wo_keep, wo_got]
        )
    at = up1.shape[0]
    up2_got, down2_got, wide1_got, dq_own = tie((up2_got, down2_got, wide1_got, dq_own))
    (up2, down2, up1, down1), (wide2, wide1), _ = combine(
        "add_3",
        [(up2, up2_got, 0), (down2, down2_got, 0), (up1, wide1_got, 0), (down1, wide1_got, at)],
        [[0, 1], [2, 3]],
    )
    qk_send, vo_send, wide1, wide2, dq_own = tie((qk_send, vo_send, wide1, wide2, dq_own))
    qk_got = exchange(qk_send, order_a[0], count)
    vo_got = exchange(vo_send, order_b[0], count)
    wide1_got = exchange(wide1, order_a[3], count)
    wide2_got = exchange(wide2, order_a[2], count)
    grad_tok, layer_out, vecs = call(
        functools.partial(last_kernel, half),
        "last",
        [high_rows, low_rows, ((8, max(2 * width, hidden)), f32, VMEM)],
        [],
        [head_s],
        [
            dq_own, dq_oth, w_qkv, w_oth, tok, attn_gain, grad_resid, sums_mid, sums_own, sums_oth,
            first[-1], second[-1], resid, out_own, out_got, down_bias,
        ],
        10,
    )
    vecs_got = lax.ppermute(vecs, "heads", SWAP)
    qk_got, vo_got, wide1_got, wide2_got, vecs_got = tie((qk_got, vo_got, wide1_got, wide2_got, vecs_got))
    at = up1.shape[0]
    (qk, vo, up2, down2), (qk_send, vo_send, wide2), (vecs,) = combine(
        "add_4",
        [(qk_keep, qk_got, 0), (vo_keep, vo_got, 0), (up2, wide2_got, 0), (down2, wide2_got, 2 * at)],
        [[0], [1], [2, 3]],
        [(vecs, vecs_got, 0, False)],
    )
    qk_got = exchange(qk_send, order_a[1], count)
    vo_got = exchange(vo_send, order_b[1], count)
    wide2_got = exchange(wide2, order_a[3], count)
    around = lambda a, b: [exchange(vecs, mask, count) for mask in (a, b, a ^ b)]
    vecs_gots = around(order_a[0], order_a[1])
    qk_got, vo_got, wide2_got, *vecs_gots = tie((qk_got, vo_got, wide2_got, *vecs_gots))
    part, up_part = width // count // 2, hidden // count
    index = (me * 2 + head).reshape(1)
    shares = [((part,), f32)] * 6 + [((2, part), f32), ((up_part,), f32)]
    if bits == 4 and block % 16 == 0:
        qk, vo, *sends, vecs = call(
            fan_kernel,
            "add_5",
            [((block, width), f32, VMEM)] * 2 + [((2 * block, width), bf16, VMEM)] * 3 + [(vecs.shape, f32, VMEM)],
            [],
            [],
            [qk, qk_got, vo, vo_got, vecs, *vecs_gots],
            4,
        )
        masks = (order_a[3], order_a[2], order_a[2] ^ order_a[3])
        gots = [exchange(send, mask, count) for send, mask in zip(sends, masks)]
        vecs_gots = around(order_a[2], order_a[3])
        grad_w_up, grad_w_down = call(
            wide_kernel, "add_wide", [((block, hidden), f32)] * 2, [], [], [up1, down1, wide1_got, up2, down2, wide2_got], 4
        )
        grad_w_up, grad_w_down, *gots = tie((grad_w_up, grad_w_down, *gots))
        grad_w_qkv, grad_w_out, *piece = call(
            functools.partial(finish_kernel, count, width, hidden),
            "finish",
            [((3, block, half), f32), ((block // 2, width), f32)] + shares,
            [],
            [index],
            [qk, vo, vecs, *gots, *vecs_gots],
            4,
        )
        grad_w_down = grad_w_down.T
    else:
        vecs = vecs + sum(vecs_gots)
        for mask in order_a[4:]:
            at = up1.shape[0]
            (up1, down1, up2, down2), (wide1, wide2), _ = combine(
                "add_more",
                [(up1, wide1_got, 0), (down1, wide1_got, at), (up2, wide2_got, 0), (down2, wide2_got, at)],
                [[0, 1], [2, 3]],
            )
            wide1_got, wide2_got = exchange(wide1, mask, count), exchange(wide2, mask, count)
        at = up1.shape[0]
        grads = [k + g[p : p + at] for k, g, p in
                 ((up1, wide1_got, 0), (up2, wide2_got, 0), (down1, wide1_got, at), (down2, wide2_got, at))]
        grad_w_up = jnp.concatenate(grads[:2], axis=1)
        grad_w_down = jnp.concatenate(grads[2:], axis=1).T
        qk, vo = qk + qk_got.astype(f32), vo + vo_got.astype(f32)
        for mask in order_a[2:]:
            at = qk.shape[0] // 2
            got = exchange(jnp.concatenate([qk[at:], vo[at:]]).astype(bf16), mask, count).astype(f32)
            qk, vo = qk[:at] + got[:at], vo[:at] + got[at:]
            before, vecs_got = vecs, exchange(vecs, mask, count)
            vecs = vecs + vecs_got
        grad_w_qkv = jnp.stack([qk[:, :half], qk[:, half:], vo[:, :half]], axis=0)
        grad_w_out = jnp.concatenate([vo[: block // 2, half:], vo[block // 2 :, half:]], axis=1)
        piece = call(
            functools.partial(spread_kernel, count, width, hidden), "spread", shares, [], [index], [before, vecs_got], 4
        )
    return (
        layer_out.reshape(n, seq, width),
        grad_tok.reshape(n, seq, width),
        piece[0],
        piece[1],
        grad_w_qkv,
        piece[6],
        grad_w_out,
        piece[4],
        piece[2],
        piece[3],
        grad_w_up,
        piece[7],
        grad_w_down,
        piece[5],
    )


def solution(mesh):
    in_specs = (
        P(("pairs", "heads"), None, None),
        P(("pairs", "heads"), None, None),
        P("pairs"),
        P(("pairs", "heads"), None),
        P(),
        P(),
        P(None, None, "heads"),
        P(None, "heads"),
        P(),
        P(),
        P(),
        P(),
        P(None, "heads"),
        P("heads"),
        P("heads", None),
        P(),
    )
    out_specs = (
        P(("pairs", "heads"), None, None),
        P(("pairs", "heads"), None, None),
        P(("pairs", "heads")),
        P(("pairs", "heads")),
        P(None, "pairs", "heads"),
        P(None, ("pairs", "heads")),
        P(("pairs", "heads"), None),
        P(("pairs", "heads")),
        P(("pairs", "heads")),
        P(("pairs", "heads")),
        P("pairs", "heads"),
        P(("pairs", "heads")),
        P("heads", "pairs"),
        P(("pairs", "heads")),
    )
    return jax.shard_map(
        per_device, mesh=mesh, in_specs=in_specs, out_specs=out_specs, check_vma=False
    )
```

```python
import functools
import math

import jax
import jax.numpy as jnp
from jax import lax
from jax.experimental import pallas as pl
from jax.experimental.pallas import tpu as pltpu
from jax.sharding import PartitionSpec as P

HEAD_DIM = 64
WORDS = 40
LANES = 128
EPSILON = 1e-06
MASKED = -1000000000.0
SWAP = [(0, 1), (1, 0)]
f32, bf16 = jnp.float32, jnp.bfloat16
MIB = 1024 * 1024


def dot(a, b, ca=1, cb=0):
    return lax.dot_general(a, b, (((ca,), (cb,)), ((), ())), preferred_element_type=f32)


def centre(rows):
    mean_val = jnp.mean(rows, axis=-1, keepdims=True)
    centred = rows - mean_val
    inv_std = lax.rsqrt(jnp.mean(centred * centred, axis=-1, keepdims=True) + EPSILON)
    return centred * inv_std, inv_std


def norm_back(grad_rows, unit_rows, inv_std, gain):
    scaled = grad_rows * gain
    first = jnp.mean(scaled, axis=-1, keepdims=True)
    second = jnp.mean(scaled * unit_rows, axis=-1, keepdims=True)
    return inv_std * (scaled - first - unit_rows * second)


def col_sum(rows):
    return jnp.sum(rows, axis=0, keepdims=True)


def gelu_parts(v):
    u = jnp.abs(v) * 0.7071067811865476
    t = 1.0 / (1.0 + 0.39 * u)
    poly = 0.8866643918219983 - 0.22753713046899435 * t
    poly = -0.6354003145887568 + poly * t
    poly = 0.6495594277724073 + poly * t
    poly = 0.09138840279707615 + poly * t
    poly = 0.23532522096757497 + poly * t
    bell = jnp.exp(v * v * -0.5)
    tail = (0.5 * t) * poly * bell
    cdf = jnp.where(v < 0.0, tail, 1.0 - tail)
    return v * cdf, cdf + v * (bell * 0.3989422804014327)


def as_row(ref):
    return ref[...].astype(f32).reshape(1, ref.shape[0])


def half_mask(value, lane, e):
    keep = (lane < HEAD_DIM) if e == 0 else (lane >= HEAD_DIM)
    return jnp.where(keep, value, jnp.zeros_like(value))


def mask_words(scores, key_ok):
    return jnp.concatenate([jnp.where(key_ok, scores[:WORDS], MASKED), scores[WORDS:]], axis=0)


def attend(n, seq, half, len_ref, head_ref, proj, ctx, lse_ref):
    scale = 1.0 / math.sqrt(HEAD_DIM)
    lane = lax.broadcasted_iota(jnp.int32, (seq, LANES), 1)
    key = lax.broadcasted_iota(jnp.int32, (WORDS, 1), 0)
    first = head_ref[0] * n

    def step(hp, carry):
        off = pl.multiple_of(hp * LANES, LANES)
        for i in range(n):
            rows = pl.ds(i * seq, seq)
            q2 = proj[rows, pl.ds(off, LANES)] * scale
            k2 = proj[rows, pl.ds(half + off, LANES)].astype(bf16)
            vt = proj[rows, pl.ds(2 * half + off, LANES)].astype(bf16).T
            key_ok = key < len_ref[first + i]
            outs = []
            for e in range(2):
                s = mask_words(dot(k2, half_mask(q2, lane, e).astype(bf16), 1, 1), key_ok)
                top = jnp.max(s, axis=0, keepdims=True)
                w = jnp.exp(s - top)
                total = jnp.sum(w, axis=0, keepdims=True)
                lse_ref[i, pl.ds(2 * hp + e, 1), :] = top + jnp.log(total)
                outs.append(dot(vt[e * HEAD_DIM : (e + 1) * HEAD_DIM], w.astype(bf16)) * (1.0 / total))
            ctx[rows, pl.ds(off, LANES)] = jnp.concatenate(outs, axis=0).T
        return carry

    lax.fori_loop(0, half // LANES, step, 0)


def project(normed, w, ready, bias, half, proj):
    for t in range(3):
        if ready is not None:
            ready[t].wait()
        part = dot(normed, w[t])
        if t != 1:
            part = part + bias[t // 2 : t // 2 + 1]
        proj[:, t * half : (t + 1) * half] = part.astype(bf16).astype(f32)


def bring(pairs, sems):
    copies = [pltpu.make_async_copy(a, b, sems.at[i]) for i, (a, b) in enumerate(pairs)]
    for c in copies:
        c.start()
    return copies


def first_kernel(
    n, seq, half, head_ref, len_h, tok_h, gain_h, shift_h, bias_h, w_h, normed, qkv_h, ctx, lse,
    lens, tok, gain, shift, bias, w, qkv, proj, ctx32, sems,
):
    copies = bring(
        [(tok_h, tok), (gain_h, gain), (shift_h, shift), (bias_h, bias)]
        + [(w_h.at[t], w.at[t]) for t in range(3)]
        + [(len_h, lens)],
        sems,
    )
    for c in copies[:4]:
        c.wait()
    unit, _ = centre(tok[...].astype(f32))
    rows = (unit * as_row(gain) + as_row(shift)).astype(bf16)
    normed[...] = rows
    project(rows, w, copies[4:7], bias, half, proj)
    for i in range(n):
        qkv[i] = proj[pl.ds(i * seq, seq)].astype(bf16)
    leave = pltpu.make_async_copy(qkv, qkv_h, sems.at[8])
    leave.start()
    copies[7].wait()
    attend(n, seq, half, lens, head_ref, proj, ctx32, lse)
    ctx[...] = ctx32[...].astype(bf16)
    leave.wait()


def second_kernel(
    n, seq, half, head_ref, normed, ctx_own, bias_h, w_h, len_h, cot_h, cot_oth_h, words_h, words_oth_h, tok_h, w_out_h,
    out_bias_h, gain_h, shift_h, qkv_h, ctx_h, lse, resid_h, mlp_low, g_all,
    lens, bias, w, cot, cot_oth, words, words_oth, tok, w_out, out_bias, gain, shift, ctx, resid, qkv, proj, ctx32,
    masked, sems,
):
    copies = bring(
        [(bias_h, bias)]
        + [(w_h.at[t], w.at[t]) for t in range(3)]
        + [(len_h, lens), (cot_h, cot), (cot_oth_h, cot_oth), (words_h, words), (words_oth_h, words_oth)]
        + [(tok_h, tok), (w_out_h, w_out), (out_bias_h, out_bias), (gain_h, gain), (shift_h, shift)],
        sems,
    )
    copies[0].wait()
    project(normed[...], w, copies[1:4], bias, half, proj)
    for i in range(n):
        qkv[i] = proj[pl.ds(i * seq, seq)].astype(bf16)
    leave = [pltpu.make_async_copy(qkv, qkv_h, sems.at[14])]
    leave[0].start()
    ctx[:, :half] = ctx_own[...]
    for c in copies[4:9]:
        c.wait()
    at = 0
    for rows_g, keep in ((cot, words), (cot_oth, words_oth)):
        keep = keep[...].astype(f32).T
        for i in range(n):
            masked[at : at + WORDS] = rows_g[i, :WORDS].astype(f32) * keep[:, i : i + 1]
            masked[at + WORDS : at + seq] = rows_g[i, WORDS:].astype(f32)
            at += seq
    g_all[...] = masked[...].astype(bf16)
    attend(n, seq, half, lens, head_ref, proj, ctx32, lse)
    ctx[:, half:] = ctx32[...].astype(bf16)
    leave.append(pltpu.make_async_copy(ctx, ctx_h, sems.at[15]))
    leave[1].start()
    for c in copies[9:14]:
        c.wait()
    own = pl.multiple_of(head_ref[0] * half, LANES)
    oth = pl.multiple_of((1 - head_ref[0]) * half, LANES)
    attn = dot(ctx[:, :half], w_out[pl.ds(own, half)]) + dot(ctx[:, half:], w_out[pl.ds(oth, half)])
    total = tok[...].astype(f32) + (attn + as_row(out_bias))
    resid[...] = total
    leave.append(pltpu.make_async_copy(resid, resid_h, sems.at[16]))
    leave[2].start()
    unit, _ = centre(total)
    mlp_low[...] = (unit * as_row(gain) + as_row(shift)).astype(bf16)
    for c in leave:
        c.wait()


def mlp_kernel(start, masks, block, me_ref, *refs):
    if start == 0:
        own, oth, g, bias, up_h, down_h, a, up_later, down_later, *refs, up, down, sems = refs
        cut = down.shape[0]
        cuts = [pl.ds(0, cut), pl.ds(cut, cut)]
        copies = bring(
            [(up_h.at[:, cuts[0]], up), (down_h.at[cuts[0]], down)]
            + [(up_h.at[:, cuts[1]], up_later), (down_h.at[cuts[1]], down_later)],
            sems,
        )
        rows = own.shape[0]
        a[:rows], a[rows:] = own[...], oth[...]
    else:
        a, g, out_in, gmi_in, up, bias, down, out_send, gmi_send, *refs = refs
    out_acc, gmi_acc, up_keep, up_send, down_keep, down_send, d_bias, scr_up, scr_down = refs
    cut = d_bias.shape[0]
    units = pl.ds(start, cut)
    if start == 0:
        copies[0].wait()
        copies[1].wait()
    w_up, w_down = up[...], down[...]
    act, slope = gelu_parts(dot(a[...], w_up) + bias[units].astype(f32).reshape(1, cut))
    act = act.astype(bf16)
    grad = (dot(g[...], w_down, 1, 1) * slope).astype(bf16)
    ordered(dot(a[...], grad, 0, 0), scr_up, up_keep, up_send, masks[0], block, me_ref)
    ordered(dot(g[...], act, 0, 0), scr_down, down_keep, down_send, masks[1], block, me_ref)
    d_bias[...] = col_sum(grad.astype(f32)).reshape(cut)
    out, gmi = dot(act, w_down), dot(grad, w_up, 1, 1)
    if start == 0:
        out_acc[...], gmi_acc[...] = out, gmi
        copies[2].wait()
        copies[3].wait()
        return
    rows = out_acc.shape[0]
    out, gmi = out_in[...] + out, gmi_in[...] + gmi
    out_acc[...], gmi_acc[...] = out[:rows], gmi[:rows]
    out_send[...], gmi_send[...] = out[rows:].astype(bf16), gmi[rows:].astype(bf16)


def ordered(value, scr, keep, send, offsets, block, me_ref, got=()):
    half, cols = keep.shape[0], pl.ds(0, value.shape[1])
    if block % 16:
        keep[:, cols] = value[:half].astype(keep.dtype)
        send[:, cols] = value[half:].astype(send.dtype)
        return
    scr[...] = value.astype(scr.dtype)
    for slot, offset in enumerate(offsets):
        late = slot * block >= half
        dest, at = (send, pl.ds(slot * block - half, block)) if late else (keep, pl.ds(slot * block, block))
        part = scr[pl.ds(pl.multiple_of((me_ref[0] ^ offset) * block, 16), block)]
        if got:
            part = part + got[late][at].astype(f32)
        dest[at, cols] = part.astype(dest.dtype)


def middle_kernel(
    n, seq, half, block, offsets, me_ref, head_ref, gmi_own, gmi_got, resid, g_all, gain, w_out, ctx,
    grad_resid, gc_own, gc_oth, keep, send, sums, scr, cuts,
):
    unit, inv_std = centre(resid[...])
    gmi = gmi_own[...] + gmi_got[...].astype(f32)
    g_final = g_all[: gmi_own.shape[0]].astype(f32)
    total = g_final + norm_back(gmi, unit, inv_std, as_row(gain))
    grad_resid[...] = total
    low = total.astype(bf16)
    sums[...] = jnp.zeros_like(sums)
    sums[0:1] = col_sum(gmi * unit)
    sums[1:2] = col_sum(gmi)
    sums[2:3] = col_sum(low.astype(f32))
    sums[3:4] = col_sum(g_final)
    own = pl.multiple_of(head_ref[0] * half, LANES)
    oth = pl.multiple_of((1 - head_ref[0]) * half, LANES)
    for dest, at in ((gc_own, own), (gc_oth, oth)):
        part = dot(low, w_out[pl.ds(at, half)], 1, 1)
        for i in range(n):
            dest[i] = part[i * seq : (i + 1) * seq].astype(bf16)
    scr[pl.ds(own, half)] = dot(ctx[:, :half], low, 0, 0)
    scr[pl.ds(oth, half)] = dot(ctx[:, half:], low, 0, 0)
    if block % 16:
        keep[...] = scr[:half].astype(bf16)
        send[...] = scr[half:].astype(bf16)
        return
    part = block // 2
    for dest, core in ((keep, head_ref[0]), (send, 1 - head_ref[0])):
        for slot, offset in enumerate(offsets):
            at = pl.multiple_of((me_ref[0] ^ offset) * block + core * part, 8)
            cuts[slot * block : slot * block + part] = scr[pl.ds(at, part), :half]
            cuts[slot * block + part : (slot + 1) * block] = scr[pl.ds(at, part), half:]
        dest[...] = cuts[...].astype(bf16)


def back_kernel(n, seq, half, block, masks, fused, len_ref, head_ref, me_ref, qkv, gc, lse, normed, *rest):
    if fused:
        got_qk, got_v, (wo, wo_got), rest = rest[:2], rest[2:4], rest[4:6], rest[6:]
    else:
        got_qk = got_v = ()
    dqkv, qk_keep, qk_send, v_keep, v_send, sums, grads, scr_qk, scr_v = rest
    scale = 1.0 / math.sqrt(HEAD_DIM)
    lane = lax.broadcasted_iota(jnp.int32, (seq, LANES), 1)
    key = lax.broadcasted_iota(jnp.int32, (WORDS, 1), 0)
    first = head_ref[0] * n

    def step(hp, carry):
        off = pl.multiple_of(hp * LANES, LANES)
        for i in range(n):
            q2 = qkv[i, :, pl.ds(off, LANES)]
            k2 = qkv[i, :, pl.ds(half + off, LANES)]
            v2 = qkv[i, :, pl.ds(2 * half + off, LANES)]
            g2 = gc[i, :, pl.ds(off, LANES)]
            kt = k2.T
            key_ok = key < len_ref[first + i]
            dq, dk, dv = [], [], []
            for e in range(2):
                qm = half_mask(q2, lane, e) * jnp.asarray(scale, bf16)
                s = mask_words(dot(k2, qm, 1, 1), key_ok)
                p = jnp.exp(s - lse[i, pl.ds(2 * hp + e, 1), :])
                dp = dot(v2, half_mask(g2, lane, e), 1, 1)
                inner = jnp.sum(p * dp, axis=0, keepdims=True)
                ds = (p * (dp - inner)).astype(bf16)
                dv.append(dot(p.astype(bf16), g2))
                dk.append(dot(ds, q2))
                dq.append(dot(kt[e * HEAD_DIM : (e + 1) * HEAD_DIM], ds))
            rows = pl.ds(i * seq, seq)
            grads[rows, pl.ds(off, LANES)] = jnp.concatenate(dq, axis=0).T * scale
            grads[rows, pl.ds(half + off, LANES)] = jnp.where(lane < HEAD_DIM, dk[0], dk[1]) * scale
            grads[rows, pl.ds(2 * half + off, LANES)] = jnp.where(lane < HEAD_DIM, dv[0], dv[1])
        return carry

    lax.fori_loop(0, half // LANES, step, 0)
    low = grads[...].astype(bf16)
    dqkv[...] = low
    sums[...] = jnp.zeros_like(sums)
    sums[0:1] = col_sum(low[:, :half].astype(f32))
    sums[1:2] = col_sum(low[:, 2 * half :].astype(f32))
    rows = normed[...]
    ordered(dot(rows, low[:, : 2 * half], 0, 0), scr_qk, qk_keep, qk_send, masks[0], block, me_ref, got_qk)
    ordered(dot(rows, low[:, 2 * half :], 0, 0), scr_v, v_keep, v_send, masks[1], block, me_ref, got_v)
    if fused:
        at = v_keep.shape[0]
        both = wo[...].astype(f32) + wo_got[...].astype(f32)
        v_keep[:, half:] = both[:at]
        v_send[:, half:] = both[at:].astype(bf16)


def last_kernel(
    half, head_ref, dq_own, dq_oth, w_own, w_oth, tok, gain, grad_resid, sums_mid, sums_own, sums_oth, up_first, up_second,
    resid, out_own, out_got, down_bias, grad_tokens, layer_out, vecs,
):
    grad = None
    for dq, w in ((dq_own, w_own), (dq_oth, w_oth)):
        for t in range(3):
            part = dot(dq[:, t * half : (t + 1) * half], w[t], 1, 1)
            grad = part if grad is None else grad + part
    unit, inv_std = centre(tok[...].astype(f32))
    layer_out[...] = (resid[...] + (out_own[...] + out_got[...].astype(f32) + as_row(down_bias))).astype(bf16)
    width = 2 * half
    grad_tokens[...] = grad_resid[...] + norm_back(grad, unit, inv_std, as_row(gain))
    width = 2 * half
    vecs[...] = jnp.zeros_like(vecs)
    vecs[0:1, :width], vecs[0:1, width:] = col_sum(grad * unit), col_sum(grad)
    vecs[1:2, :width], vecs[1:2, width:] = sums_mid[0:1], sums_mid[1:2]
    vecs[2:3, :width], vecs[2:3, width:] = sums_mid[2:3], sums_mid[3:4]
    first = head_ref[0] == 0
    for i in range(2):
        own, oth = sums_own[i : i + 1], sums_oth[i : i + 1]
        vecs[3:4, i * width : i * width + half] = jnp.where(first, own, oth)
        vecs[3:4, i * width + half : (i + 1) * width] = jnp.where(first, oth, own)
    for place, sums in enumerate((up_first, up_second)):
        up = as_row(sums)
        cut = up.shape[1]
        for i in range(2):
            at = place * cut
            vecs[4 + i : 5 + i, at : at + cut] = jnp.where(head_ref[0] == i, up, jnp.zeros_like(up))


def spread_vectors(count, width, hidden, index, total, outs):
    lanes = total.shape[1]
    part = width // count // 2
    rolled = pltpu.roll(total, lanes - index * part, 1)
    for i in range(6):
        at = (i % 2) * width
        outs[i][...] = rolled[i // 2 : i // 2 + 1, at : at + part].reshape(part)
    for i in range(2):
        outs[6][i : i + 1] = rolled[3:4, i * width : i * width + part]
    part = hidden // count
    up = jnp.where(index < count, total[4:5], total[5:6])
    up = pltpu.roll(jnp.concatenate([up] * 8, axis=0), lanes - (index % count) * part, 1)
    outs[7][...] = up[0:1, :part].reshape(part)


def spread_kernel(count, width, hidden, index_ref, vec, vec_got, *outs):
    spread_vectors(count, width, hidden, index_ref[0], vec[...] + vec_got[...], outs)


def pack(vec):
    width = vec.shape[1] // 2
    rows = jnp.concatenate([vec[:, :width], vec[:, width:]], axis=0)
    high = rows.astype(bf16)
    return high, (rows - high.astype(f32)).astype(bf16)


def unpack(got, at):
    rows = got[at : at + 16].astype(f32) + got[at + 16 : at + 32].astype(f32)
    return jnp.concatenate([rows[:8], rows[8:]], axis=1)


def append(send, at, vec):
    send[at : at + 16], send[at + 16 : at + 32] = pack(vec)


def third_kernel(
    qk, qk_got, vo, vo_got, up, down, wide_got, vec, vec_got,
    qk_keep, vo_keep, up_keep, down_keep, qk_send, vo_send, wide_send, vec_keep,
):
    total = vec[...] + vec_got[...]
    vec_keep[...] = total
    half = qk_keep.shape[0]
    append(qk_send, half, total)
    for have, got, keep, send in ((qk, qk_got, qk_keep, qk_send), (vo, vo_got, vo_keep, vo_send)):
        keep[...] = have[:half] + got[:half].astype(f32)
        send[:half] = (have[half:] + got[half:].astype(f32)).astype(bf16)
    half = up_keep.shape[0]
    for i, (have, keep) in enumerate(((up, up_keep), (down, down_keep))):
        at = 2 * half * i
        keep[...] = have[:half] + wide_got[at : at + half].astype(f32)
        low = have[half:] + wide_got[at + half : at + 2 * half].astype(f32)
        wide_send[i * half : (i + 1) * half] = low.astype(bf16)


def fan_kernel(qk, qk_got, vo, vo_got, vec, qk_keep, vo_keep, send1, send2, send3, vec_keep):
    block = qk.shape[0] // 4
    total = vec[...] + unpack(qk_got, 4 * block)
    vec_keep[...] = total
    for place, (have, got, keep) in enumerate(((qk, qk_got, qk_keep), (vo, vo_got, vo_keep))):
        keep[...] = have[:block] + got[:block].astype(f32)
        for i, send in enumerate((send1, send2, send3)):
            at = pl.ds((i + 1) * block, block)
            send[place * block : (place + 1) * block] = (have[at] + got[at].astype(f32)).astype(bf16)
    for send in (send1, send2, send3):
        append(send, 2 * block, total)


def finish_kernel(count, width, hidden, index_ref, qk, vo, vec, *refs):
    gots, (w_qkv, w_out, *outs) = refs[:3], refs[3:]
    block, half = qk.shape[0], width // 2
    both = [have[...] + sum(g[i * block : (i + 1) * block].astype(f32) for g in gots) for i, have in enumerate((qk, vo))]
    w_qkv[0], w_qkv[1], w_qkv[2] = both[0][:, :half], both[0][:, half:], both[1][:, :half]
    part = block // 2
    w_out[:, :half], w_out[:, half:] = both[1][:part, half:], both[1][part:, half:]
    spread_vectors(count, width, hidden, index_ref[0], vec[...] + sum(unpack(g, 2 * block) for g in gots), outs)


def wide_kernel(up1, down1, got1, up2, down2, got2, up, down):
    block = up1.shape[0]
    for place, (a, b, got) in enumerate(((up1, down1, got1), (up2, down2, got2))):
        at = pl.ds(place * a.shape[1], a.shape[1])
        up[:, at] = a[...] + got[:block].astype(f32)
        down[:, at] = b[...] + got[block:].astype(f32)


def combine_kernel(plan, adds, *refs):
    ins, outs = refs[: plan["ins"]], refs[plan["ins"] :]
    for keep, got, at, kept, send, place in plan["parts"]:
        rows = ins[keep].shape[0]
        half = rows // 2
        outs[kept][...] = ins[keep][:half].astype(f32) + ins[got][at : at + half].astype(f32)
        low = ins[keep][half:].astype(f32) + ins[got][at + half : at + rows].astype(f32)
        outs[send][place : place + half] = low.astype(bf16)
    for a, b, at, out, turned in adds:
        total = ins[a][...].astype(f32) + ins[b][at : at + ins[a].shape[0]].astype(f32)
        outs[out][...] = total.T if turned else total


def combine(name, parts, groups, adds=()):
    if any(keep.shape[0] % 32 for keep, _, _ in parts) or any(a.shape[0] % 8 for a, *_ in adds):
        total = [k.astype(f32) + g[at : at + k.shape[0]].astype(f32) for k, g, at in parts]
        keeps = [t[: t.shape[0] // 2] for t in total]
        sends = [jnp.concatenate([total[i][total[i].shape[0] // 2 :].astype(bf16) for i in g], 0) for g in groups]
        sums = [a.astype(f32) + b[at : at + a.shape[0]].astype(f32) for a, b, at, _ in adds]
        return keeps, sends, [v.T if turned else v for v, (*_, turned) in zip(sums, adds)]
    arrays, outs, plan, plan_adds = [], [], [], []

    def put(array):
        for i, have in enumerate(arrays):
            if have is array:
                return i
        arrays.append(array)
        return len(arrays) - 1

    for keep, _, _ in parts:
        outs.append(((keep.shape[0] // 2, keep.shape[1]), f32, VMEM))
    for g in groups:
        outs.append(((sum(parts[i][0].shape[0] // 2 for i in g), parts[g[0]][0].shape[1]), bf16, VMEM))
    for number, g in enumerate(groups):
        place = 0
        for i in g:
            keep, got, at = parts[i]
            plan.append((put(keep), put(got), at, i, len(parts) + number, place))
            place += keep.shape[0] // 2
    for a, b, at, turned in adds:
        plan_adds.append((put(a), put(b), at, len(outs), turned))
        outs.append((a.shape[::-1] if turned else a.shape, f32, VMEM))
    got = call(
        functools.partial(combine_kernel, {"ins": len(arrays), "parts": plan}, plan_adds),
        name, outs, [], [], arrays, 4,
    )
    return got[: len(parts)], got[len(parts) : len(parts) + len(groups)], got[len(parts) + len(groups) :]


SMEM = pl.BlockSpec(memory_space=pltpu.SMEM)
HBM, VMEM = pltpu.HBM, pltpu.VMEM


def params(limit):
    return dict(
        compiler_params=pltpu.CompilerParams(vmem_limit_bytes=limit * MIB),
        cost_estimate=pl.CostEstimate(flops=0, bytes_accessed=MIB, transcendentals=0),
    )


def scratch_of(what):
    if what == 0:
        return pltpu.SemaphoreType.DMA
    if isinstance(what, int):
        return pltpu.SemaphoreType.DMA((what,))
    return (what[2] if len(what) > 2 else VMEM)(*what[:2])


def call(body, name, outs, scratch, scalars, args, limit):
    place = lambda where: pl.BlockSpec(memory_space=pltpu.HBM if where is HBM else pltpu.VMEM)
    outs = [(*o, None)[:3] for o in outs]
    args = [a if isinstance(a, tuple) else (a, None) for a in args]
    arrays = [pltpu.with_memory_space_constraint(a, pltpu.HBM) if w is HBM else a for a, w in args]
    return pl.pallas_call(
        body,
        name=name,
        out_shape=[jax.ShapeDtypeStruct(s, d) if w is None else w(s, d) for s, d, w in outs],
        in_specs=[SMEM] * len(scalars) + [place(w) for _, w in args],
        out_specs=[place(w) for *_, w in outs],
        scratch_shapes=[scratch_of(v) for v in scratch],
        **params(limit),
    )(*scalars, *arrays)


def slots(masks):
    offsets = [0]
    for mask in reversed(masks):
        offsets = offsets + [o ^ mask for o in offsets]
    return offsets


def arrange(blocks, offsets, me):
    return jnp.concatenate([lax.dynamic_slice_in_dim(blocks, me ^ o, 1, axis=0) for o in offsets], axis=0)


def exchange(send, mask, count):
    return lax.ppermute(send, "pairs", [(i, i ^ mask) for i in range(count)])


def per_device(
    tokens, cotangent, text_len, word_mask, attn_gain, attn_shift, w_qkv, qv_bias, w_out, out_bias,
    mlp_gain, mlp_shift, w_up, up_bias, w_down, down_bias,
):
    n, seq, width = tokens.shape
    half = w_qkv.shape[2]
    hidden = w_up.shape[1]
    rows = n * seq
    count = lax.axis_size("pairs")
    block = width // count
    head = lax.axis_index("heads")
    me = lax.axis_index("pairs")
    head_s, me_s = head.reshape(1), me.reshape(1)
    bits = count.bit_length() - 1
    order_a = [1 << b for b in range(bits)]
    order_b = order_a[1::-1] + order_a[2:]
    slots_a, slots_b = slots(order_a), slots(order_b)
    tie = lax.optimization_barrier
    tok = tokens.reshape(rows, width)

    w_oth = lax.ppermute(w_qkv, "heads", SWAP)
    bias_oth = lax.ppermute(qv_bias, "heads", SWAP)
    words_oth = lax.ppermute(word_mask, "heads", SWAP)
    cot_oth = lax.ppermute(cotangent, "heads", SWAP)

    qkv_shape = ((n, seq, 3 * half), bf16)
    lse_shape = ((n, 8, seq), f32, VMEM)
    low_rows, high_rows = ((rows, width), bf16), ((rows, width), f32)
    vector = ((width,), f32)
    weights = ((3, width, half), bf16)
    bias = ((2, half), f32)
    lens = (text_len.shape, jnp.int32, pltpu.SMEM)
    attn_scratch = [qkv_shape, ((rows, 3 * half), f32), ((rows, half), f32)]
    normed, qkv_own, ctx_own, lse_own = call(
        functools.partial(first_kernel, n, seq, half),
        "attend_own",
        [(*low_rows, VMEM), (*qkv_shape, HBM), ((rows, half), bf16, VMEM), lse_shape],
        [lens, low_rows, vector, vector, bias, weights, *attn_scratch, 9],
        [head_s],
        [(v, HBM) for v in (text_len, tok, attn_gain, attn_shift, qv_bias, w_qkv)],
        40,
    )
    w_oth, bias_oth, words_oth, cot_oth, normed = tie((w_oth, bias_oth, words_oth, cot_oth, normed))
    qkv_oth, ctx, lse_oth, resid, mlp_low, g_all = call(
        functools.partial(second_kernel, n, seq, half),
        "attend_other",
        [
            (*qkv_shape, HBM),
            (*low_rows, HBM),
            lse_shape,
            (*high_rows, HBM),
            (*low_rows, VMEM),
            ((2 * rows, width), bf16, VMEM),
        ],
        [
            lens, bias, weights, *[((n, seq, width), bf16)] * 2, *[(word_mask.shape, jnp.int32)] * 2, low_rows,
            ((width, width), bf16), vector, vector, vector, low_rows, high_rows, *attn_scratch,
            ((2 * rows, width), f32), 17,
        ],
        [head_s],
        [normed, ctx_own]
        + [
            (v, HBM)
            for v in (
                bias_oth, w_oth, text_len, cotangent, cot_oth, word_mask, words_oth, tok, w_out, out_bias, mlp_gain,
                mlp_shift,
            )
        ],
        26,
    )
    mlp_oth = lax.ppermute(mlp_low, "heads", SWAP)

    cut = hidden // 2

    def mlp(name, start, outs, args):
        return call(
            functools.partial(mlp_kernel, start, (slots_a, slots_b), block),
            name,
            outs + [((width // 2, cut), bf16, VMEM)] * 4 + [((cut,), f32, VMEM)],
            [((width, cut), bf16)] * 2 + ([((width, cut), bf16), ((cut, width), bf16), 4] if start == 0 else []),
            [me_s],
            args,
            20,
        )

    a_all, up_later, down_later, out_part, gmi_part, *first = mlp(
        "mlp_first",
        0,
        [((2 * rows, width), bf16, VMEM), ((width, cut), bf16, VMEM), ((cut, width), bf16, VMEM)]
        + [((2 * rows, width), f32, VMEM)] * 2,
        [mlp_low, mlp_oth, g_all, up_bias, (w_up, HBM), (w_down, HBM)],
    )
    def take(keep, send, offsets):
        if block % 16 == 0:
            return keep, send
        total = jnp.concatenate([keep, send], axis=0).reshape(count, block, -1)
        total = arrange(total, offsets, me).reshape(width, -1)
        return total[: width // 2], total[width // 2 :]

    def first_exchange(up_keep, up_send, down_keep, down_send, up_sums):
        up_keep, up_send = take(up_keep, up_send, slots_a)
        down_keep, down_send = take(down_keep, down_send, slots_b)
        return up_keep, exchange(up_send, order_a[0], count), down_keep, exchange(down_send, order_b[0], count)

    def second_exchange(sends):
        return exchange(sends[0], order_a[1], count), exchange(sends[1], order_b[1], count)

    up1, up1_got, down1, down1_got = first_exchange(*first)
    out_send, gmi_send, out_own, gmi_own, *second = mlp(
        "mlp_second",
        cut,
        [((rows, width), bf16)] * 2 + [((rows, width), f32)] * 2,
        [a_all, g_all, out_part, gmi_part, up_later, up_bias, down_later],
    )
    gmi_send, up1_got, down1_got, *second = tie((gmi_send, up1_got, down1_got, *second))
    gmi_got = lax.ppermute(gmi_send, "heads", SWAP)
    out_got = lax.ppermute(out_send, "heads", SWAP)
    up2, up2_got, down2, down2_got = first_exchange(*second)

    grad_resid, gc_own, gc_oth, wo_keep, wo_send, sums_mid = call(
        functools.partial(middle_kernel, n, seq, half, block, slots_b),
        "middle",
        [
            (*high_rows, VMEM),
            ((n, seq, half), bf16, VMEM),
            ((n, seq, half), bf16, VMEM),
            *[((width, half) if block % 16 == 0 else (half, width), bf16, VMEM)] * 2,
            ((8, width), f32, VMEM),
        ],
        [((width, width), f32), ((width, half), f32)],
        [me_s, head_s],
        [gmi_own, gmi_got, resid, g_all, mlp_gain, w_out, ctx],
        8,
    )
    if block % 16:
        wo = jnp.concatenate([wo_keep, wo_send], axis=0).reshape(count, 2, block // 2, 2, half)
        wo = arrange(wo, slots_b, me).swapaxes(2, 3)
        wo_keep = lax.dynamic_index_in_dim(wo, head, 1, keepdims=False).reshape(width, half)
        wo_send = lax.dynamic_index_in_dim(wo, 1 - head, 1, keepdims=False).reshape(width, half)
    wo_got = lax.ppermute(wo_send, "heads", SWAP)

    def back(name, qkv, gc, lse, fused, kinds, more):
        wide = width if fused else half
        return call(
            functools.partial(back_kernel, n, seq, half, block, (slots_a, slots_b), fused),
            name,
            [
                ((rows, 3 * half), bf16, VMEM),
                *[((width // 2, 2 * half), k, VMEM) for k in kinds],
                *[((width // 2, wide), k, VMEM) for k in kinds],
                ((8, half), f32, VMEM),
            ],
            [((rows, 3 * half), f32), ((width, 2 * half), kinds[0]), ((width, half), kinds[0])],
            [text_len, head_s, me_s],
            [qkv, gc, lse, normed, *more],
            10,
        )

    (up1, down1), sends1, _ = combine("add_1", [(up1, up1_got, 0), (down1, down1_got, 0)], [[0], [1]])
    qkv_oth, *sends1 = tie((qkv_oth, *sends1))
    up1_got, down1_got = second_exchange(sends1)
    dq_oth, *dw_oth, sums_oth = back("back_other", qkv_oth, gc_oth, lse_oth, False, (bf16, bf16), [])
    dw_got = [lax.ppermute(d, "heads", SWAP) for d in dw_oth]
    up1_got, down1_got, up2_got, down2_got, *dw_oth = tie((up1_got, down1_got, up2_got, down2_got, *dw_oth))
    (up2, down2, up1, down1), (*sends2, wide1), _ = combine(
        "add_2",
        [(up2, up2_got, 0), (down2, down2_got, 0), (up1, up1_got, 0), (down1, down1_got, 0)],
        [[0], [1], [2, 3]],
    )
    qkv_own, wide1, *sends2 = tie((qkv_own, wide1, *sends2))
    up2_got, down2_got = second_exchange(sends2)
    wide1_got = exchange(wide1, order_a[2], count)
    if block % 16:
        dq_own, *dw_own, sums_own = back("back_own", qkv_own, gc_own, lse_own, False, (f32, f32), [])
        qk_keep, qk_send, v_keep, v_send = [d + o.astype(f32) for d, o in zip(dw_own, dw_got)]
        qk_keep, qk_send = take(qk_keep, qk_send, slots_a)
        v_keep, v_send = take(v_keep, v_send, slots_b)
        wo = wo_keep.astype(f32) + wo_got.astype(f32)
        vo_keep = jnp.concatenate([v_keep, wo[: width // 2]], axis=1)
        vo_send = jnp.concatenate([v_send, wo[width // 2 :]], axis=1).astype(bf16)
        qk_send = qk_send.astype(bf16)
    else:
        dq_own, qk_keep, qk_send, vo_keep, vo_send, sums_own = back(
            "back_own", qkv_own, gc_own, lse_own, True, (f32, bf16), [*dw_got, wo_keep, wo_got]
        )
    at = up1.shape[0]
    up2_got, down2_got, wide1_got, dq_own = tie((up2_got, down2_got, wide1_got, dq_own))
    (up2, down2, up1, down1), (wide2, wide1), _ = combine(
        "add_3",
        [(up2, up2_got, 0), (down2, down2_got, 0), (up1, wide1_got, 0), (down1, wide1_got, at)],
        [[0, 1], [2, 3]],
    )
    qk_send, vo_send, wide1, wide2, dq_own = tie((qk_send, vo_send, wide1, wide2, dq_own))
    qk_got = exchange(qk_send, order_a[0], count)
    vo_got = exchange(vo_send, order_b[0], count)
    wide1_got = exchange(wide1, order_a[3], count)
    wide2_got = exchange(wide2, order_a[2], count)
    grad_tok, layer_out, vecs = call(
        functools.partial(last_kernel, half),
        "last",
        [high_rows, low_rows, ((8, max(2 * width, hidden)), f32, VMEM)],
        [],
        [head_s],
        [
            dq_own, dq_oth, w_qkv, w_oth, tok, attn_gain, grad_resid, sums_mid, sums_own, sums_oth,
            first[-1], second[-1], resid, out_own, out_got, down_bias,
        ],
        16,
    )
    vecs = vecs + lax.ppermute(vecs, "heads", SWAP)
    vecs_got = exchange(vecs, order_a[0], count)
    qk_got, vo_got, wide1_got, wide2_got, vecs_got = tie((qk_got, vo_got, wide1_got, wide2_got, vecs_got))
    part, up_part = width // count // 2, hidden // count
    index = (me * 2 + head).reshape(1)
    shares = [((part,), f32)] * 6 + [((2, part), f32), ((up_part,), f32)]
    if bits == 4 and block % 16 == 0:
        kept = [((4 * block, width), f32, VMEM)] * 2 + [((block, hidden // 2), f32, VMEM)] * 2
        sent = [((4 * block + 32, width), bf16, VMEM), ((4 * block, width), bf16, VMEM)]
        qk, vo, up2, down2, qk_send, vo_send, wide2, vecs = call(
            third_kernel,
            "add_4",
            kept + sent + [((2 * block, hidden // 2), bf16, VMEM), (vecs.shape, f32, VMEM)],
            [],
            [],
            [qk_keep, qk_got, vo_keep, vo_got, up2, down2, wide2_got, vecs, vecs_got],
            4,
        )
        qk_got = exchange(qk_send, order_a[1], count)
        vo_got = exchange(vo_send, order_b[1], count)
        wide2_got = exchange(wide2, order_a[3], count)
        qk_got, vo_got, wide2_got = tie((qk_got, vo_got, wide2_got))
        qk, vo, *sends, vecs = call(
            fan_kernel,
            "add_5",
            [((block, width), f32, VMEM)] * 2
            + [((2 * block + 32, width), bf16, VMEM)] * 3
            + [(vecs.shape, f32, VMEM)],
            [],
            [],
            [qk, qk_got, vo, vo_got, vecs],
            4,
        )
        masks = (order_a[3], order_a[2], order_a[2] ^ order_a[3])
        gots = [exchange(send, mask, count) for send, mask in zip(sends, masks)]
        grad_w_up, grad_w_down = call(
            wide_kernel, "add_wide", [((block, hidden), f32)] * 2, [], [], [up1, down1, wide1_got, up2, down2, wide2_got], 4
        )
        grad_w_up, grad_w_down, *gots = tie((grad_w_up, grad_w_down, *gots))
        grad_w_qkv, grad_w_out, *piece = call(
            functools.partial(finish_kernel, count, width, hidden),
            "finish",
            [((3, block, half), f32), ((block // 2, width), f32)] + shares,
            [],
            [index],
            [qk, vo, vecs, *gots],
            4,
        )
        grad_w_down = grad_w_down.T
    else:
        at = up1.shape[0]
        (qk, vo, up2, down2), (qk_send, vo_send, wide2), (vecs,) = combine(
            "add_4",
            [(qk_keep, qk_got, 0), (vo_keep, vo_got, 0), (up2, wide2_got, 0), (down2, wide2_got, 2 * at)],
            [[0], [1], [2, 3]],
            [(vecs, vecs_got, 0, False)],
        )
        qk_got = exchange(qk_send, order_a[1], count)
        vo_got = exchange(vo_send, order_b[1], count)
        wide2_got = exchange(wide2, order_a[3], count)
        vecs = vecs + exchange(vecs, order_a[1], count)
        for mask in order_a[4:]:
            at = up1.shape[0]
            (up1, down1, up2, down2), (wide1, wide2), _ = combine(
                "add_more",
                [(up1, wide1_got, 0), (down1, wide1_got, at), (up2, wide2_got, 0), (down2, wide2_got, at)],
                [[0, 1], [2, 3]],
            )
            wide1_got, wide2_got = exchange(wide1, mask, count), exchange(wide2, mask, count)
        at = up1.shape[0]
        grads = [k + g[p : p + at] for k, g, p in
                 ((up1, wide1_got, 0), (up2, wide2_got, 0), (down1, wide1_got, at), (down2, wide2_got, at))]
        grad_w_up = jnp.concatenate(grads[:2], axis=1)
        grad_w_down = jnp.concatenate(grads[2:], axis=1).T
        qk, vo = qk + qk_got.astype(f32), vo + vo_got.astype(f32)
        for mask in order_a[2:]:
            at = qk.shape[0] // 2
            got = exchange(jnp.concatenate([qk[at:], vo[at:]]).astype(bf16), mask, count).astype(f32)
            qk, vo = qk[:at] + got[:at], vo[:at] + got[at:]
            before, vecs_got = vecs, exchange(vecs, mask, count)
            vecs = vecs + vecs_got
        grad_w_qkv = jnp.stack([qk[:, :half], qk[:, half:], vo[:, :half]], axis=0)
        grad_w_out = jnp.concatenate([vo[: block // 2, half:], vo[block // 2 :, half:]], axis=1)
        piece = call(
            functools.partial(spread_kernel, count, width, hidden), "spread", shares, [], [index], [before, vecs_got], 4
        )
    return (
        layer_out.reshape(n, seq, width),
        grad_tok.reshape(n, seq, width),
        piece[0],
        piece[1],
        grad_w_qkv,
        piece[6],
        grad_w_out,
        piece[4],
        piece[2],
        piece[3],
        grad_w_up,
        piece[7],
        grad_w_down,
        piece[5],
    )


def solution(mesh):
    in_specs = (
        P(("pairs", "heads"), None, None),
        P(("pairs", "heads"), None, None),
        P("pairs"),
        P(("pairs", "heads"), None),
        P(),
        P(),
        P(None, None, "heads"),
        P(None, "heads"),
        P(),
        P(),
        P(),
        P(),
        P(None, "heads"),
        P("heads"),
        P("heads", None),
        P(),
    )
    out_specs = (
        P(("pairs", "heads"), None, None),
        P(("pairs", "heads"), None, None),
        P(("pairs", "heads")),
        P(("pairs", "heads")),
        P(None, "pairs", "heads"),
        P(None, ("pairs", "heads")),
        P(("pairs", "heads"), None),
        P(("pairs", "heads")),
        P(("pairs", "heads")),
        P(("pairs", "heads")),
        P("pairs", "heads"),
        P(("pairs", "heads")),
        P("heads", "pairs"),
        P(("pairs", "heads")),
    )
    return jax.shard_map(
        per_device, mesh=mesh, in_specs=in_specs, out_specs=out_specs, check_vma=False
    )
```

```python
import functools
import math

import jax
import jax.numpy as jnp
from jax import lax
from jax.experimental import pallas as pl
from jax.experimental.pallas import tpu as pltpu
from jax.sharding import PartitionSpec as P

HEAD_DIM = 64
WORDS = 40
LANES = 128
EPSILON = 1e-06
MASKED = -1000000000.0
SWAP = [(0, 1), (1, 0)]
f32, bf16 = jnp.float32, jnp.bfloat16
MIB = 1024 * 1024


def dot(a, b, ca=1, cb=0):
    return lax.dot_general(a, b, (((ca,), (cb,)), ((), ())), preferred_element_type=f32)


def centre(rows):
    mean_val = jnp.mean(rows, axis=-1, keepdims=True)
    centred = rows - mean_val
    inv_std = lax.rsqrt(jnp.mean(centred * centred, axis=-1, keepdims=True) + EPSILON)
    return centred * inv_std, inv_std


def norm_back(grad_rows, unit_rows, inv_std, gain):
    scaled = grad_rows * gain
    first = jnp.mean(scaled, axis=-1, keepdims=True)
    second = jnp.mean(scaled * unit_rows, axis=-1, keepdims=True)
    return inv_std * (scaled - first - unit_rows * second)


def col_sum(rows):
    return jnp.sum(rows, axis=0, keepdims=True)


def gelu_parts(v):
    u = jnp.abs(v) * 0.7071067811865476
    t = 1.0 / (1.0 + 0.39 * u)
    poly = 0.8866643918219983 - 0.22753713046899435 * t
    poly = -0.6354003145887568 + poly * t
    poly = 0.6495594277724073 + poly * t
    poly = 0.09138840279707615 + poly * t
    poly = 0.23532522096757497 + poly * t
    bell = jnp.exp(v * v * -0.5)
    tail = (0.5 * t) * poly * bell
    cdf = jnp.where(v < 0.0, tail, 1.0 - tail)
    return v * cdf, cdf + v * (bell * 0.3989422804014327)


def as_row(ref):
    return ref[...].astype(f32).reshape(1, ref.shape[0])


def half_mask(value, lane, e):
    keep = (lane < HEAD_DIM) if e == 0 else (lane >= HEAD_DIM)
    return jnp.where(keep, value, jnp.zeros_like(value))


def mask_words(scores, key_ok):
    return jnp.concatenate([jnp.where(key_ok, scores[:WORDS], MASKED), scores[WORDS:]], axis=0)


def attend(n, seq, half, len_ref, head_ref, proj, ctx, lse_ref):
    scale = 1.0 / math.sqrt(HEAD_DIM)
    lane = lax.broadcasted_iota(jnp.int32, (seq, LANES), 1)
    key = lax.broadcasted_iota(jnp.int32, (WORDS, 1), 0)
    first = head_ref[0] * n

    def step(hp, carry):
        off = pl.multiple_of(hp * LANES, LANES)
        for i in range(n):
            rows = pl.ds(i * seq, seq)
            q2 = proj[rows, pl.ds(off, LANES)] * scale
            k2 = proj[rows, pl.ds(half + off, LANES)].astype(bf16)
            vt = proj[rows, pl.ds(2 * half + off, LANES)].astype(bf16).T
            key_ok = key < len_ref[first + i]
            outs = []
            for e in range(2):
                s = mask_words(dot(k2, half_mask(q2, lane, e).astype(bf16), 1, 1), key_ok)
                top = jnp.max(s, axis=0, keepdims=True)
                w = jnp.exp(s - top)
                total = jnp.sum(w, axis=0, keepdims=True)
                lse_ref[i, pl.ds(2 * hp + e, 1), :] = top + jnp.log(total)
                outs.append(dot(vt[e * HEAD_DIM : (e + 1) * HEAD_DIM], w.astype(bf16)) * (1.0 / total))
            ctx[rows, pl.ds(off, LANES)] = jnp.concatenate(outs, axis=0).T
        return carry

    lax.fori_loop(0, half // LANES, step, 0)


def project(normed, w, ready, bias, half, proj):
    for t in range(3):
        if ready is not None:
            ready[t].wait()
        part = dot(normed, w[t])
        if t != 1:
            part = part + bias[t // 2 : t // 2 + 1]
        proj[:, t * half : (t + 1) * half] = part.astype(bf16).astype(f32)


def bring(pairs, sems):
    copies = [pltpu.make_async_copy(a, b, sems.at[i]) for i, (a, b) in enumerate(pairs)]
    for c in copies:
        c.start()
    return copies


def first_kernel(
    n, seq, half, head_ref, len_h, tok_h, gain_h, shift_h, bias_h, w_h, normed, qkv_h, ctx, lse,
    lens, tok, gain, shift, bias, w, qkv, proj, ctx32, sems,
):
    copies = bring(
        [(tok_h, tok), (gain_h, gain), (shift_h, shift), (bias_h, bias)]
        + [(w_h.at[t], w.at[t]) for t in range(3)]
        + [(len_h, lens)],
        sems,
    )
    for c in copies[:4]:
        c.wait()
    unit, _ = centre(tok[...].astype(f32))
    rows = (unit * as_row(gain) + as_row(shift)).astype(bf16)
    normed[...] = rows
    project(rows, w, copies[4:7], bias, half, proj)
    for i in range(n):
        qkv[i] = proj[pl.ds(i * seq, seq)].astype(bf16)
    leave = pltpu.make_async_copy(qkv, qkv_h, sems.at[8])
    leave.start()
    copies[7].wait()
    attend(n, seq, half, lens, head_ref, proj, ctx32, lse)
    ctx[...] = ctx32[...].astype(bf16)
    leave.wait()


def second_kernel(
    n, seq, half, head_ref, normed, ctx_own, bias_h, w_h, len_h, cot_h, cot_oth_h, words_h, words_oth_h, tok_h, w_out_h,
    out_bias_h, gain_h, shift_h, qkv_h, ctx_h, lse, resid_h, mlp_low, g_all,
    lens, bias, w, cot, cot_oth, words, words_oth, tok, w_out, out_bias, gain, shift, ctx, resid, qkv, proj, ctx32,
    masked, sems,
):
    copies = bring(
        [(bias_h, bias)]
        + [(w_h.at[t], w.at[t]) for t in range(3)]
        + [(len_h, lens), (cot_h, cot), (cot_oth_h, cot_oth), (words_h, words), (words_oth_h, words_oth)]
        + [(tok_h, tok), (w_out_h, w_out), (out_bias_h, out_bias), (gain_h, gain), (shift_h, shift)],
        sems,
    )
    copies[0].wait()
    project(normed[...], w, copies[1:4], bias, half, proj)
    for i in range(n):
        qkv[i] = proj[pl.ds(i * seq, seq)].astype(bf16)
    leave = [pltpu.make_async_copy(qkv, qkv_h, sems.at[14])]
    leave[0].start()
    ctx[:, :half] = ctx_own[...]
    for c in copies[4:9]:
        c.wait()
    at = 0
    for rows_g, keep in ((cot, words), (cot_oth, words_oth)):
        keep = keep[...].astype(f32).T
        for i in range(n):
            masked[at : at + WORDS] = rows_g[i, :WORDS].astype(f32) * keep[:, i : i + 1]
            masked[at + WORDS : at + seq] = rows_g[i, WORDS:].astype(f32)
            at += seq
    g_all[...] = masked[...].astype(bf16)
    attend(n, seq, half, lens, head_ref, proj, ctx32, lse)
    ctx[:, half:] = ctx32[...].astype(bf16)
    leave.append(pltpu.make_async_copy(ctx, ctx_h, sems.at[15]))
    leave[1].start()
    for c in copies[9:14]:
        c.wait()
    own = pl.multiple_of(head_ref[0] * half, LANES)
    oth = pl.multiple_of((1 - head_ref[0]) * half, LANES)
    attn = dot(ctx[:, :half], w_out[pl.ds(own, half)]) + dot(ctx[:, half:], w_out[pl.ds(oth, half)])
    total = tok[...].astype(f32) + (attn + as_row(out_bias))
    resid[...] = total
    leave.append(pltpu.make_async_copy(resid, resid_h, sems.at[16]))
    leave[2].start()
    unit, _ = centre(total)
    mlp_low[...] = (unit * as_row(gain) + as_row(shift)).astype(bf16)
    for c in leave:
        c.wait()


def mlp_kernel(start, orders, block, me_ref, head_ref, *refs):
    if start == 0:
        own, oth, g, bias, up_h, down_h, a, up_later, down_later, *refs, up, down, sems = refs
        cut = down.shape[0]
        cuts = [pl.ds(0, cut), pl.ds(cut, cut)]
        copies = bring(
            [(up_h.at[:, cuts[0]], up), (down_h.at[cuts[0]], down)]
            + [(up_h.at[:, cuts[1]], up_later), (down_h.at[cuts[1]], down_later)],
            sems,
        )
        rows = own.shape[0]
        a[:rows], a[rows:] = own[...], oth[...]
    else:
        a, g, out_in, gmi_in, up, bias, down, out_send, gmi_send, *refs = refs
    out_acc, gmi_acc, keep, send, d_bias, scr_up, scr_down = refs
    core = head_ref[0]
    cut = d_bias.shape[0]
    units = pl.ds(start, cut)
    if start == 0:
        copies[0].wait()
        copies[1].wait()
    w_up, w_down = up[...], down[...]
    act, slope = gelu_parts(dot(a[...], w_up) + bias[units].astype(f32).reshape(1, cut))
    act = act.astype(bf16)
    grad = (dot(g[...], w_down, 1, 1) * slope).astype(bf16)
    ordered(dot(a[...], grad, 0, 0), scr_up, (keep, send), 0, orders, block, me_ref, core)
    ordered(dot(g[...], act, 0, 0), scr_down, (keep, send), cut, orders, block, me_ref, core)
    d_bias[...] = col_sum(grad.astype(f32)).reshape(cut)
    out, gmi = dot(act, w_down), dot(grad, w_up, 1, 1)
    if start == 0:
        out_acc[...], gmi_acc[...] = out, gmi
        copies[2].wait()
        copies[3].wait()
        return
    rows = out_acc.shape[0]
    out, gmi = out_in[...] + out, gmi_in[...] + gmi
    out_acc[...], gmi_acc[...] = out[:rows], gmi[:rows]
    out_send[...], gmi_send[...] = out[rows:].astype(bf16), gmi[rows:].astype(bf16)


def slot_row(orders, slot, core, me_ref, block):
    first, second = orders[0][slot], orders[1][slot]
    offset = first if first == second else jnp.where(core == 0, first, second)
    return (me_ref[0] ^ offset) * block


def ordered(value, scr, dests, col, orders, block, me_ref, core):
    each, cols = value.shape[0] // len(dests), pl.ds(col, value.shape[1])
    if block % 16:
        for i, dest in enumerate(dests):
            dest[:, cols] = value[i * each : (i + 1) * each].astype(dest.dtype)
        return
    scr[...] = value.astype(scr.dtype)
    for slot in range(len(orders[0])):
        at = pl.multiple_of(slot_row(orders, slot, core, me_ref, block), 16)
        dest, row = dests[slot * block // each], slot * block % each
        dest[row : row + block, cols] = scr[pl.ds(at, block)].astype(dest.dtype)


def middle_kernel(
    n, seq, half, block, orders, me_ref, head_ref, gmi_own, gmi_got, resid, g_all, gain, w_out, ctx,
    grad_resid, gc_own, gc_oth, keep, send, sums, scr, cuts,
):
    unit, inv_std = centre(resid[...])
    gmi = gmi_own[...] + gmi_got[...].astype(f32)
    g_final = g_all[: gmi_own.shape[0]].astype(f32)
    total = g_final + norm_back(gmi, unit, inv_std, as_row(gain))
    grad_resid[...] = total
    low = total.astype(bf16)
    sums[...] = jnp.zeros_like(sums)
    sums[0:1] = col_sum(gmi * unit)
    sums[1:2] = col_sum(gmi)
    sums[2:3] = col_sum(low.astype(f32))
    sums[3:4] = col_sum(g_final)
    own = pl.multiple_of(head_ref[0] * half, LANES)
    oth = pl.multiple_of((1 - head_ref[0]) * half, LANES)
    for dest, at in ((gc_own, own), (gc_oth, oth)):
        part = dot(low, w_out[pl.ds(at, half)], 1, 1)
        for i in range(n):
            dest[i] = part[i * seq : (i + 1) * seq].astype(bf16)
    scr[pl.ds(own, half)] = dot(ctx[:, :half], low, 0, 0)
    scr[pl.ds(oth, half)] = dot(ctx[:, half:], low, 0, 0)
    if block % 16:
        keep[...] = scr[:half].astype(bf16)
        send[...] = scr[half:].astype(bf16)
        return
    part = block // 2
    for dest, core in ((keep, head_ref[0]), (send, 1 - head_ref[0])):
        for slot in range(len(orders[0])):
            at = pl.multiple_of(slot_row(orders, slot, core, me_ref, block) + core * part, 8)
            cuts[slot * block : slot * block + part] = scr[pl.ds(at, part), :half]
            cuts[slot * block + part : (slot + 1) * block] = scr[pl.ds(at, part), half:]
        dest[...] = cuts[...].astype(bf16)


def back_kernel(n, seq, half, block, orders, other, len_ref, head_ref, me_ref, qkv, gc, lse, normed, *refs):
    if other:
        wo, dqkv, d_qk, d_v, sums, grads, scr_qk, scr_v = refs
        at_v = 0
        if wo.shape[1] == half:
            d_v[:, half:] = wo[...]
    else:
        dqkv, d_qk, sums, grads, scr_qk, scr_v = refs
        d_v, at_v = d_qk, 2 * half
    scale = 1.0 / math.sqrt(HEAD_DIM)
    lane = lax.broadcasted_iota(jnp.int32, (seq, LANES), 1)
    key = lax.broadcasted_iota(jnp.int32, (WORDS, 1), 0)
    first = head_ref[0] * n

    def step(hp, carry):
        off = pl.multiple_of(hp * LANES, LANES)
        for i in range(n):
            q2 = qkv[i, :, pl.ds(off, LANES)]
            k2 = qkv[i, :, pl.ds(half + off, LANES)]
            v2 = qkv[i, :, pl.ds(2 * half + off, LANES)]
            g2 = gc[i, :, pl.ds(off, LANES)]
            kt = k2.T
            key_ok = key < len_ref[first + i]
            dq, dk, dv = [], [], []
            for e in range(2):
                qm = half_mask(q2, lane, e) * jnp.asarray(scale, bf16)
                s = mask_words(dot(k2, qm, 1, 1), key_ok)
                p = jnp.exp(s - lse[i, pl.ds(2 * hp + e, 1), :])
                dp = dot(v2, half_mask(g2, lane, e), 1, 1)
                inner = jnp.sum(p * dp, axis=0, keepdims=True)
                ds = (p * (dp - inner)).astype(bf16)
                dv.append(dot(p.astype(bf16), g2))
                dk.append(dot(ds, q2))
                dq.append(dot(kt[e * HEAD_DIM : (e + 1) * HEAD_DIM], ds))
            rows = pl.ds(i * seq, seq)
            grads[rows, pl.ds(off, LANES)] = jnp.concatenate(dq, axis=0).T * scale
            grads[rows, pl.ds(half + off, LANES)] = jnp.where(lane < HEAD_DIM, dk[0], dk[1]) * scale
            grads[rows, pl.ds(2 * half + off, LANES)] = jnp.where(lane < HEAD_DIM, dv[0], dv[1])
        return carry

    lax.fori_loop(0, half // LANES, step, 0)
    low = grads[...].astype(bf16)
    dqkv[...] = low
    sums[...] = jnp.zeros_like(sums)
    sums[0:1] = col_sum(low[:, :half].astype(f32))
    sums[1:2] = col_sum(low[:, 2 * half :].astype(f32))
    core = 1 - head_ref[0] if other else head_ref[0]
    rows = normed[...]
    ordered(dot(rows, low[:, : 2 * half], 0, 0), scr_qk, (d_qk,), 0, orders, block, me_ref, core)
    ordered(dot(rows, low[:, 2 * half :], 0, 0), scr_v, (d_v,), at_v, orders, block, me_ref, core)


def last_kernel(
    half, head_ref, dq_own, dq_oth, w_own, w_oth, tok, gain, grad_resid, sums_mid, sums_own, sums_oth, up_first, up_second,
    grad_tokens, vecs,
):
    grad = None
    for dq, w in ((dq_own, w_own), (dq_oth, w_oth)):
        for t in range(3):
            part = dot(dq[:, t * half : (t + 1) * half], w[t], 1, 1)
            grad = part if grad is None else grad + part
    unit, inv_std = centre(tok[...].astype(f32))
    width = 2 * half
    grad_tokens[...] = grad_resid[...] + norm_back(grad, unit, inv_std, as_row(gain))
    width = 2 * half
    vecs[...] = jnp.zeros_like(vecs)
    vecs[0:1, :width], vecs[0:1, width:] = col_sum(grad * unit), col_sum(grad)
    vecs[1:2, :width], vecs[1:2, width:] = sums_mid[0:1], sums_mid[1:2]
    vecs[2:3, :width], vecs[2:3, width:] = sums_mid[2:3], sums_mid[3:4]
    first = head_ref[0] == 0
    for i in range(2):
        own, oth = sums_own[i : i + 1], sums_oth[i : i + 1]
        vecs[3:4, i * width : i * width + half] = jnp.where(first, own, oth)
        vecs[3:4, i * width + half : (i + 1) * width] = jnp.where(first, oth, own)
    for place, sums in enumerate((up_first, up_second)):
        up = as_row(sums)
        cut = up.shape[1]
        for i in range(2):
            at = place * cut
            vecs[4 + i : 5 + i, at : at + cut] = jnp.where(head_ref[0] == i, up, jnp.zeros_like(up))


def layer_kernel(resid, out_own, out_got, down_bias, layer_out):
    layer_out[...] = (resid[...] + (out_own[...] + out_got[...].astype(f32) + as_row(down_bias))).astype(bf16)


def spread_vectors(count, width, hidden, index, total, outs):
    lanes = total.shape[1]
    part = width // count // 2
    rolled = pltpu.roll(total, lanes - index * part, 1)
    for i in range(6):
        at = (i % 2) * width
        outs[i][...] = rolled[i // 2 : i // 2 + 1, at : at + part].reshape(part)
    for i in range(2):
        outs[6][i : i + 1] = rolled[3:4, i * width : i * width + part]
    part = hidden // count
    up = jnp.where(index < count, total[4:5], total[5:6])
    up = pltpu.roll(jnp.concatenate([up] * 8, axis=0), lanes - (index % count) * part, 1)
    outs[7][...] = up[0:1, :part].reshape(part)


def spread_kernel(count, width, hidden, index_ref, vec, vec_got, *outs):
    spread_vectors(count, width, hidden, index_ref[0], vec[...] + vec_got[...], outs)


def pack(vec):
    high = vec.astype(bf16).astype(f32)
    return jnp.concatenate([high, vec - high], axis=0).astype(bf16)


def unpack(rows):
    rows = rows.astype(f32)
    return rows[:8] + rows[8:]


def halve(have, got, keep, send):
    half = keep.shape[0]
    keep[...] = have[:half].astype(f32) + got[:half].astype(f32)
    send[:half] = (have[half : 2 * half].astype(f32) + got[half : 2 * half].astype(f32)).astype(bf16)


def halve_kernel(have, got, keep, send):
    halve(have, got, keep, send)


def merge_kernel(have, got, own, oth_qk, oth_v, wo, keep, at_keep, send, at_b):
    quarter, half, cols = keep.shape[0], at_keep.shape[0], own.shape[1]
    halve(have, got, keep, send)
    at = at_b.shape[1]
    at_keep[:, :at] = own[:half, :at] + oth_qk[:half].astype(f32)
    at_keep[:, at:cols] = own[:half, at:] + oth_v[:half, : cols - at].astype(f32)
    at_keep[:, cols:] = wo[:half].astype(f32) + oth_v[:half, cols - at :].astype(f32)
    low = (own[half:, :at] + oth_qk[half:].astype(f32)).astype(bf16)
    send[quarter:, :at], send[quarter:, at:] = low[:quarter], low[quarter:]
    at_b[:, : cols - at] = (own[half:, at:] + oth_v[half:, : cols - at].astype(f32)).astype(bf16)
    at_b[:, cols - at :] = (wo[half:].astype(f32) + oth_v[half:, cols - at :].astype(f32)).astype(bf16)


def fan_kernel(have, got, *refs):
    vec, (keep, *sends) = (refs[0], refs[1:]) if len(refs) == 6 else (None, refs)
    block = keep.shape[0]
    keep[...] = have[:block] + got[:block].astype(f32)
    if vec is not None:
        vec_keep = sends.pop()
        total = vec[...] + unpack(got[4 * block : 4 * block + 16])
        vec_keep[...] = total
    for i, send in enumerate(sends):
        at = pl.ds((i + 1) * block, block)
        send[:block] = (have[at] + got[at].astype(f32)).astype(bf16)
        if vec is not None:
            send[block : block + 16] = pack(total)


def fourth_kernel(at_have, both, at_b, vec, vec_got, have, got, at_keep, at_send, vec_keep, keep, send):
    half, cols = at_keep.shape[0], at_b.shape[1]
    total = vec[...] + vec_got[...]
    vec_keep[...] = total
    low, high = pl.ds(0, cols), pl.ds(cols, cols)
    at_keep[:, low] = at_have[:half, low] + both[half:, low].astype(f32)
    at_send[:half, low] = (at_have[half:, low] + both[half:, high].astype(f32)).astype(bf16)
    at_keep[:, high] = at_have[:half, high] + at_b[:half].astype(f32)
    at_send[:half, high] = (at_have[half:, high] + at_b[half:].astype(f32)).astype(bf16)
    at_send[half : half + 16] = pack(total)
    halve(have, got, keep, send)


def wide_kernel(first, got1, got2, got3, second, got, up, down):
    cut = first.shape[1] // 2
    one = first[...] + (got1[...].astype(f32) + got2[...].astype(f32) + got3[...].astype(f32))
    two = second[...] + got[...].astype(f32)
    up[:, :cut], up[:, cut:] = one[:, :cut], two[:, :cut]
    down[:, :cut], down[:, cut:] = one[:, cut:], two[:, cut:]


def finish_kernel(count, width, hidden, index_ref, have, vec, *refs):
    gots, (w_qkv, w_out, *outs) = refs[:3], refs[3:]
    block, half = have.shape[0], width // 2
    total = have[...] + sum(g[:block].astype(f32) for g in gots)
    for t in range(3):
        w_qkv[t] = total[:, t * half : (t + 1) * half]
    part = block // 2
    w_out[:, :half], w_out[:, half:] = total[:part, 3 * half :], total[part:, 3 * half :]
    vec = vec[...] + sum(unpack(g[block : block + 16]) for g in gots)
    spread_vectors(count, width, hidden, index_ref[0], vec, outs)


SMEM = pl.BlockSpec(memory_space=pltpu.SMEM)
HBM, VMEM = pltpu.HBM, pltpu.VMEM


def params(limit):
    return dict(
        compiler_params=pltpu.CompilerParams(vmem_limit_bytes=limit * MIB),
        cost_estimate=pl.CostEstimate(flops=0, bytes_accessed=MIB, transcendentals=0),
    )


def scratch_of(what):
    if what == 0:
        return pltpu.SemaphoreType.DMA
    if isinstance(what, int):
        return pltpu.SemaphoreType.DMA((what,))
    return (what[2] if len(what) > 2 else VMEM)(*what[:2])


def call(body, name, outs, scratch, scalars, args, limit):
    place = lambda where: pl.BlockSpec(memory_space=pltpu.HBM if where is HBM else pltpu.VMEM)
    outs = [(*o, None)[:3] for o in outs]
    args = [a if isinstance(a, tuple) else (a, None) for a in args]
    arrays = [pltpu.with_memory_space_constraint(a, pltpu.HBM) if w is HBM else a for a, w in args]
    return pl.pallas_call(
        body,
        name=name,
        out_shape=[jax.ShapeDtypeStruct(s, d) if w is None else w(s, d) for s, d, w in outs],
        in_specs=[SMEM] * len(scalars) + [place(w) for _, w in args],
        out_specs=[place(w) for *_, w in outs],
        scratch_shapes=[scratch_of(v) for v in scratch],
        **params(limit),
    )(*scalars, *arrays)


def slots(masks):
    offsets = [0]
    for mask in reversed(masks):
        offsets = offsets + [o ^ mask for o in offsets]
    return offsets


def arrange(blocks, places):
    return jnp.concatenate([lax.dynamic_slice_in_dim(blocks, at, 1, axis=0) for at in places], axis=0)


def per_device(
    tokens, cotangent, text_len, word_mask, attn_gain, attn_shift, w_qkv, qv_bias, w_out, out_bias,
    mlp_gain, mlp_shift, w_up, up_bias, w_down, down_bias,
):
    n, seq, width = tokens.shape
    half = w_qkv.shape[2]
    hidden = w_up.shape[1]
    rows = n * seq
    count = lax.axis_size("pairs")
    block = width // count
    head = lax.axis_index("heads")
    me = lax.axis_index("pairs")
    head_s, me_s = head.reshape(1), me.reshape(1)
    bits = count.bit_length() - 1
    order_a = [1 << b for b in range(bits)]
    order_b = order_a[1::-1] + order_a[2:]
    orders = (slots(order_a), slots(order_b))
    direct = bits == 4 and block % 16 == 0

    def exchange(send, stage, mask=None, swap=False):
        masks = [order[stage] if mask is None else mask for order in (order_a, order_b)]
        masks = masks[::-1] if swap else masks
        pairs = [(p * 2 + h, (p ^ masks[h]) * 2 + h) for p in range(count) for h in range(2)]
        return lax.ppermute(send, ("pairs", "heads"), pairs)

    tie = lax.optimization_barrier
    tok = tokens.reshape(rows, width)

    w_oth = lax.ppermute(w_qkv, "heads", SWAP)
    bias_oth = lax.ppermute(qv_bias, "heads", SWAP)
    words_oth = lax.ppermute(word_mask, "heads", SWAP)
    cot_oth = lax.ppermute(cotangent, "heads", SWAP)

    qkv_shape = ((n, seq, 3 * half), bf16)
    lse_shape = ((n, 8, seq), f32, VMEM)
    low_rows, high_rows = ((rows, width), bf16), ((rows, width), f32)
    vector = ((width,), f32)
    weights = ((3, width, half), bf16)
    bias = ((2, half), f32)
    lens = (text_len.shape, jnp.int32, pltpu.SMEM)
    attn_scratch = [qkv_shape, ((rows, 3 * half), f32), ((rows, half), f32)]
    normed, qkv_own, ctx_own, lse_own = call(
        functools.partial(first_kernel, n, seq, half),
        "attend_own",
        [(*low_rows, VMEM), (*qkv_shape, HBM), ((rows, half), bf16, VMEM), lse_shape],
        [lens, low_rows, vector, vector, bias, weights, *attn_scratch, 9],
        [head_s],
        [(v, HBM) for v in (text_len, tok, attn_gain, attn_shift, qv_bias, w_qkv)],
        40,
    )
    w_oth, bias_oth, words_oth, cot_oth, normed = tie((w_oth, bias_oth, words_oth, cot_oth, normed))
    qkv_oth, ctx, lse_oth, resid, mlp_low, g_all = call(
        functools.partial(second_kernel, n, seq, half),
        "attend_other",
        [
            (*qkv_shape, HBM),
            (*low_rows, HBM),
            lse_shape,
            (*high_rows, HBM),
            (*low_rows, VMEM),
            ((2 * rows, width), bf16, VMEM),
        ],
        [
            lens, bias, weights, *[((n, seq, width), bf16)] * 2, *[(word_mask.shape, jnp.int32)] * 2, low_rows,
            ((width, width), bf16), vector, vector, vector, low_rows, high_rows, *attn_scratch,
            ((2 * rows, width), f32), 17,
        ],
        [head_s],
        [normed, ctx_own]
        + [
            (v, HBM)
            for v in (
                bias_oth, w_oth, text_len, cotangent, cot_oth, word_mask, words_oth, tok, w_out, out_bias, mlp_gain,
                mlp_shift,
            )
        ],
        26,
    )
    mlp_oth = lax.ppermute(mlp_low, "heads", SWAP)

    cut = hidden // 2

    def mlp(name, start, outs, args):
        return call(
            functools.partial(mlp_kernel, start, orders, block),
            name,
            outs + [((width // 2, 2 * cut), bf16, VMEM)] * 2 + [((cut,), f32, VMEM)],
            [((width, cut), bf16)] * 2 + ([((width, cut), bf16), ((cut, width), bf16), 4] if start == 0 else []),
            [me_s, head_s],
            args,
            20,
        )

    a_all, up_later, down_later, out_part, gmi_part, c1, c1_send, up_first = mlp(
        "mlp_first",
        0,
        [((2 * rows, width), bf16, VMEM), ((width, cut), bf16, VMEM), ((cut, width), bf16, VMEM)]
        + [((2 * rows, width), f32, VMEM)] * 2,
        [mlp_low, mlp_oth, g_all, up_bias, (w_up, HBM), (w_down, HBM)],
    )
    c1_got = exchange(c1_send, 0) if direct else None
    out_send, gmi_send, out_own, gmi_own, c2, c2_send, up_second = mlp(
        "mlp_second",
        cut,
        [((rows, width), bf16)] * 2 + [((rows, width), f32)] * 2,
        [a_all, g_all, out_part, gmi_part, up_later, up_bias, down_later],
    )
    if direct:
        c2_got = exchange(c2_send, 0)
        add = lambda name, body, outs, args, scalars=(): call(body, name, outs, [], list(scalars), args, 4)
        unit = lambda size, kind: ((size * block, 2 * width), kind, VMEM)
    gmi_got = lax.ppermute(gmi_send, "heads", SWAP)
    out_got = lax.ppermute(out_send, "heads", SWAP)

    grad_resid, gc_own, gc_oth, wo_keep, wo_send, sums_mid = call(
        functools.partial(middle_kernel, n, seq, half, block, orders[::-1]),
        "middle",
        [
            (*high_rows, VMEM),
            ((n, seq, half), bf16, VMEM),
            ((n, seq, half), bf16, VMEM),
            *[((width, half) if block % 16 == 0 else (half, width), bf16, VMEM)] * 2,
            ((8, width), f32, VMEM),
        ],
        [((width, width), f32), ((width, half), f32)],
        [me_s, head_s],
        [gmi_own, gmi_got, resid, g_all, mlp_gain, w_out, ctx],
        8,
    )
    if direct:
        c1_got, gc_oth = tie((c1_got, gc_oth))
        c1, c1_send = add("add_1", halve_kernel, [unit(4, f32), unit(4, bf16)], [c1, c1_got])
        qkv_oth, c1_send = tie((qkv_oth, c1_send))
        c1_got = exchange(c1_send, 1)

    def back(name, qkv, gc, lse, other, kind, sizes, more):
        return call(
            functools.partial(back_kernel, n, seq, half, block, orders[::-1], other),
            name,
            [((rows, 3 * half), bf16, VMEM), *[((width, v), kind, VMEM) for v in sizes], ((8, half), f32, VMEM)],
            [((rows, 3 * half), f32), ((width, 2 * half), kind), ((width, half), kind)],
            [text_len, head_s, me_s],
            [qkv, gc, lse, normed, *more],
            12,
        )

    dq_oth, *d_oth, sums_oth = back("back_other", qkv_oth, gc_oth, lse_oth, True, bf16, (width, width), [wo_send])
    d_got = [lax.ppermute(d, "heads", SWAP) for d in d_oth]
    dq_own, d_own, sums_own = back("back_own", qkv_own, gc_own, lse_own, False, f32, (3 * half,), [])
    if direct:
        c1_got, c2_got, d_own, dq_own = tie((c1_got, c2_got, d_own, dq_own))
        c1, *c1_sends = add("add_z", fan_kernel, [unit(1, f32)] + [unit(1, bf16)] * 3, [c1, c1_got])
        d_own, *rest = tie((d_own, *d_got, *c1_sends))
        d_got, c1_sends = rest[:2], rest[2:]
        c2, at_sum, both, at_b = add(
            "add_2",
            merge_kernel,
            [unit(4, f32), unit(8, f32), unit(8, bf16), ((8 * block, width), bf16, VMEM)],
            [c2, c2_got, d_own, *d_got, wo_keep],
        )
        along = (order_a[3], order_a[2], order_a[2] ^ order_a[3])
        dq_own, both, at_b, *c1_sends = tie((dq_own, both, at_b, *c1_sends))
        c1_gots = [exchange(send, 2, mask) for send, mask in zip(c1_sends[:2], along)]
        both_got, b_got = exchange(both, 1), exchange(at_b, 0, swap=True)
    grad_tok, vecs = call(
        functools.partial(last_kernel, half),
        "last",
        [high_rows, ((8, 2 * width), f32, VMEM)],
        [],
        [head_s],
        [
            dq_own, dq_oth, w_qkv, w_oth, tok, attn_gain, grad_resid, sums_mid, sums_own, sums_oth, up_first, up_second,
        ],
        16,
    )
    if direct:
        both_got, vecs, c1_send, *c1_gots = tie((both_got, vecs, c1_sends[2], *c1_gots))
        c1_gots.append(exchange(c1_send, 2, along[2]))
        c2, c2_send = add("add_3", halve_kernel, [unit(2, f32), unit(2, bf16)], [c2, both_got])
        c2_got = exchange(c2_send, 2)
        out_own, c2_send, vecs = tie((out_own, c2_send, vecs))
    vecs = vecs + lax.ppermute(vecs, "heads", SWAP)
    vecs_got = exchange(vecs, 0, swap=True)
    (layer_out,) = call(layer_kernel, "layer_out", [low_rows], [], [], [resid, out_own, out_got, down_bias], 8)
    part, up_part = width // count // 2, hidden // count
    index = (me * 2 + head).reshape(1)
    shares = [((part,), f32)] * 6 + [((2, part), f32), ((up_part,), f32)]
    if direct:
        b_got, c2_got, layer_out, vecs_got, *c1_gots = tie((b_got, c2_got, layer_out, vecs_got, *c1_gots))
        vec_shape = (vecs.shape, f32, VMEM)
        tall = lambda size: ((size * block + 16, 2 * width), bf16, VMEM)
        at_sum, at_send, vecs, c2, c2_send = add(
            "add_4",
            fourth_kernel,
            [unit(4, f32), tall(4), vec_shape, unit(1, f32), unit(1, bf16)],
            [at_sum, both_got, b_got, vecs, vecs_got, c2, c2_got],
        )
        at_got, c2_got = tie((exchange(at_send, 1, swap=True), exchange(c2_send, 3)))
        at_sum, *sends, vecs = add(
            "add_5", fan_kernel, [unit(1, f32)] + [tall(1)] * 3 + [vec_shape], [at_sum, at_got, vecs]
        )
        gots = [exchange(send, 2, mask) for send, mask in zip(sends, along)]
        grad_w_up, grad_w_down = add(
            "add_wide", wide_kernel, [((block, hidden), f32)] * 2, [c1, *c1_gots, c2, c2_got]
        )
        grad_w_up, grad_w_down, *gots = tie((grad_w_up, grad_w_down, *gots))
        grad_w_qkv, grad_w_out, *piece = add(
            "finish",
            functools.partial(finish_kernel, count, width, hidden),
            [((3, block, half), f32), ((block // 2, width), f32)] + shares,
            [at_sum, vecs, *gots],
            [index],
        )
        grad_w_down = grad_w_down.T
    else:
        places = [me ^ jnp.where(head == 0, a, b) for a, b in zip(*orders)]
        here = lambda v: arrange(v.reshape(count, block, -1), places)

        def pair_sum(total):
            for stage in range(bits):
                at = total.shape[0] // 2
                total = total[:at].astype(f32) + exchange(total[at:].astype(bf16), stage).astype(f32)
            return total[0]

        c1, c2 = [pair_sum(here(jnp.concatenate(c))) for c in ((c1, c1_send), (c2, c2_send))]
        grad_w_up = jnp.concatenate([c1[:, :cut], c2[:, :cut]], axis=1)
        grad_w_down = jnp.concatenate([c1[:, cut:], c2[:, cut:]], axis=1).T
        grad_qkv = pair_sum(here(d_own + jnp.concatenate(d_got, axis=1)[:, : 3 * half].astype(f32)))
        grad_w_qkv = jnp.stack([grad_qkv[:, t * half : (t + 1) * half] for t in range(3)])
        wo = jnp.concatenate([wo_keep, wo_send], axis=0).reshape(count, 2, block // 2, width)
        mine, theirs = [lax.dynamic_index_in_dim(wo, c, 1, keepdims=False) for c in (head, 1 - head)]
        wo = mine.astype(f32) + lax.ppermute(theirs, "heads", SWAP).astype(f32)
        grad_w_out = pair_sum(arrange(wo, places))
        for stage in range(1, bits):
            vecs = vecs + vecs_got
            vecs_got = exchange(vecs, stage, swap=True)
        piece = call(
            functools.partial(spread_kernel, count, width, hidden), "spread", shares, [], [index], [vecs, vecs_got], 4
        )
    return (
        layer_out.reshape(n, seq, width),
        grad_tok.reshape(n, seq, width),
        piece[0],
        piece[1],
        grad_w_qkv,
        piece[6],
        grad_w_out,
        piece[4],
        piece[2],
        piece[3],
        grad_w_up,
        piece[7],
        grad_w_down,
        piece[5],
    )


def solution(mesh):
    in_specs = (
        P(("pairs", "heads"), None, None),
        P(("pairs", "heads"), None, None),
        P("pairs"),
        P(("pairs", "heads"), None),
        P(),
        P(),
        P(None, None, "heads"),
        P(None, "heads"),
        P(),
        P(),
        P(),
        P(),
        P(None, "heads"),
        P("heads"),
        P("heads", None),
        P(),
    )
    out_specs = (
        P(("pairs", "heads"), None, None),
        P(("pairs", "heads"), None, None),
        P(("pairs", "heads")),
        P(("pairs", "heads")),
        P(None, "pairs", "heads"),
        P(None, ("pairs", "heads")),
        P(("pairs", "heads"), None),
        P(("pairs", "heads")),
        P(("pairs", "heads")),
        P(("pairs", "heads")),
        P("pairs", "heads"),
        P(("pairs", "heads")),
        P("heads", "pairs"),
        P(("pairs", "heads")),
    )
    return jax.shard_map(
        per_device, mesh=mesh, in_specs=in_specs, out_specs=out_specs, check_vma=False
    )
```

```python
import functools
import math

import jax
import jax.numpy as jnp
from jax import lax
from jax.experimental import pallas as pl
from jax.experimental.pallas import tpu as pltpu
from jax.sharding import PartitionSpec as P

HEAD_DIM = 64
WORDS = 40
LANES = 128
EPSILON = 1e-06
MASKED = -1000000000.0
SWAP = [(0, 1), (1, 0)]
f32, bf16 = jnp.float32, jnp.bfloat16
MIB = 1024 * 1024


def dot(a, b, ca=1, cb=0):
    return lax.dot_general(a, b, (((ca,), (cb,)), ((), ())), preferred_element_type=f32)


def centre(rows):
    mean_val = jnp.mean(rows, axis=-1, keepdims=True)
    centred = rows - mean_val
    inv_std = lax.rsqrt(jnp.mean(centred * centred, axis=-1, keepdims=True) + EPSILON)
    return centred * inv_std, inv_std


def norm_back(grad_rows, unit_rows, inv_std, gain):
    scaled = grad_rows * gain
    first = jnp.mean(scaled, axis=-1, keepdims=True)
    second = jnp.mean(scaled * unit_rows, axis=-1, keepdims=True)
    return inv_std * (scaled - first - unit_rows * second)


def col_sum(rows):
    return jnp.sum(rows, axis=0, keepdims=True)


def gelu_parts(v):
    u = jnp.abs(v) * 0.7071067811865476
    t = 1.0 / (1.0 + 0.39 * u)
    poly = 0.8866643918219983 - 0.22753713046899435 * t
    poly = -0.6354003145887568 + poly * t
    poly = 0.6495594277724073 + poly * t
    poly = 0.09138840279707615 + poly * t
    poly = 0.23532522096757497 + poly * t
    bell = jnp.exp(v * v * -0.5)
    tail = (0.5 * t) * poly * bell
    cdf = jnp.where(v < 0.0, tail, 1.0 - tail)
    return v * cdf, cdf + v * (bell * 0.3989422804014327)


def as_row(ref):
    return ref[...].astype(f32).reshape(1, ref.shape[0])


def half_mask(value, lane, e):
    keep = (lane < HEAD_DIM) if e == 0 else (lane >= HEAD_DIM)
    return jnp.where(keep, value, jnp.zeros_like(value))


def mask_words(scores, key_ok):
    return jnp.concatenate([jnp.where(key_ok, scores[:WORDS], MASKED), scores[WORDS:]], axis=0)


def attend(n, seq, half, len_ref, head_ref, proj, ctx, lse_ref):
    scale = 1.0 / math.sqrt(HEAD_DIM)
    lane = lax.broadcasted_iota(jnp.int32, (seq, LANES), 1)
    key = lax.broadcasted_iota(jnp.int32, (WORDS, 1), 0)
    first = head_ref[0] * n

    def step(hp, carry):
        off = pl.multiple_of(hp * LANES, LANES)
        for i in range(n):
            rows = pl.ds(i * seq, seq)
            q2 = proj[rows, pl.ds(off, LANES)] * scale
            k2 = proj[rows, pl.ds(half + off, LANES)].astype(bf16)
            vt = proj[rows, pl.ds(2 * half + off, LANES)].astype(bf16).T
            key_ok = key < len_ref[first + i]
            outs = []
            for e in range(2):
                s = mask_words(dot(k2, half_mask(q2, lane, e).astype(bf16), 1, 1), key_ok)
                top = jnp.max(s, axis=0, keepdims=True)
                w = jnp.exp(s - top)
                total = jnp.sum(w, axis=0, keepdims=True)
                lse_ref[i, pl.ds(2 * hp + e, 1), :] = top + jnp.log(total)
                outs.append(dot(vt[e * HEAD_DIM : (e + 1) * HEAD_DIM], w.astype(bf16)) * (1.0 / total))
            ctx[rows, pl.ds(off, LANES)] = jnp.concatenate(outs, axis=0).T
        return carry

    lax.fori_loop(0, half // LANES, step, 0, unroll=True)


def project(normed, w, ready, bias, half, proj):
    for t in range(3):
        if ready is not None:
            ready[t].wait()
        part = dot(normed, w[t])
        if t != 1:
            part = part + bias[t // 2 : t // 2 + 1]
        proj[:, t * half : (t + 1) * half] = part.astype(bf16).astype(f32)


def bring(pairs, sems):
    copies = [pltpu.make_async_copy(a, b, sems.at[i]) for i, (a, b) in enumerate(pairs)]
    for c in copies:
        c.start()
    return copies


def first_kernel(
    n, seq, half, head_ref, len_h, tok_h, gain_h, shift_h, bias_h, w_h, normed, qkv_h, ctx, lse,
    lens, tok, gain, shift, bias, w, qkv, proj, ctx32, sems,
):
    copies = bring(
        [(tok_h, tok), (gain_h, gain), (shift_h, shift), (bias_h, bias)]
        + [(w_h.at[t], w.at[t]) for t in range(3)]
        + [(len_h, lens)],
        sems,
    )
    for c in copies[:4]:
        c.wait()
    unit, _ = centre(tok[...].astype(f32))
    rows = (unit * as_row(gain) + as_row(shift)).astype(bf16)
    normed[...] = rows
    project(rows, w, copies[4:7], bias, half, proj)
    for i in range(n):
        qkv[i] = proj[pl.ds(i * seq, seq)].astype(bf16)
    leave = pltpu.make_async_copy(qkv, qkv_h, sems.at[8])
    leave.start()
    copies[7].wait()
    attend(n, seq, half, lens, head_ref, proj, ctx32, lse)
    ctx[...] = ctx32[...].astype(bf16)
    leave.wait()


def second_kernel(
    n, seq, half, head_ref, normed, ctx_own, bias_h, w_h, len_h, cot_h, cot_oth_h, words_h, words_oth_h, tok_h, w_out_h,
    out_bias_h, gain_h, shift_h, qkv_h, ctx_h, lse, resid_h, mlp_low, g_all,
    lens, bias, w, cot, cot_oth, words, words_oth, tok, w_out, out_bias, gain, shift, ctx, resid, qkv, proj, ctx32,
    masked, sems,
):
    copies = bring(
        [(bias_h, bias)]
        + [(w_h.at[t], w.at[t]) for t in range(3)]
        + [(len_h, lens), (cot_h, cot), (cot_oth_h, cot_oth), (words_h, words), (words_oth_h, words_oth)]
        + [(tok_h, tok), (w_out_h, w_out), (out_bias_h, out_bias), (gain_h, gain), (shift_h, shift)],
        sems,
    )
    copies[0].wait()
    project(normed[...], w, copies[1:4], bias, half, proj)
    for i in range(n):
        qkv[i] = proj[pl.ds(i * seq, seq)].astype(bf16)
    leave = [pltpu.make_async_copy(qkv, qkv_h, sems.at[14])]
    leave[0].start()
    ctx[:, :half] = ctx_own[...]
    for c in copies[4:9]:
        c.wait()
    at = 0
    for rows_g, keep in ((cot, words), (cot_oth, words_oth)):
        keep = keep[...].astype(f32).T
        for i in range(n):
            masked[at : at + WORDS] = rows_g[i, :WORDS].astype(f32) * keep[:, i : i + 1]
            masked[at + WORDS : at + seq] = rows_g[i, WORDS:].astype(f32)
            at += seq
    g_all[...] = masked[...].astype(bf16)
    attend(n, seq, half, lens, head_ref, proj, ctx32, lse)
    ctx[:, half:] = ctx32[...].astype(bf16)
    leave.append(pltpu.make_async_copy(ctx, ctx_h, sems.at[15]))
    leave[1].start()
    for c in copies[9:14]:
        c.wait()
    own = pl.multiple_of(head_ref[0] * half, LANES)
    oth = pl.multiple_of((1 - head_ref[0]) * half, LANES)
    attn = dot(ctx[:, :half], w_out[pl.ds(own, half)]) + dot(ctx[:, half:], w_out[pl.ds(oth, half)])
    total = tok[...].astype(f32) + (attn + as_row(out_bias))
    resid[...] = total
    leave.append(pltpu.make_async_copy(resid, resid_h, sems.at[16]))
    leave[2].start()
    unit, _ = centre(total)
    mlp_low[...] = (unit * as_row(gain) + as_row(shift)).astype(bf16)
    for c in leave:
        c.wait()


def mlp_kernel(start, orders, block, me_ref, head_ref, *refs):
    if start == 0:
        own, oth, g, bias, up_h, down_h, a, up_later, down_later, *refs, up, down, sems = refs
        cut = down.shape[0]
        cuts = [pl.ds(0, cut), pl.ds(cut, cut)]
        copies = bring(
            [(up_h.at[:, cuts[0]], up), (down_h.at[cuts[0]], down)]
            + [(up_h.at[:, cuts[1]], up_later), (down_h.at[cuts[1]], down_later)],
            sems,
        )
        rows = own.shape[0]
        a[:rows], a[rows:] = own[...], oth[...]
    else:
        a, g, out_in, gmi_in, up, bias, down, out_send, gmi_send, *refs = refs
    out_acc, gmi_acc, keep, send, d_bias, scr_up, scr_down = refs
    core = head_ref[0]
    cut = d_bias.shape[0]
    units = pl.ds(start, cut)
    if start == 0:
        copies[0].wait()
        copies[1].wait()
    w_up, w_down = up[...], down[...]
    act, slope = gelu_parts(dot(a[...], w_up) + bias[units].astype(f32).reshape(1, cut))
    act = act.astype(bf16)
    grad = (dot(g[...], w_down, 1, 1) * slope).astype(bf16)
    ordered(dot(a[...], grad, 0, 0), scr_up, (keep, send), 0, orders, block, me_ref, core)
    ordered(dot(g[...], act, 0, 0), scr_down, (keep, send), cut, orders, block, me_ref, core)
    d_bias[...] = col_sum(grad.astype(f32)).reshape(cut)
    out, gmi = dot(act, w_down), dot(grad, w_up, 1, 1)
    if start == 0:
        out_acc[...], gmi_acc[...] = out, gmi
        copies[2].wait()
        copies[3].wait()
        return
    rows = out_acc.shape[0]
    out, gmi = out_in[...] + out, gmi_in[...] + gmi
    out_acc[...], gmi_acc[...] = out[:rows], gmi[:rows]
    out_send[...], gmi_send[...] = out[rows:].astype(bf16), gmi[rows:].astype(bf16)


def slot_row(orders, slot, core, me_ref, block):
    first, second = orders[0][slot], orders[1][slot]
    offset = first if first == second else jnp.where(core == 0, first, second)
    return (me_ref[0] ^ offset) * block


def ordered(value, scr, dests, col, orders, block, me_ref, core):
    each, cols = value.shape[0] // len(dests), pl.ds(col, value.shape[1])
    if block % 16:
        for i, dest in enumerate(dests):
            dest[:, cols] = value[i * each : (i + 1) * each].astype(dest.dtype)
        return
    scr[...] = value.astype(scr.dtype)
    for slot in range(len(orders[0])):
        at = pl.multiple_of(slot_row(orders, slot, core, me_ref, block), 16)
        dest, row = dests[slot * block // each], slot * block % each
        dest[row : row + block, cols] = scr[pl.ds(at, block)].astype(dest.dtype)


def middle_kernel(
    n, seq, half, block, orders, me_ref, head_ref, gmi_own, gmi_got, resid, g_all, gain, w_out, ctx,
    grad_resid, gc_own, gc_oth, keep, send, sums, scr, cuts,
):
    unit, inv_std = centre(resid[...])
    gmi = gmi_own[...] + gmi_got[...].astype(f32)
    g_final = g_all[: gmi_own.shape[0]].astype(f32)
    total = g_final + norm_back(gmi, unit, inv_std, as_row(gain))
    grad_resid[...] = total
    low = total.astype(bf16)
    sums[...] = jnp.zeros_like(sums)
    sums[0:1] = col_sum(gmi * unit)
    sums[1:2] = col_sum(gmi)
    sums[2:3] = col_sum(low.astype(f32))
    sums[3:4] = col_sum(g_final)
    own = pl.multiple_of(head_ref[0] * half, LANES)
    oth = pl.multiple_of((1 - head_ref[0]) * half, LANES)
    for dest, at in ((gc_own, own), (gc_oth, oth)):
        part = dot(low, w_out[pl.ds(at, half)], 1, 1)
        for i in range(n):
            dest[i] = part[i * seq : (i + 1) * seq].astype(bf16)
    scr[pl.ds(own, half)] = dot(ctx[:, :half], low, 0, 0)
    scr[pl.ds(oth, half)] = dot(ctx[:, half:], low, 0, 0)
    if block % 16:
        keep[...] = scr[:half].astype(bf16)
        send[...] = scr[half:].astype(bf16)
        return
    part = block // 2
    for dest, core in ((keep, head_ref[0]), (send, 1 - head_ref[0])):
        for slot in range(len(orders[0])):
            at = pl.multiple_of(slot_row(orders, slot, core, me_ref, block) + core * part, 8)
            cuts[slot * block : slot * block + part] = scr[pl.ds(at, part), :half]
            cuts[slot * block + part : (slot + 1) * block] = scr[pl.ds(at, part), half:]
        dest[...] = cuts[...].astype(bf16)


def back_kernel(n, seq, half, block, orders, other, len_ref, head_ref, me_ref, qkv, gc, lse, normed, *refs):
    if other:
        wo, dqkv, d_qk, d_v, sums, grads, scr_qk, scr_v = refs
        at_v = 0
        if wo.shape[1] == half:
            d_v[:, half:] = wo[...]
    else:
        dqkv, d_qk, sums, grads, scr_qk, scr_v = refs
        d_v, at_v = d_qk, 2 * half
    scale = 1.0 / math.sqrt(HEAD_DIM)
    lane = lax.broadcasted_iota(jnp.int32, (seq, LANES), 1)
    key = lax.broadcasted_iota(jnp.int32, (WORDS, 1), 0)
    first = head_ref[0] * n

    def step(hp, carry):
        off = pl.multiple_of(hp * LANES, LANES)
        for i in range(n):
            q2 = qkv[i, :, pl.ds(off, LANES)]
            k2 = qkv[i, :, pl.ds(half + off, LANES)]
            v2 = qkv[i, :, pl.ds(2 * half + off, LANES)]
            g2 = gc[i, :, pl.ds(off, LANES)]
            kt = k2.T
            key_ok = key < len_ref[first + i]
            dq, dk, dv = [], [], []
            for e in range(2):
                qm = half_mask(q2, lane, e) * jnp.asarray(scale, bf16)
                s = mask_words(dot(k2, qm, 1, 1), key_ok)
                p = jnp.exp(s - lse[i, pl.ds(2 * hp + e, 1), :])
                dp = dot(v2, half_mask(g2, lane, e), 1, 1)
                inner = jnp.sum(p * dp, axis=0, keepdims=True)
                ds = (p * (dp - inner)).astype(bf16)
                dv.append(dot(p.astype(bf16), g2))
                dk.append(dot(ds, q2))
                dq.append(dot(kt[e * HEAD_DIM : (e + 1) * HEAD_DIM], ds))
            rows = pl.ds(i * seq, seq)
            grads[rows, pl.ds(off, LANES)] = jnp.concatenate(dq, axis=0).T * scale
            grads[rows, pl.ds(half + off, LANES)] = jnp.where(lane < HEAD_DIM, dk[0], dk[1]) * scale
            grads[rows, pl.ds(2 * half + off, LANES)] = jnp.where(lane < HEAD_DIM, dv[0], dv[1])
        return carry

    lax.fori_loop(0, half // LANES, step, 0, unroll=True)
    low = grads[...].astype(bf16)
    dqkv[...] = low
    sums[...] = jnp.zeros_like(sums)
    sums[0:1] = col_sum(low[:, :half].astype(f32))
    sums[1:2] = col_sum(low[:, 2 * half :].astype(f32))
    core = 1 - head_ref[0] if other else head_ref[0]
    rows = normed[...]
    ordered(dot(rows, low[:, : 2 * half], 0, 0), scr_qk, (d_qk,), 0, orders, block, me_ref, core)
    ordered(dot(rows, low[:, 2 * half :], 0, 0), scr_v, (d_v,), at_v, orders, block, me_ref, core)


def last_kernel(
    half, head_ref, dq_own, dq_oth, w_own, w_oth, tok, gain, grad_resid, sums_mid, sums_own, sums_oth, up_first, up_second,
    grad_tokens, vecs,
):
    grad = None
    for dq, w in ((dq_own, w_own), (dq_oth, w_oth)):
        for t in range(3):
            part = dot(dq[:, t * half : (t + 1) * half], w[t], 1, 1)
            grad = part if grad is None else grad + part
    unit, inv_std = centre(tok[...].astype(f32))
    width = 2 * half
    grad_tokens[...] = grad_resid[...] + norm_back(grad, unit, inv_std, as_row(gain))
    width = 2 * half
    vecs[...] = jnp.zeros_like(vecs)
    vecs[0:1, :width], vecs[0:1, width:] = col_sum(grad * unit), col_sum(grad)
    vecs[1:2, :width], vecs[1:2, width:] = sums_mid[0:1], sums_mid[1:2]
    vecs[2:3, :width], vecs[2:3, width:] = sums_mid[2:3], sums_mid[3:4]
    first = head_ref[0] == 0
    for i in range(2):
        own, oth = sums_own[i : i + 1], sums_oth[i : i + 1]
        vecs[3:4, i * width : i * width + half] = jnp.where(first, own, oth)
        vecs[3:4, i * width + half : (i + 1) * width] = jnp.where(first, oth, own)
    for place, sums in enumerate((up_first, up_second)):
        up = as_row(sums)
        cut = up.shape[1]
        for i in range(2):
            at = place * cut
            vecs[4 + i : 5 + i, at : at + cut] = jnp.where(head_ref[0] == i, up, jnp.zeros_like(up))


def layer_kernel(resid, out_own, out_got, down_bias, layer_out):
    layer_out[...] = (resid[...] + (out_own[...] + out_got[...].astype(f32) + as_row(down_bias))).astype(bf16)


def spread_vectors(count, width, hidden, index, total, outs):
    lanes = total.shape[1]
    part = width // count // 2
    rolled = pltpu.roll(total, lanes - index * part, 1)
    for i in range(6):
        at = (i % 2) * width
        outs[i][...] = rolled[i // 2 : i // 2 + 1, at : at + part].reshape(part)
    for i in range(2):
        outs[6][i : i + 1] = rolled[3:4, i * width : i * width + part]
    part = hidden // count
    up = jnp.where(index < count, total[4:5], total[5:6])
    up = pltpu.roll(jnp.concatenate([up] * 8, axis=0), lanes - (index % count) * part, 1)
    outs[7][...] = up[0:1, :part].reshape(part)


def spread_kernel(count, width, hidden, index_ref, vec, vec_got, *outs):
    spread_vectors(count, width, hidden, index_ref[0], vec[...] + vec_got[...], outs)


def pack(vec):
    high = vec.astype(bf16).astype(f32)
    return jnp.concatenate([high, vec - high], axis=0).astype(bf16)


def unpack(rows):
    rows = rows.astype(f32)
    return rows[:8] + rows[8:]


def halve(have, got, keep, send):
    half = keep.shape[0]
    keep[...] = have[:half].astype(f32) + got[:half].astype(f32)
    send[:half] = (have[half : 2 * half].astype(f32) + got[half : 2 * half].astype(f32)).astype(bf16)


def halve_kernel(have, got, keep, send):
    halve(have, got, keep, send)


def merge_kernel(have, got, own, oth_qk, oth_v, wo, keep, send, at_keep, at_a, at_b):
    halve(have, got, keep, send)
    half, cols, at = at_keep.shape[0], own.shape[1], oth_qk.shape[1]
    for i, (left, right) in enumerate(((at_keep.at[:, :at], at_keep.at[:, at:]), (at_a, at_b))):
        rows = pl.ds(i * half, half)
        left[...] = (own[rows, :at] + oth_qk[rows].astype(f32)).astype(left.dtype)
        right[:, : cols - at] = (own[rows, at:] + oth_v[rows, : cols - at].astype(f32)).astype(right.dtype)
        right[:, cols - at :] = (wo[rows].astype(f32) + oth_v[rows, cols - at :].astype(f32)).astype(right.dtype)


def fan_kernel(have, got, *refs):
    vec, (keep, *sends) = (refs[0], refs[1:]) if len(refs) == 6 else (None, refs)
    block = keep.shape[0]
    keep[...] = have[:block] + got[:block].astype(f32)
    if vec is not None:
        vec_keep = sends.pop()
        total = vec[...] + unpack(got[4 * block : 4 * block + 16])
        vec_keep[...] = total
    for i, send in enumerate(sends):
        at = pl.ds((i + 1) * block, block)
        send[:block] = (have[at] + got[at].astype(f32)).astype(bf16)
        if vec is not None:
            send[block : block + 16] = pack(total)


def fourth_kernel(at_have, at_a, at_b, vec, vec_got, have, got, at_keep, at_send, vec_keep, keep, send):
    total = vec[...] + vec_got[...]
    vec_keep[...] = total
    half, cols = at_keep.shape[0], at_a.shape[1]
    for part, here in ((at_a, pl.ds(0, cols)), (at_b, pl.ds(cols, cols))):
        at_keep[:, here] = at_have[:half, here] + part[:half].astype(f32)
        at_send[:half, here] = (at_have[half:, here] + part[half:].astype(f32)).astype(bf16)
    at_send[half : half + 16] = pack(total)
    halve(have, got, keep, send)


def wide_kernel(first, got1, second, got2, up, down):
    cut = first.shape[1] // 2
    one, two = first[...] + got1[...].astype(f32), second[...] + got2[...].astype(f32)
    up[:, :cut], up[:, cut:] = one[:, :cut], two[:, :cut]
    down[:, :cut], down[:, cut:] = one[:, cut:], two[:, cut:]


def finish_kernel(count, width, hidden, index_ref, have, vec, *refs):
    gots, (w_qkv, w_out, *outs) = refs[:3], refs[3:]
    block, half = have.shape[0], width // 2
    total = have[...] + sum(g[:block].astype(f32) for g in gots)
    for t in range(3):
        w_qkv[t] = total[:, t * half : (t + 1) * half]
    part = block // 2
    w_out[:, :half], w_out[:, half:] = total[:part, 3 * half :], total[part:, 3 * half :]
    vec = vec[...] + sum(unpack(g[block : block + 16]) for g in gots)
    spread_vectors(count, width, hidden, index_ref[0], vec, outs)


SMEM = pl.BlockSpec(memory_space=pltpu.SMEM)
HBM, VMEM = pltpu.HBM, pltpu.VMEM


def params(limit):
    return dict(
        compiler_params=pltpu.CompilerParams(vmem_limit_bytes=limit * MIB),
        cost_estimate=pl.CostEstimate(flops=0, bytes_accessed=MIB, transcendentals=0),
    )


def scratch_of(what):
    if what == 0:
        return pltpu.SemaphoreType.DMA
    if isinstance(what, int):
        return pltpu.SemaphoreType.DMA((what,))
    return (what[2] if len(what) > 2 else VMEM)(*what[:2])


def call(body, name, outs, scratch, scalars, args, limit):
    place = lambda where: pl.BlockSpec(memory_space=pltpu.HBM if where is HBM else pltpu.VMEM)
    outs = [(*o, None)[:3] for o in outs]
    args = [a if isinstance(a, tuple) else (a, None) for a in args]
    arrays = [pltpu.with_memory_space_constraint(a, pltpu.HBM) if w is HBM else a for a, w in args]
    return pl.pallas_call(
        body,
        name=name,
        out_shape=[jax.ShapeDtypeStruct(s, d) if w is None else w(s, d) for s, d, w in outs],
        in_specs=[SMEM] * len(scalars) + [place(w) for _, w in args],
        out_specs=[place(w) for *_, w in outs],
        scratch_shapes=[scratch_of(v) for v in scratch],
        **params(limit),
    )(*scalars, *arrays)


def slots(masks):
    offsets = [0]
    for mask in reversed(masks):
        offsets = offsets + [o ^ mask for o in offsets]
    return offsets


def arrange(blocks, places):
    return jnp.concatenate([lax.dynamic_slice_in_dim(blocks, at, 1, axis=0) for at in places], axis=0)


def per_device(
    tokens, cotangent, text_len, word_mask, attn_gain, attn_shift, w_qkv, qv_bias, w_out, out_bias,
    mlp_gain, mlp_shift, w_up, up_bias, w_down, down_bias,
):
    n, seq, width = tokens.shape
    half = w_qkv.shape[2]
    hidden = w_up.shape[1]
    rows = n * seq
    count = lax.axis_size("pairs")
    block = width // count
    head = lax.axis_index("heads")
    me = lax.axis_index("pairs")
    head_s, me_s = head.reshape(1), me.reshape(1)
    bits = count.bit_length() - 1
    order_a = [1 << b for b in range(bits)]
    order_b = order_a[1::-1] + order_a[2:]
    orders = (slots(order_a), slots(order_b))
    direct = bits == 4 and block % 16 == 0

    def exchange(send, stage, mask=None, swap=False):
        masks = [order[stage] if mask is None else mask for order in (order_a, order_b)]
        masks = masks[::-1] if swap else masks
        pairs = [(p * 2 + h, (p ^ masks[h]) * 2 + h) for p in range(count) for h in range(2)]
        return lax.ppermute(send, ("pairs", "heads"), pairs)

    tie = lax.optimization_barrier
    tok = tokens.reshape(rows, width)

    w_oth = lax.ppermute(w_qkv, "heads", SWAP)
    bias_oth = lax.ppermute(qv_bias, "heads", SWAP)
    words_oth = lax.ppermute(word_mask, "heads", SWAP)
    cot_oth = lax.ppermute(cotangent, "heads", SWAP)

    qkv_shape = ((n, seq, 3 * half), bf16)
    lse_shape = ((n, 8, seq), f32, VMEM)
    low_rows, high_rows = ((rows, width), bf16), ((rows, width), f32)
    vector = ((width,), f32)
    weights = ((3, width, half), bf16)
    bias = ((2, half), f32)
    lens = (text_len.shape, jnp.int32, pltpu.SMEM)
    attn_scratch = [qkv_shape, ((rows, 3 * half), f32), ((rows, half), f32)]
    normed, qkv_own, ctx_own, lse_own = call(
        functools.partial(first_kernel, n, seq, half),
        "attend_own",
        [(*low_rows, VMEM), (*qkv_shape, HBM), ((rows, half), bf16, VMEM), lse_shape],
        [lens, low_rows, vector, vector, bias, weights, *attn_scratch, 9],
        [head_s],
        [(v, HBM) for v in (text_len, tok, attn_gain, attn_shift, qv_bias, w_qkv)],
        40,
    )
    w_oth, bias_oth, words_oth, cot_oth, normed = tie((w_oth, bias_oth, words_oth, cot_oth, normed))
    qkv_oth, ctx, lse_oth, resid, mlp_low, g_all = call(
        functools.partial(second_kernel, n, seq, half),
        "attend_other",
        [
            (*qkv_shape, HBM),
            (*low_rows, HBM),
            lse_shape,
            (*high_rows, HBM),
            (*low_rows, VMEM),
            ((2 * rows, width), bf16, VMEM),
        ],
        [
            lens, bias, weights, *[((n, seq, width), bf16)] * 2, *[(word_mask.shape, jnp.int32)] * 2, low_rows,
            ((width, width), bf16), vector, vector, vector, low_rows, high_rows, *attn_scratch,
            ((2 * rows, width), f32), 17,
        ],
        [head_s],
        [normed, ctx_own]
        + [
            (v, HBM)
            for v in (
                bias_oth, w_oth, text_len, cotangent, cot_oth, word_mask, words_oth, tok, w_out, out_bias, mlp_gain,
                mlp_shift,
            )
        ],
        26,
    )
    mlp_oth = lax.ppermute(mlp_low, "heads", SWAP)

    cut = hidden // 2

    def mlp(name, start, outs, args):
        return call(
            functools.partial(mlp_kernel, start, orders, block),
            name,
            outs + [((width // 2, 2 * cut), bf16, VMEM)] * 2 + [((cut,), f32, VMEM)],
            [((width, cut), bf16)] * 2 + ([((width, cut), bf16), ((cut, width), bf16), 4] if start == 0 else []),
            [me_s, head_s],
            args,
            20,
        )

    a_all, up_later, down_later, out_part, gmi_part, c1, c1_send, up_first = mlp(
        "mlp_first",
        0,
        [((2 * rows, width), bf16, VMEM), ((width, cut), bf16, VMEM), ((cut, width), bf16, VMEM)]
        + [((2 * rows, width), f32, VMEM)] * 2,
        [mlp_low, mlp_oth, g_all, up_bias, (w_up, HBM), (w_down, HBM)],
    )
    c1_got = exchange(c1_send, 0) if direct else None
    out_send, gmi_send, out_own, gmi_own, c2, c2_send, up_second = mlp(
        "mlp_second",
        cut,
        [((rows, width), bf16)] * 2 + [((rows, width), f32)] * 2,
        [a_all, g_all, out_part, gmi_part, up_later, up_bias, down_later],
    )
    if direct:
        c2_got = exchange(c2_send, 0)
        add = lambda name, body, outs, args, scalars=(): call(body, name, outs, [], list(scalars), args, 4)
        unit = lambda size, kind: ((size * block, 2 * width), kind, VMEM)
    gmi_got = lax.ppermute(gmi_send, "heads", SWAP)
    out_got = lax.ppermute(out_send, "heads", SWAP)

    grad_resid, gc_own, gc_oth, wo_keep, wo_send, sums_mid = call(
        functools.partial(middle_kernel, n, seq, half, block, orders[::-1]),
        "middle",
        [
            (*high_rows, VMEM),
            ((n, seq, half), bf16, VMEM),
            ((n, seq, half), bf16, VMEM),
            *[((width, half) if block % 16 == 0 else (half, width), bf16, VMEM)] * 2,
            ((8, width), f32, VMEM),
        ],
        [((width, width), f32), ((width, half), f32)],
        [me_s, head_s],
        [gmi_own, gmi_got, resid, g_all, mlp_gain, w_out, ctx],
        8,
    )
    if direct:
        c1_got, gc_oth = tie((c1_got, gc_oth))
        c1, c1_send = add("add_1", halve_kernel, [unit(4, f32), unit(4, bf16)], [c1, c1_got])
        qkv_oth, c1_send = tie((qkv_oth, c1_send))
        c1_got = exchange(c1_send, 1)

    def back(name, qkv, gc, lse, other, kind, sizes, more):
        return call(
            functools.partial(back_kernel, n, seq, half, block, orders[::-1], other),
            name,
            [((rows, 3 * half), bf16, VMEM), *[((width, v), kind, VMEM) for v in sizes], ((8, half), f32, VMEM)],
            [((rows, 3 * half), f32), ((width, 2 * half), kind), ((width, half), kind)],
            [text_len, head_s, me_s],
            [qkv, gc, lse, normed, *more],
            12,
        )

    dq_oth, *d_oth, sums_oth = back("back_other", qkv_oth, gc_oth, lse_oth, True, bf16, (width, width), [wo_send])
    d_got = [lax.ppermute(d, "heads", SWAP) for d in d_oth]
    dq_own, d_own, sums_own = back("back_own", qkv_own, gc_own, lse_own, False, f32, (3 * half,), [])
    if direct:
        c1_got, c2_got, d_own, dq_own = tie((c1_got, c2_got, d_own, dq_own))
        c1, c1_send = add("add_z", halve_kernel, [unit(2, f32), unit(2, bf16)], [c1, c1_got])
        d_own, c1_send, *d_got = tie((d_own, c1_send, *d_got))
        c2, c2_send, at_sum, *at_sends = add(
            "add_2",
            merge_kernel,
            [unit(4, f32), unit(4, bf16), unit(8, f32)] + [((8 * block, width), bf16, VMEM)] * 2,
            [c2, c2_got, d_own, *d_got, wo_keep],
        )
        dq_own, c2_send, c1_send, *at_sends = tie((dq_own, c2_send, c1_send, *at_sends))
        c2_got, at_gots = exchange(c2_send, 1), [exchange(v, 0, swap=True) for v in at_sends]
        c1_got = exchange(c1_send, 2)
    grad_tok, vecs = call(
        functools.partial(last_kernel, half),
        "last",
        [high_rows, ((8, 2 * width), f32, VMEM)],
        [],
        [head_s],
        [
            dq_own, dq_oth, w_qkv, w_oth, tok, attn_gain, grad_resid, sums_mid, sums_own, sums_oth, up_first, up_second,
        ],
        16,
    )
    if direct:
        c2_got, c1_got, vecs = tie((c2_got, c1_got, vecs))
        c2, c2_send = add("add_3", halve_kernel, [unit(2, f32), unit(2, bf16)], [c2, c2_got])
        c1, c1_send = add("add_y", halve_kernel, [unit(1, f32), unit(1, bf16)], [c1, c1_got])
        c2_got, c1_got = exchange(c2_send, 2), exchange(c1_send, 3)
        out_own, c2_send, c1_send, vecs = tie((out_own, c2_send, c1_send, vecs))
    vecs = vecs + lax.ppermute(vecs, "heads", SWAP)
    vecs_got = exchange(vecs, 0, swap=True)
    (layer_out,) = call(layer_kernel, "layer_out", [low_rows], [], [], [resid, out_own, out_got, down_bias], 8)
    part, up_part = width // count // 2, hidden // count
    index = (me * 2 + head).reshape(1)
    shares = [((part,), f32)] * 6 + [((2, part), f32), ((up_part,), f32)]
    if direct:
        c2_got, layer_out, vecs_got, c1_got, *at_gots = tie((c2_got, layer_out, vecs_got, c1_got, *at_gots))
        along = (order_a[3], order_a[2], order_a[2] ^ order_a[3])
        vec_shape = (vecs.shape, f32, VMEM)
        tall = lambda size: ((size * block + 16, 2 * width), bf16, VMEM)
        at_sum, at_send, vecs, c2, c2_send = add(
            "add_4",
            fourth_kernel,
            [unit(4, f32), tall(4), vec_shape, unit(1, f32), unit(1, bf16)],
            [at_sum, *at_gots, vecs, vecs_got, c2, c2_got],
        )
        at_got, c2_got = tie((exchange(at_send, 1, swap=True), exchange(c2_send, 3)))
        at_sum, *sends, vecs = add(
            "add_5", fan_kernel, [unit(1, f32)] + [tall(1)] * 3 + [vec_shape], [at_sum, at_got, vecs]
        )
        gots = [exchange(send, 2, mask) for send, mask in zip(sends, along)]
        grad_w_up, grad_w_down = add(
            "add_wide", wide_kernel, [((block, hidden), f32)] * 2, [c1, c1_got, c2, c2_got]
        )
        grad_w_up, grad_w_down, *gots = tie((grad_w_up, grad_w_down, *gots))
        grad_w_qkv, grad_w_out, *piece = add(
            "finish",
            functools.partial(finish_kernel, count, width, hidden),
            [((3, block, half), f32), ((block // 2, width), f32)] + shares,
            [at_sum, vecs, *gots],
            [index],
        )
        grad_w_down = grad_w_down.T
    else:
        places = [me ^ jnp.where(head == 0, a, b) for a, b in zip(*orders)]
        here = lambda v: arrange(v.reshape(count, block, -1), places)

        def pair_sum(total):
            for stage in range(bits):
                at = total.shape[0] // 2
                total = total[:at].astype(f32) + exchange(total[at:].astype(bf16), stage).astype(f32)
            return total[0]

        c1, c2 = [pair_sum(here(jnp.concatenate(c))) for c in ((c1, c1_send), (c2, c2_send))]
        grad_w_up = jnp.concatenate([c1[:, :cut], c2[:, :cut]], axis=1)
        grad_w_down = jnp.concatenate([c1[:, cut:], c2[:, cut:]], axis=1).T
        grad_qkv = pair_sum(here(d_own + jnp.concatenate(d_got, axis=1)[:, : 3 * half].astype(f32)))
        grad_w_qkv = jnp.stack([grad_qkv[:, t * half : (t + 1) * half] for t in range(3)])
        wo = jnp.concatenate([wo_keep, wo_send], axis=0).reshape(count, 2, block // 2, width)
        mine, theirs = [lax.dynamic_index_in_dim(wo, c, 1, keepdims=False) for c in (head, 1 - head)]
        wo = mine.astype(f32) + lax.ppermute(theirs, "heads", SWAP).astype(f32)
        grad_w_out = pair_sum(arrange(wo, places))
        for stage in range(1, bits):
            vecs = vecs + vecs_got
            vecs_got = exchange(vecs, stage, swap=True)
        piece = call(
            functools.partial(spread_kernel, count, width, hidden), "spread", shares, [], [index], [vecs, vecs_got], 4
        )
    return (
        layer_out.reshape(n, seq, width),
        grad_tok.reshape(n, seq, width),
        piece[0],
        piece[1],
        grad_w_qkv,
        piece[6],
        grad_w_out,
        piece[4],
        piece[2],
        piece[3],
        grad_w_up,
        piece[7],
        grad_w_down,
        piece[5],
    )


def solution(mesh):
    in_specs = (
        P(("pairs", "heads"), None, None),
        P(("pairs", "heads"), None, None),
        P("pairs"),
        P(("pairs", "heads"), None),
        P(),
        P(),
        P(None, None, "heads"),
        P(None, "heads"),
        P(),
        P(),
        P(),
        P(),
        P(None, "heads"),
        P("heads"),
        P("heads", None),
        P(),
    )
    out_specs = (
        P(("pairs", "heads"), None, None),
        P(("pairs", "heads"), None, None),
        P(("pairs", "heads")),
        P(("pairs", "heads")),
        P(None, "pairs", "heads"),
        P(None, ("pairs", "heads")),
        P(("pairs", "heads"), None),
        P(("pairs", "heads")),
        P(("pairs", "heads")),
        P(("pairs", "heads")),
        P("pairs", "heads"),
        P(("pairs", "heads")),
        P("heads", "pairs"),
        P(("pairs", "heads")),
    )
    return jax.shard_map(
        per_device, mesh=mesh, in_specs=in_specs, out_specs=out_specs, check_vma=False
    )
```

```python
import functools
import math

import jax
import jax.numpy as jnp
from jax import lax
from jax.experimental import pallas as pl
from jax.experimental.pallas import tpu as pltpu
from jax.sharding import PartitionSpec as P

HEAD_DIM = 64
WORDS = 40
LANES = 128
EPSILON = 1e-06
MASKED = -1000000000.0
SWAP = [(0, 1), (1, 0)]
f32, bf16 = jnp.float32, jnp.bfloat16
MIB = 1024 * 1024


def dot(a, b, ca=1, cb=0):
    return lax.dot_general(a, b, (((ca,), (cb,)), ((), ())), preferred_element_type=f32)


def centre(rows):
    mean_val = jnp.mean(rows, axis=-1, keepdims=True)
    centred = rows - mean_val
    inv_std = lax.rsqrt(jnp.mean(centred * centred, axis=-1, keepdims=True) + EPSILON)
    return centred * inv_std, inv_std


def norm_back(grad_rows, unit_rows, inv_std, gain):
    scaled = grad_rows * gain
    first = jnp.mean(scaled, axis=-1, keepdims=True)
    second = jnp.mean(scaled * unit_rows, axis=-1, keepdims=True)
    return inv_std * (scaled - first - unit_rows * second)


def col_sum(rows):
    return jnp.sum(rows, axis=0, keepdims=True)


def gelu_parts(v):
    u = jnp.abs(v) * 0.7071067811865476
    t = 1.0 / (1.0 + 0.39 * u)
    poly = 0.8866643918219983 - 0.22753713046899435 * t
    poly = -0.6354003145887568 + poly * t
    poly = 0.6495594277724073 + poly * t
    poly = 0.09138840279707615 + poly * t
    poly = 0.23532522096757497 + poly * t
    bell = jnp.exp(v * v * -0.5)
    tail = (0.5 * t) * poly * bell
    cdf = jnp.where(v < 0.0, tail, 1.0 - tail)
    return v * cdf, cdf + v * (bell * 0.3989422804014327)


def as_row(ref):
    return ref[...].astype(f32).reshape(1, ref.shape[0])


def half_mask(value, lane, e):
    keep = (lane < HEAD_DIM) if e == 0 else (lane >= HEAD_DIM)
    return jnp.where(keep, value, jnp.zeros_like(value))


def mask_words(scores, key_ok):
    return jnp.concatenate([jnp.where(key_ok, scores[:WORDS], MASKED), scores[WORDS:]], axis=0)


def attend(n, seq, half, len_ref, head_ref, proj, ctx, lse_ref):
    scale = 1.0 / math.sqrt(HEAD_DIM)
    lane = lax.broadcasted_iota(jnp.int32, (seq, LANES), 1)
    key = lax.broadcasted_iota(jnp.int32, (WORDS, 1), 0)
    first = head_ref[0] * n

    def step(hp, carry):
        off = pl.multiple_of(hp * LANES, LANES)
        for i in range(n):
            rows = pl.ds(i * seq, seq)
            q2 = proj[rows, pl.ds(off, LANES)] * scale
            k2 = proj[rows, pl.ds(half + off, LANES)].astype(bf16)
            vt = proj[rows, pl.ds(2 * half + off, LANES)].astype(bf16).T
            key_ok = key < len_ref[first + i]
            outs = []
            for e in range(2):
                s = mask_words(dot(k2, half_mask(q2, lane, e).astype(bf16), 1, 1), key_ok)
                top = jnp.max(s, axis=0, keepdims=True)
                w = jnp.exp(s - top)
                total = jnp.sum(w, axis=0, keepdims=True)
                lse_ref[i, pl.ds(2 * hp + e, 1), :] = top + jnp.log(total)
                outs.append(dot(vt[e * HEAD_DIM : (e + 1) * HEAD_DIM], w.astype(bf16)) * (1.0 / total))
            ctx[rows, pl.ds(off, LANES)] = jnp.concatenate(outs, axis=0).T
        return carry

    lax.fori_loop(0, half // LANES, step, 0)


def project(normed, w, ready, bias, half, proj):
    for t in range(3):
        if ready is not None:
            ready[t].wait()
        part = dot(normed, w[t])
        if t != 1:
            part = part + bias[t // 2 : t // 2 + 1]
        proj[:, t * half : (t + 1) * half] = part.astype(bf16).astype(f32)


def bring(pairs, sems):
    copies = [pltpu.make_async_copy(a, b, sems.at[i]) for i, (a, b) in enumerate(pairs)]
    for c in copies:
        c.start()
    return copies


def first_kernel(
    n, seq, half, head_ref, len_h, tok_h, gain_h, shift_h, bias_h, w_h, normed, qkv_h, ctx, lse,
    lens, tok, gain, shift, bias, w, qkv, proj, ctx32, sems,
):
    copies = bring(
        [(tok_h, tok), (gain_h, gain), (shift_h, shift), (bias_h, bias)]
        + [(w_h.at[t], w.at[t]) for t in range(3)]
        + [(len_h, lens)],
        sems,
    )
    for c in copies[:4]:
        c.wait()
    unit, _ = centre(tok[...].astype(f32))
    rows = (unit * as_row(gain) + as_row(shift)).astype(bf16)
    normed[...] = rows
    project(rows, w, copies[4:7], bias, half, proj)
    for i in range(n):
        qkv[i] = proj[pl.ds(i * seq, seq)].astype(bf16)
    leave = pltpu.make_async_copy(qkv, qkv_h, sems.at[8])
    leave.start()
    copies[7].wait()
    attend(n, seq, half, lens, head_ref, proj, ctx32, lse)
    ctx[...] = ctx32[...].astype(bf16)
    leave.wait()


def second_kernel(
    n, seq, half, head_ref, normed, ctx_own, bias_h, w_h, len_h, cot_h, cot_oth_h, words_h, words_oth_h, tok_h, w_out_h,
    out_bias_h, gain_h, shift_h, qkv_h, ctx_h, lse, resid_h, mlp_low, g_all,
    lens, bias, w, cot, cot_oth, words, words_oth, tok, w_out, out_bias, gain, shift, ctx, resid, qkv, proj, ctx32,
    masked, sems,
):
    copies = bring(
        [(bias_h, bias)]
        + [(w_h.at[t], w.at[t]) for t in range(3)]
        + [(len_h, lens), (cot_h, cot), (cot_oth_h, cot_oth), (words_h, words), (words_oth_h, words_oth)]
        + [(tok_h, tok), (w_out_h, w_out), (out_bias_h, out_bias), (gain_h, gain), (shift_h, shift)],
        sems,
    )
    copies[0].wait()
    project(normed[...], w, copies[1:4], bias, half, proj)
    for i in range(n):
        qkv[i] = proj[pl.ds(i * seq, seq)].astype(bf16)
    leave = [pltpu.make_async_copy(qkv, qkv_h, sems.at[14])]
    leave[0].start()
    ctx[:, :half] = ctx_own[...]
    for c in copies[4:9]:
        c.wait()
    at = 0
    for rows_g, keep in ((cot, words), (cot_oth, words_oth)):
        keep = keep[...].astype(f32).T
        for i in range(n):
            masked[at : at + WORDS] = rows_g[i, :WORDS].astype(f32) * keep[:, i : i + 1]
            masked[at + WORDS : at + seq] = rows_g[i, WORDS:].astype(f32)
            at += seq
    g_all[...] = masked[...].astype(bf16)
    attend(n, seq, half, lens, head_ref, proj, ctx32, lse)
    ctx[:, half:] = ctx32[...].astype(bf16)
    leave.append(pltpu.make_async_copy(ctx, ctx_h, sems.at[15]))
    leave[1].start()
    for c in copies[9:14]:
        c.wait()
    own = pl.multiple_of(head_ref[0] * half, LANES)
    oth = pl.multiple_of((1 - head_ref[0]) * half, LANES)
    attn = dot(ctx[:, :half], w_out[pl.ds(own, half)]) + dot(ctx[:, half:], w_out[pl.ds(oth, half)])
    total = tok[...].astype(f32) + (attn + as_row(out_bias))
    resid[...] = total
    leave.append(pltpu.make_async_copy(resid, resid_h, sems.at[16]))
    leave[2].start()
    unit, _ = centre(total)
    mlp_low[...] = (unit * as_row(gain) + as_row(shift)).astype(bf16)
    for c in leave:
        c.wait()


def mlp_kernel(start, orders, block, me_ref, head_ref, *refs):
    if start == 0:
        own, oth, g, bias, up_h, down_h, a, up_later, down_later, *refs, up, down, sems = refs
        cut = down.shape[0]
        cuts = [pl.ds(0, cut), pl.ds(cut, cut)]
        copies = bring(
            [(up_h.at[:, cuts[0]], up), (down_h.at[cuts[0]], down)]
            + [(up_h.at[:, cuts[1]], up_later), (down_h.at[cuts[1]], down_later)],
            sems,
        )
        rows = own.shape[0]
        a[:rows], a[rows:] = own[...], oth[...]
    else:
        a, g, out_in, gmi_in, up, bias, down, out_send, gmi_send, *refs = refs
    out_acc, gmi_acc, keep, send, d_bias, scr_up, scr_down = refs
    core = head_ref[0]
    cut = d_bias.shape[0]
    units = pl.ds(start, cut)
    if start == 0:
        copies[0].wait()
        copies[1].wait()
    w_up, w_down = up[...], down[...]
    act, slope = gelu_parts(dot(a[...], w_up) + bias[units].astype(f32).reshape(1, cut))
    act = act.astype(bf16)
    grad = (dot(g[...], w_down, 1, 1) * slope).astype(bf16)
    ordered(dot(a[...], grad, 0, 0), scr_up, (keep, send), 0, orders, block, me_ref, core)
    ordered(dot(g[...], act, 0, 0), scr_down, (keep, send), cut, orders, block, me_ref, core)
    d_bias[...] = col_sum(grad.astype(f32)).reshape(cut)
    out, gmi = dot(act, w_down), dot(grad, w_up, 1, 1)
    if start == 0:
        out_acc[...], gmi_acc[...] = out, gmi
        copies[2].wait()
        copies[3].wait()
        return
    rows = out_acc.shape[0]
    out, gmi = out_in[...] + out, gmi_in[...] + gmi
    out_acc[...], gmi_acc[...] = out[:rows], gmi[:rows]
    out_send[...], gmi_send[...] = out[rows:].astype(bf16), gmi[rows:].astype(bf16)


def slot_row(orders, slot, core, me_ref, block):
    first, second = orders[0][slot], orders[1][slot]
    offset = first if first == second else jnp.where(core == 0, first, second)
    return (me_ref[0] ^ offset) * block


def ordered(value, scr, dests, col, orders, block, me_ref, core):
    each, cols = value.shape[0] // len(dests), pl.ds(col, value.shape[1])
    if block % 16:
        for i, dest in enumerate(dests):
            dest[:, cols] = value[i * each : (i + 1) * each].astype(dest.dtype)
        return
    scr[...] = value.astype(scr.dtype)
    for slot in range(len(orders[0])):
        at = pl.multiple_of(slot_row(orders, slot, core, me_ref, block), 16)
        dest, row = dests[slot * block // each], slot * block % each
        dest[row : row + block, cols] = scr[pl.ds(at, block)].astype(dest.dtype)


def middle_kernel(
    n, seq, half, block, orders, me_ref, head_ref, gmi_own, gmi_got, resid, g_all, gain, w_out, ctx,
    grad_resid, gc_own, gc_oth, keep, send, sums, scr, cuts,
):
    unit, inv_std = centre(resid[...])
    gmi = gmi_own[...] + gmi_got[...].astype(f32)
    g_final = g_all[: gmi_own.shape[0]].astype(f32)
    total = g_final + norm_back(gmi, unit, inv_std, as_row(gain))
    grad_resid[...] = total
    low = total.astype(bf16)
    sums[...] = jnp.zeros_like(sums)
    sums[0:1] = col_sum(gmi * unit)
    sums[1:2] = col_sum(gmi)
    sums[2:3] = col_sum(low.astype(f32))
    sums[3:4] = col_sum(g_final)
    own = pl.multiple_of(head_ref[0] * half, LANES)
    oth = pl.multiple_of((1 - head_ref[0]) * half, LANES)
    for dest, at in ((gc_own, own), (gc_oth, oth)):
        part = dot(low, w_out[pl.ds(at, half)], 1, 1)
        for i in range(n):
            dest[i] = part[i * seq : (i + 1) * seq].astype(bf16)
    scr[pl.ds(own, half)] = dot(ctx[:, :half], low, 0, 0)
    scr[pl.ds(oth, half)] = dot(ctx[:, half:], low, 0, 0)
    if block % 16:
        keep[...] = scr[:half].astype(bf16)
        send[...] = scr[half:].astype(bf16)
        return
    part = block // 2
    for dest, core in ((keep, head_ref[0]), (send, 1 - head_ref[0])):
        for slot in range(len(orders[0])):
            at = pl.multiple_of(slot_row(orders, slot, core, me_ref, block) + core * part, 8)
            cuts[slot * block : slot * block + part] = scr[pl.ds(at, part), :half]
            cuts[slot * block + part : (slot + 1) * block] = scr[pl.ds(at, part), half:]
        dest[...] = cuts[...].astype(bf16)


def back_kernel(n, seq, half, block, orders, other, len_ref, head_ref, me_ref, qkv, gc, lse, normed, *refs):
    if other:
        wo, dqkv, d_qk, d_v, sums, grads, scr_qk, scr_v = refs
        at_v = 0
        if wo.shape[1] == half:
            d_v[:, half:] = wo[...]
    else:
        dqkv, d_qk, sums, grads, scr_qk, scr_v = refs
        d_v, at_v = d_qk, 2 * half
    scale = 1.0 / math.sqrt(HEAD_DIM)
    lane = lax.broadcasted_iota(jnp.int32, (seq, LANES), 1)
    key = lax.broadcasted_iota(jnp.int32, (WORDS, 1), 0)
    first = head_ref[0] * n

    def step(hp, carry):
        off = pl.multiple_of(hp * LANES, LANES)
        for i in range(n):
            q2 = qkv[i, :, pl.ds(off, LANES)]
            k2 = qkv[i, :, pl.ds(half + off, LANES)]
            v2 = qkv[i, :, pl.ds(2 * half + off, LANES)]
            g2 = gc[i, :, pl.ds(off, LANES)]
            kt = k2.T
            key_ok = key < len_ref[first + i]
            dq, dk, dv = [], [], []
            for e in range(2):
                qm = half_mask(q2, lane, e) * jnp.asarray(scale, bf16)
                s = mask_words(dot(k2, qm, 1, 1), key_ok)
                p = jnp.exp(s - lse[i, pl.ds(2 * hp + e, 1), :])
                dp = dot(v2, half_mask(g2, lane, e), 1, 1)
                inner = jnp.sum(p * dp, axis=0, keepdims=True)
                ds = (p * (dp - inner)).astype(bf16)
                dv.append(dot(p.astype(bf16), g2))
                dk.append(dot(ds, q2))
                dq.append(dot(kt[e * HEAD_DIM : (e + 1) * HEAD_DIM], ds))
            rows = pl.ds(i * seq, seq)
            grads[rows, pl.ds(off, LANES)] = jnp.concatenate(dq, axis=0).T * scale
            grads[rows, pl.ds(half + off, LANES)] = jnp.where(lane < HEAD_DIM, dk[0], dk[1]) * scale
            grads[rows, pl.ds(2 * half + off, LANES)] = jnp.where(lane < HEAD_DIM, dv[0], dv[1])
        return carry

    lax.fori_loop(0, half // LANES, step, 0)
    low = grads[...].astype(bf16)
    dqkv[...] = low
    sums[...] = jnp.zeros_like(sums)
    sums[0:1] = col_sum(low[:, :half].astype(f32))
    sums[1:2] = col_sum(low[:, 2 * half :].astype(f32))
    core = 1 - head_ref[0] if other else head_ref[0]
    rows = normed[...]
    ordered(dot(rows, low[:, : 2 * half], 0, 0), scr_qk, (d_qk,), 0, orders, block, me_ref, core)
    ordered(dot(rows, low[:, 2 * half :], 0, 0), scr_v, (d_v,), at_v, orders, block, me_ref, core)


def last_kernel(
    half, head_ref, dq_own, dq_oth, w_own, w_oth, tok, gain, grad_resid, sums_mid, sums_own, sums_oth, up_first, up_second,
    grad_tokens, vecs,
):
    grad_tokens[...] = jnp.zeros_like(grad_tokens)

    def step(t, carry):
        at = pl.ds(pl.multiple_of(t * half, LANES), half)
        grad_tokens[...] += dot(dq_own[:, at], w_own[t], 1, 1) + dot(dq_oth[:, at], w_oth[t], 1, 1)
        return carry

    lax.fori_loop(0, 3, step, 0)
    grad = grad_tokens[...]
    unit, inv_std = centre(tok[...].astype(f32))
    width = 2 * half
    grad_tokens[...] = grad_resid[...] + norm_back(grad, unit, inv_std, as_row(gain))
    width = 2 * half
    vecs[...] = jnp.zeros_like(vecs)
    vecs[0:1, :width], vecs[0:1, width:] = col_sum(grad * unit), col_sum(grad)
    vecs[1:2, :width], vecs[1:2, width:] = sums_mid[0:1], sums_mid[1:2]
    vecs[2:3, :width], vecs[2:3, width:] = sums_mid[2:3], sums_mid[3:4]
    first = head_ref[0] == 0
    for i in range(2):
        own, oth = sums_own[i : i + 1], sums_oth[i : i + 1]
        vecs[3:4, i * width : i * width + half] = jnp.where(first, own, oth)
        vecs[3:4, i * width + half : (i + 1) * width] = jnp.where(first, oth, own)
    for place, sums in enumerate((up_first, up_second)):
        up = as_row(sums)
        cut = up.shape[1]
        for i in range(2):
            at = place * cut
            vecs[4 + i : 5 + i, at : at + cut] = jnp.where(head_ref[0] == i, up, jnp.zeros_like(up))


def by_rows(count, step, *bases):
    size = next((v for v in (48, 80) if count % v == 0), count)

    def body(i, carry):
        step(*[pl.ds(pl.multiple_of(base + i * size, 16), size) for base in (0, *bases)])
        return carry

    lax.fori_loop(0, count // size, body, 0)


def layer_kernel(resid, out_own, out_got, down_bias, layer_out):
    def step(at):
        total = resid[at] + (out_own[at] + out_got[at].astype(f32) + as_row(down_bias))
        layer_out[at] = total.astype(bf16)

    by_rows(resid.shape[0], step)


def spread_vectors(count, width, hidden, index, total, outs):
    lanes = total.shape[1]
    part = width // count // 2
    rolled = pltpu.roll(total, lanes - index * part, 1)
    for i in range(6):
        at = (i % 2) * width
        outs[i][...] = rolled[i // 2 : i // 2 + 1, at : at + part].reshape(part)
    for i in range(2):
        outs[6][i : i + 1] = rolled[3:4, i * width : i * width + part]
    part = hidden // count
    up = jnp.where(index < count, total[4:5], total[5:6])
    up = pltpu.roll(jnp.concatenate([up] * 8, axis=0), lanes - (index % count) * part, 1)
    outs[7][...] = up[0:1, :part].reshape(part)


def spread_kernel(count, width, hidden, index_ref, vec, vec_got, *outs):
    spread_vectors(count, width, hidden, index_ref[0], vec[...] + vec_got[...], outs)


def pack(vec):
    high = vec.astype(bf16).astype(f32)
    return jnp.concatenate([high, vec - high], axis=0).astype(bf16)


def unpack(rows):
    rows = rows.astype(f32)
    return rows[:8] + rows[8:]


def halve(have, got, keep, send):
    half = keep.shape[0]

    def step(at, low):
        keep[at] = have[at].astype(f32) + got[at].astype(f32)
        send[at] = (have[low].astype(f32) + got[low].astype(f32)).astype(bf16)

    by_rows(half, step, half)


def halve_kernel(have, got, keep, send):
    halve(have, got, keep, send)


def merge_kernel(have, got, own, oth_qk, oth_v, wo, keep, send, at_keep, at_a, at_b):
    halve(have, got, keep, send)
    half, cols, at = at_keep.shape[0], own.shape[1], oth_qk.shape[1]

    def step(here, low):
        at_keep[here, :at] = own[here, :at] + oth_qk[here].astype(f32)
        at_keep[here, at:cols] = own[here, at:] + oth_v[here, : cols - at].astype(f32)
        at_keep[here, cols:] = wo[here].astype(f32) + oth_v[here, cols - at :].astype(f32)
        at_a[here] = (own[low, :at] + oth_qk[low].astype(f32)).astype(bf16)
        at_b[here, : cols - at] = (own[low, at:] + oth_v[low, : cols - at].astype(f32)).astype(bf16)
        at_b[here, cols - at :] = (wo[low].astype(f32) + oth_v[low, cols - at :].astype(f32)).astype(bf16)

    by_rows(half, step, half)


def fan_kernel(have, got, *refs):
    vec, (keep, *sends) = (refs[0], refs[1:]) if len(refs) == 6 else (None, refs)
    block = keep.shape[0]
    keep[...] = have[:block] + got[:block].astype(f32)
    if vec is not None:
        vec_keep = sends.pop()
        total = vec[...] + unpack(got[4 * block : 4 * block + 16])
        vec_keep[...] = total
    for i, send in enumerate(sends):
        at = pl.ds((i + 1) * block, block)
        send[:block] = (have[at] + got[at].astype(f32)).astype(bf16)
        if vec is not None:
            send[block : block + 16] = pack(total)


def fourth_kernel(at_have, at_a, at_b, vec, vec_got, have, got, at_keep, at_send, vec_keep, keep, send):
    total = vec[...] + vec_got[...]
    vec_keep[...] = total
    half, cols = at_keep.shape[0], at_a.shape[1]

    def step(at, low):
        for part, here in ((at_a, pl.ds(0, cols)), (at_b, pl.ds(cols, cols))):
            at_keep[at, here] = at_have[at, here] + part[at].astype(f32)
            at_send[at, here] = (at_have[low, here] + part[low].astype(f32)).astype(bf16)

    by_rows(half, step, half)
    at_send[half : half + 16] = pack(total)
    halve(have, got, keep, send)


def wide_kernel(first, got1, second, got2, up, down):
    cut = first.shape[1] // 2
    one, two = first[...] + got1[...].astype(f32), second[...] + got2[...].astype(f32)
    up[:, :cut], up[:, cut:] = one[:, :cut], two[:, :cut]
    down[:, :cut], down[:, cut:] = one[:, cut:], two[:, cut:]


def finish_kernel(count, width, hidden, index_ref, have, vec, *refs):
    gots, (w_qkv, w_out, *outs) = refs[:3], refs[3:]
    block, half = have.shape[0], width // 2
    total = have[...] + sum(g[:block].astype(f32) for g in gots)
    for t in range(3):
        w_qkv[t] = total[:, t * half : (t + 1) * half]
    part = block // 2
    w_out[:, :half], w_out[:, half:] = total[:part, 3 * half :], total[part:, 3 * half :]
    vec = vec[...] + sum(unpack(g[block : block + 16]) for g in gots)
    spread_vectors(count, width, hidden, index_ref[0], vec, outs)


SMEM = pl.BlockSpec(memory_space=pltpu.SMEM)
HBM, VMEM = pltpu.HBM, pltpu.VMEM


def params(limit):
    return dict(
        compiler_params=pltpu.CompilerParams(vmem_limit_bytes=limit * MIB),
        cost_estimate=pl.CostEstimate(flops=0, bytes_accessed=MIB, transcendentals=0),
    )


def scratch_of(what):
    if what == 0:
        return pltpu.SemaphoreType.DMA
    if isinstance(what, int):
        return pltpu.SemaphoreType.DMA((what,))
    return (what[2] if len(what) > 2 else VMEM)(*what[:2])


def call(body, name, outs, scratch, scalars, args, limit):
    place = lambda where: pl.BlockSpec(memory_space=pltpu.HBM if where is HBM else pltpu.VMEM)
    outs = [(*o, None)[:3] for o in outs]
    args = [a if isinstance(a, tuple) else (a, None) for a in args]
    arrays = [pltpu.with_memory_space_constraint(a, pltpu.HBM) if w is HBM else a for a, w in args]
    return pl.pallas_call(
        body,
        name=name,
        out_shape=[jax.ShapeDtypeStruct(s, d) if w is None else w(s, d) for s, d, w in outs],
        in_specs=[SMEM] * len(scalars) + [place(w) for _, w in args],
        out_specs=[place(w) for *_, w in outs],
        scratch_shapes=[scratch_of(v) for v in scratch],
        **params(limit),
    )(*scalars, *arrays)


def slots(masks):
    offsets = [0]
    for mask in reversed(masks):
        offsets = offsets + [o ^ mask for o in offsets]
    return offsets


def arrange(blocks, places):
    return jnp.concatenate([lax.dynamic_slice_in_dim(blocks, at, 1, axis=0) for at in places], axis=0)


def per_device(
    tokens, cotangent, text_len, word_mask, attn_gain, attn_shift, w_qkv, qv_bias, w_out, out_bias,
    mlp_gain, mlp_shift, w_up, up_bias, w_down, down_bias,
):
    n, seq, width = tokens.shape
    half = w_qkv.shape[2]
    hidden = w_up.shape[1]
    rows = n * seq
    count = lax.axis_size("pairs")
    block = width // count
    head = lax.axis_index("heads")
    me = lax.axis_index("pairs")
    head_s, me_s = head.reshape(1), me.reshape(1)
    bits = count.bit_length() - 1
    order_a = [1 << b for b in range(bits)]
    order_b = order_a[1::-1] + order_a[2:]
    orders = (slots(order_a), slots(order_b))
    direct = bits == 4 and block % 16 == 0

    def exchange(send, stage, mask=None, swap=False):
        masks = [order[stage] if mask is None else mask for order in (order_a, order_b)]
        masks = masks[::-1] if swap else masks
        pairs = [(p * 2 + h, (p ^ masks[h]) * 2 + h) for p in range(count) for h in range(2)]
        return lax.ppermute(send, ("pairs", "heads"), pairs)

    tie = lax.optimization_barrier
    tok = tokens.reshape(rows, width)

    w_oth = lax.ppermute(w_qkv, "heads", SWAP)
    bias_oth = lax.ppermute(qv_bias, "heads", SWAP)
    words_oth = lax.ppermute(word_mask, "heads", SWAP)
    cot_oth = lax.ppermute(cotangent, "heads", SWAP)

    qkv_shape = ((n, seq, 3 * half), bf16)
    lse_shape = ((n, 8, seq), f32, VMEM)
    low_rows, high_rows = ((rows, width), bf16), ((rows, width), f32)
    vector = ((width,), f32)
    weights = ((3, width, half), bf16)
    bias = ((2, half), f32)
    lens = (text_len.shape, jnp.int32, pltpu.SMEM)
    attn_scratch = [qkv_shape, ((rows, 3 * half), f32), ((rows, half), f32)]
    normed, qkv_own, ctx_own, lse_own = call(
        functools.partial(first_kernel, n, seq, half),
        "attend_own",
        [(*low_rows, VMEM), (*qkv_shape, HBM), ((rows, half), bf16, VMEM), lse_shape],
        [lens, low_rows, vector, vector, bias, weights, *attn_scratch, 9],
        [head_s],
        [(v, HBM) for v in (text_len, tok, attn_gain, attn_shift, qv_bias, w_qkv)],
        40,
    )
    w_oth, bias_oth, words_oth, cot_oth, normed = tie((w_oth, bias_oth, words_oth, cot_oth, normed))
    qkv_oth, ctx, lse_oth, resid, mlp_low, g_all = call(
        functools.partial(second_kernel, n, seq, half),
        "attend_other",
        [
            (*qkv_shape, HBM),
            (*low_rows, HBM),
            lse_shape,
            (*high_rows, HBM),
            (*low_rows, VMEM),
            ((2 * rows, width), bf16, VMEM),
        ],
        [
            lens, bias, weights, *[((n, seq, width), bf16)] * 2, *[(word_mask.shape, jnp.int32)] * 2, low_rows,
            ((width, width), bf16), vector, vector, vector, low_rows, high_rows, *attn_scratch,
            ((2 * rows, width), f32), 17,
        ],
        [head_s],
        [normed, ctx_own]
        + [
            (v, HBM)
            for v in (
                bias_oth, w_oth, text_len, cotangent, cot_oth, word_mask, words_oth, tok, w_out, out_bias, mlp_gain,
                mlp_shift,
            )
        ],
        26,
    )
    mlp_oth = lax.ppermute(mlp_low, "heads", SWAP)

    cut = hidden // 2

    def mlp(name, start, outs, args):
        return call(
            functools.partial(mlp_kernel, start, orders, block),
            name,
            outs + [((width // 2, 2 * cut), bf16, VMEM)] * 2 + [((cut,), f32, VMEM)],
            [((width, cut), bf16)] * 2 + ([((width, cut), bf16), ((cut, width), bf16), 4] if start == 0 else []),
            [me_s, head_s],
            args,
            20,
        )

    a_all, up_later, down_later, out_part, gmi_part, c1, c1_send, up_first = mlp(
        "mlp_first",
        0,
        [((2 * rows, width), bf16, VMEM), ((width, cut), bf16, VMEM), ((cut, width), bf16, VMEM)]
        + [((2 * rows, width), f32, VMEM)] * 2,
        [mlp_low, mlp_oth, g_all, up_bias, (w_up, HBM), (w_down, HBM)],
    )
    c1_got = exchange(c1_send, 0) if direct else None
    out_send, gmi_send, out_own, gmi_own, c2, c2_send, up_second = mlp(
        "mlp_second",
        cut,
        [((rows, width), bf16)] * 2 + [((rows, width), f32)] * 2,
        [a_all, g_all, out_part, gmi_part, up_later, up_bias, down_later],
    )
    if direct:
        c2_got = exchange(c2_send, 0)
        add = lambda name, body, outs, args, scalars=(): call(body, name, outs, [], list(scalars), args, 4)
        unit = lambda size, kind: ((size * block, 2 * width), kind, VMEM)
    gmi_got = lax.ppermute(gmi_send, "heads", SWAP)
    out_got = lax.ppermute(out_send, "heads", SWAP)

    grad_resid, gc_own, gc_oth, wo_keep, wo_send, sums_mid = call(
        functools.partial(middle_kernel, n, seq, half, block, orders[::-1]),
        "middle",
        [
            (*high_rows, VMEM),
            ((n, seq, half), bf16, VMEM),
            ((n, seq, half), bf16, VMEM),
            *[((width, half) if block % 16 == 0 else (half, width), bf16, VMEM)] * 2,
            ((8, width), f32, VMEM),
        ],
        [((width, width), f32), ((width, half), f32)],
        [me_s, head_s],
        [gmi_own, gmi_got, resid, g_all, mlp_gain, w_out, ctx],
        8,
    )
    if direct:
        c1_got, gc_oth = tie((c1_got, gc_oth))
        c1, c1_send = add("add_1", halve_kernel, [unit(4, f32), unit(4, bf16)], [c1, c1_got])
        qkv_oth, c1_send = tie((qkv_oth, c1_send))
        c1_got = exchange(c1_send, 1)

    def back(name, qkv, gc, lse, other, kind, sizes, more):
        return call(
            functools.partial(back_kernel, n, seq, half, block, orders[::-1], other),
            name,
            [((rows, 3 * half), bf16, VMEM), *[((width, v), kind, VMEM) for v in sizes], ((8, half), f32, VMEM)],
            [((rows, 3 * half), f32), ((width, 2 * half), kind), ((width, half), kind)],
            [text_len, head_s, me_s],
            [qkv, gc, lse, normed, *more],
            12,
        )

    dq_oth, *d_oth, sums_oth = back("back_other", qkv_oth, gc_oth, lse_oth, True, bf16, (width, width), [wo_send])
    d_got = [lax.ppermute(d, "heads", SWAP) for d in d_oth]
    dq_own, d_own, sums_own = back("back_own", qkv_own, gc_own, lse_own, False, f32, (3 * half,), [])
    if direct:
        c1_got, c2_got, d_own, dq_own = tie((c1_got, c2_got, d_own, dq_own))
        c1, c1_send = add("add_z", halve_kernel, [unit(2, f32), unit(2, bf16)], [c1, c1_got])
        d_own, c1_send, *d_got = tie((d_own, c1_send, *d_got))
        c2, c2_send, at_sum, *at_sends = add(
            "add_2",
            merge_kernel,
            [unit(4, f32), unit(4, bf16), unit(8, f32)] + [((8 * block, width), bf16, VMEM)] * 2,
            [c2, c2_got, d_own, *d_got, wo_keep],
        )
        dq_own, c2_send, c1_send, *at_sends = tie((dq_own, c2_send, c1_send, *at_sends))
        c2_got, at_gots = exchange(c2_send, 1), [exchange(v, 0, swap=True) for v in at_sends]
        c1_got = exchange(c1_send, 2)
    grad_tok, vecs = call(
        functools.partial(last_kernel, half),
        "last",
        [high_rows, ((8, 2 * width), f32, VMEM)],
        [],
        [head_s],
        [
            dq_own, dq_oth, w_qkv, w_oth, tok, attn_gain, grad_resid, sums_mid, sums_own, sums_oth, up_first, up_second,
        ],
        16,
    )
    if direct:
        c2_got, c1_got, vecs = tie((c2_got, c1_got, vecs))
        c2, c2_send = add("add_3", halve_kernel, [unit(2, f32), unit(2, bf16)], [c2, c2_got])
        c1, c1_send = add("add_y", halve_kernel, [unit(1, f32), unit(1, bf16)], [c1, c1_got])
        c2_got, c1_got = exchange(c2_send, 2), exchange(c1_send, 3)
        out_own, c2_send, c1_send, vecs = tie((out_own, c2_send, c1_send, vecs))
    vecs = vecs + lax.ppermute(vecs, "heads", SWAP)
    vecs_got = exchange(vecs, 0, swap=True)
    (layer_out,) = call(layer_kernel, "layer_out", [low_rows], [], [], [resid, out_own, out_got, down_bias], 8)
    part, up_part = width // count // 2, hidden // count
    index = (me * 2 + head).reshape(1)
    shares = [((part,), f32)] * 6 + [((2, part), f32), ((up_part,), f32)]
    if direct:
        c2_got, layer_out, vecs_got, c1_got, *at_gots = tie((c2_got, layer_out, vecs_got, c1_got, *at_gots))
        along = (order_a[3], order_a[2], order_a[2] ^ order_a[3])
        vec_shape = (vecs.shape, f32, VMEM)
        tall = lambda size: ((size * block + 16, 2 * width), bf16, VMEM)
        at_sum, at_send, vecs, c2, c2_send = add(
            "add_4",
            fourth_kernel,
            [unit(4, f32), tall(4), vec_shape, unit(1, f32), unit(1, bf16)],
            [at_sum, *at_gots, vecs, vecs_got, c2, c2_got],
        )
        at_got, c2_got = tie((exchange(at_send, 1, swap=True), exchange(c2_send, 3)))
        at_sum, *sends, vecs = add(
            "add_5", fan_kernel, [unit(1, f32)] + [tall(1)] * 3 + [vec_shape], [at_sum, at_got, vecs]
        )
        gots = [exchange(send, 2, mask) for send, mask in zip(sends, along)]
        grad_w_up, grad_w_down = add(
            "add_wide", wide_kernel, [((block, hidden), f32)] * 2, [c1, c1_got, c2, c2_got]
        )
        grad_w_up, grad_w_down, *gots = tie((grad_w_up, grad_w_down, *gots))
        grad_w_qkv, grad_w_out, *piece = add(
            "finish",
            functools.partial(finish_kernel, count, width, hidden),
            [((3, block, half), f32), ((block // 2, width), f32)] + shares,
            [at_sum, vecs, *gots],
            [index],
        )
        grad_w_down = grad_w_down.T
    else:
        places = [me ^ jnp.where(head == 0, a, b) for a, b in zip(*orders)]
        here = lambda v: arrange(v.reshape(count, block, -1), places)

        def pair_sum(total):
            for stage in range(bits):
                at = total.shape[0] // 2
                total = total[:at].astype(f32) + exchange(total[at:].astype(bf16), stage).astype(f32)
            return total[0]

        c1, c2 = [pair_sum(here(jnp.concatenate(c))) for c in ((c1, c1_send), (c2, c2_send))]
        grad_w_up = jnp.concatenate([c1[:, :cut], c2[:, :cut]], axis=1)
        grad_w_down = jnp.concatenate([c1[:, cut:], c2[:, cut:]], axis=1).T
        grad_qkv = pair_sum(here(d_own + jnp.concatenate(d_got, axis=1)[:, : 3 * half].astype(f32)))
        grad_w_qkv = jnp.stack([grad_qkv[:, t * half : (t + 1) * half] for t in range(3)])
        wo = jnp.concatenate([wo_keep, wo_send], axis=0).reshape(count, 2, block // 2, width)
        mine, theirs = [lax.dynamic_index_in_dim(wo, c, 1, keepdims=False) for c in (head, 1 - head)]
        wo = mine.astype(f32) + lax.ppermute(theirs, "heads", SWAP).astype(f32)
        grad_w_out = pair_sum(arrange(wo, places))
        for stage in range(1, bits):
            vecs = vecs + vecs_got
            vecs_got = exchange(vecs, stage, swap=True)
        piece = call(
            functools.partial(spread_kernel, count, width, hidden), "spread", shares, [], [index], [vecs, vecs_got], 4
        )
    return (
        layer_out.reshape(n, seq, width),
        grad_tok.reshape(n, seq, width),
        piece[0],
        piece[1],
        grad_w_qkv,
        piece[6],
        grad_w_out,
        piece[4],
        piece[2],
        piece[3],
        grad_w_up,
        piece[7],
        grad_w_down,
        piece[5],
    )


def solution(mesh):
    in_specs = (
        P(("pairs", "heads"), None, None),
        P(("pairs", "heads"), None, None),
        P("pairs"),
        P(("pairs", "heads"), None),
        P(),
        P(),
        P(None, None, "heads"),
        P(None, "heads"),
        P(),
        P(),
        P(),
        P(),
        P(None, "heads"),
        P("heads"),
        P("heads", None),
        P(),
    )
    out_specs = (
        P(("pairs", "heads"), None, None),
        P(("pairs", "heads"), None, None),
        P(("pairs", "heads")),
        P(("pairs", "heads")),
        P(None, "pairs", "heads"),
        P(None, ("pairs", "heads")),
        P(("pairs", "heads"), None),
        P(("pairs", "heads")),
        P(("pairs", "heads")),
        P(("pairs", "heads")),
        P("pairs", "heads"),
        P(("pairs", "heads")),
        P("heads", "pairs"),
        P(("pairs", "heads")),
    )
    return jax.shard_map(
        per_device, mesh=mesh, in_specs=in_specs, out_specs=out_specs, check_vma=False
    )
```

```python
import functools
import math

import jax
import jax.numpy as jnp
from jax import lax
from jax.experimental import pallas as pl
from jax.experimental.pallas import tpu as pltpu
from jax.sharding import PartitionSpec as P

HEAD_DIM = 64
WORDS = 40
LANES = 128
EPSILON = 1e-06
MASKED = -1000000000.0
SWAP = [(0, 1), (1, 0)]
f32, bf16 = jnp.float32, jnp.bfloat16
MIB = 1024 * 1024


def dot(a, b, ca=1, cb=0):
    return lax.dot_general(a, b, (((ca,), (cb,)), ((), ())), preferred_element_type=f32)


def centre(rows):
    mean_val = jnp.mean(rows, axis=-1, keepdims=True)
    centred = rows - mean_val
    inv_std = lax.rsqrt(jnp.mean(centred * centred, axis=-1, keepdims=True) + EPSILON)
    return centred * inv_std, inv_std


def norm_back(grad_rows, unit_rows, inv_std, gain):
    scaled = grad_rows * gain
    first = jnp.mean(scaled, axis=-1, keepdims=True)
    second = jnp.mean(scaled * unit_rows, axis=-1, keepdims=True)
    return inv_std * (scaled - first - unit_rows * second)


def col_sum(rows):
    return jnp.sum(rows, axis=0, keepdims=True)


def gelu_parts(v):
    u = jnp.abs(v) * 0.7071067811865476
    t = 1.0 / (1.0 + 0.39 * u)
    poly = 0.8866643918219983 - 0.22753713046899435 * t
    poly = -0.6354003145887568 + poly * t
    poly = 0.6495594277724073 + poly * t
    poly = 0.09138840279707615 + poly * t
    poly = 0.23532522096757497 + poly * t
    bell = jnp.exp(v * v * -0.5)
    tail = (0.5 * t) * poly * bell
    cdf = jnp.where(v < 0.0, tail, 1.0 - tail)
    return v * cdf, cdf + v * (bell * 0.3989422804014327)


def as_row(ref):
    return ref[...].astype(f32).reshape(1, ref.shape[0])


def half_mask(value, lane, e):
    keep = (lane < HEAD_DIM) if e == 0 else (lane >= HEAD_DIM)
    return jnp.where(keep, value, jnp.zeros_like(value))


def mask_words(scores, key_ok):
    return jnp.concatenate([jnp.where(key_ok, scores[:WORDS], MASKED), scores[WORDS:]], axis=0)


def attend(n, seq, half, len_ref, head_ref, proj, ctx, lse_ref):
    scale = 1.0 / math.sqrt(HEAD_DIM)
    lane = lax.broadcasted_iota(jnp.int32, (seq, LANES), 1)
    key = lax.broadcasted_iota(jnp.int32, (WORDS, 1), 0)
    first = head_ref[0] * n

    def step(hp, carry):
        off = pl.multiple_of(hp * LANES, LANES)
        for i in range(n):
            rows = pl.ds(i * seq, seq)
            q2 = proj[rows, pl.ds(off, LANES)] * scale
            k2 = proj[rows, pl.ds(half + off, LANES)].astype(bf16)
            vt = proj[rows, pl.ds(2 * half + off, LANES)].astype(bf16).T
            key_ok = key < len_ref[first + i]
            outs = []
            for e in range(2):
                s = mask_words(dot(k2, half_mask(q2, lane, e).astype(bf16), 1, 1), key_ok)
                top = jnp.max(s, axis=0, keepdims=True)
                w = jnp.exp(s - top)
                total = jnp.sum(w, axis=0, keepdims=True)
                lse_ref[i, pl.ds(2 * hp + e, 1), :] = top + jnp.log(total)
                outs.append(dot(vt[e * HEAD_DIM : (e + 1) * HEAD_DIM], w.astype(bf16)) * (1.0 / total))
            ctx[rows, pl.ds(off, LANES)] = jnp.concatenate(outs, axis=0).T
        return carry

    lax.fori_loop(0, half // LANES, step, 0)


def project(normed, w, ready, bias, half, proj):
    for t in range(3):
        if ready is not None:
            ready[t].wait()
        part = dot(normed, w[t])
        if t != 1:
            part = part + bias[t // 2 : t // 2 + 1]
        proj[:, t * half : (t + 1) * half] = part.astype(bf16).astype(f32)


def bring(pairs, sems):
    copies = [pltpu.make_async_copy(a, b, sems.at[i]) for i, (a, b) in enumerate(pairs)]
    for c in copies:
        c.start()
    return copies


def first_kernel(
    n, seq, half, head_ref, len_h, tok_h, gain_h, shift_h, bias_h, w_h, normed, qkv_h, ctx, lse,
    lens, tok, gain, shift, bias, w, qkv, proj, ctx32, sems,
):
    copies = bring(
        [(tok_h, tok), (gain_h, gain), (shift_h, shift), (bias_h, bias)]
        + [(w_h.at[t], w.at[t]) for t in range(3)]
        + [(len_h, lens)],
        sems,
    )
    for c in copies[:4]:
        c.wait()
    unit, _ = centre(tok[...].astype(f32))
    rows = (unit * as_row(gain) + as_row(shift)).astype(bf16)
    normed[...] = rows
    project(rows, w, copies[4:7], bias, half, proj)
    for i in range(n):
        qkv[i] = proj[pl.ds(i * seq, seq)].astype(bf16)
    leave = pltpu.make_async_copy(qkv, qkv_h, sems.at[8])
    leave.start()
    copies[7].wait()
    attend(n, seq, half, lens, head_ref, proj, ctx32, lse)
    ctx[...] = ctx32[...].astype(bf16)
    leave.wait()


def second_kernel(
    n, seq, half, head_ref, normed, ctx_own, bias_h, w_h, len_h, cot_h, cot_oth_h, words_h, words_oth_h, tok_h, w_out_h,
    out_bias_h, gain_h, shift_h, qkv_h, ctx_h, lse, resid_h, mlp_low, g_all,
    lens, bias, w, cot, cot_oth, words, words_oth, tok, w_out, out_bias, gain, shift, ctx, resid, qkv, proj, ctx32,
    masked, sems,
):
    copies = bring(
        [(bias_h, bias)]
        + [(w_h.at[t], w.at[t]) for t in range(3)]
        + [(len_h, lens), (cot_h, cot), (cot_oth_h, cot_oth), (words_h, words), (words_oth_h, words_oth)]
        + [(tok_h, tok), (w_out_h, w_out), (out_bias_h, out_bias), (gain_h, gain), (shift_h, shift)],
        sems,
    )
    copies[0].wait()
    project(normed[...], w, copies[1:4], bias, half, proj)
    for i in range(n):
        qkv[i] = proj[pl.ds(i * seq, seq)].astype(bf16)
    leave = [pltpu.make_async_copy(qkv, qkv_h, sems.at[14])]
    leave[0].start()
    ctx[:, :half] = ctx_own[...]
    for c in copies[4:9]:
        c.wait()
    at = 0
    for rows_g, keep in ((cot, words), (cot_oth, words_oth)):
        keep = keep[...].astype(f32).T
        for i in range(n):
            masked[at : at + WORDS] = rows_g[i, :WORDS].astype(f32) * keep[:, i : i + 1]
            masked[at + WORDS : at + seq] = rows_g[i, WORDS:].astype(f32)
            at += seq
    g_all[...] = masked[...].astype(bf16)
    attend(n, seq, half, lens, head_ref, proj, ctx32, lse)
    ctx[:, half:] = ctx32[...].astype(bf16)
    leave.append(pltpu.make_async_copy(ctx, ctx_h, sems.at[15]))
    leave[1].start()
    for c in copies[9:14]:
        c.wait()
    own = pl.multiple_of(head_ref[0] * half, LANES)
    oth = pl.multiple_of((1 - head_ref[0]) * half, LANES)
    attn = dot(ctx[:, :half], w_out[pl.ds(own, half)]) + dot(ctx[:, half:], w_out[pl.ds(oth, half)])
    total = tok[...].astype(f32) + (attn + as_row(out_bias))
    resid[...] = total
    leave.append(pltpu.make_async_copy(resid, resid_h, sems.at[16]))
    leave[2].start()
    unit, _ = centre(total)
    mlp_low[...] = (unit * as_row(gain) + as_row(shift)).astype(bf16)
    for c in leave:
        c.wait()


def mlp_kernel(start, orders, block, me_ref, head_ref, *refs):
    if start == 0:
        own, oth, g, bias, up_h, down_h, a, up_later, down_later, *refs, up, down, sems = refs
        cut = down.shape[0]
        cuts = [pl.ds(0, cut), pl.ds(cut, cut)]
        copies = bring(
            [(up_h.at[:, cuts[0]], up), (down_h.at[cuts[0]], down)]
            + [(up_h.at[:, cuts[1]], up_later), (down_h.at[cuts[1]], down_later)],
            sems,
        )
        rows = own.shape[0]
        a[:rows], a[rows:] = own[...], oth[...]
    else:
        a, g, out_in, gmi_in, up, bias, down, out_send, gmi_send, *refs = refs
    out_acc, gmi_acc, keep, send, d_bias, scr_up, scr_down = refs
    core = head_ref[0]
    cut = d_bias.shape[0]
    units = pl.ds(start, cut)
    if start == 0:
        copies[0].wait()
        copies[1].wait()
    w_up, w_down = up[...], down[...]
    act, slope = gelu_parts(dot(a[...], w_up) + bias[units].astype(f32).reshape(1, cut))
    act = act.astype(bf16)
    grad = (dot(g[...], w_down, 1, 1) * slope).astype(bf16)
    ordered(dot(a[...], grad, 0, 0), scr_up, (keep, send), 0, orders, block, me_ref, core)
    ordered(dot(g[...], act, 0, 0), scr_down, (keep, send), cut, orders, block, me_ref, core)
    d_bias[...] = col_sum(grad.astype(f32)).reshape(cut)
    out, gmi = dot(act, w_down), dot(grad, w_up, 1, 1)
    if start == 0:
        out_acc[...], gmi_acc[...] = out, gmi
        copies[2].wait()
        copies[3].wait()
        return
    rows = out_acc.shape[0]
    out, gmi = out_in[...] + out, gmi_in[...] + gmi
    out_acc[...], gmi_acc[...] = out[:rows], gmi[:rows]
    out_send[...], gmi_send[...] = out[rows:].astype(bf16), gmi[rows:].astype(bf16)


def slot_row(orders, slot, core, me_ref, block):
    first, second = orders[0][slot], orders[1][slot]
    offset = first if first == second else jnp.where(core == 0, first, second)
    return (me_ref[0] ^ offset) * block


def ordered(value, scr, dests, col, orders, block, me_ref, core):
    each, cols = value.shape[0] // len(dests), pl.ds(col, value.shape[1])
    if block % 16:
        for i, dest in enumerate(dests):
            dest[:, cols] = value[i * each : (i + 1) * each].astype(dest.dtype)
        return
    scr[...] = value.astype(scr.dtype)
    for slot in range(len(orders[0])):
        at = pl.multiple_of(slot_row(orders, slot, core, me_ref, block), 16)
        dest, row = dests[slot * block // each], slot * block % each
        dest[row : row + block, cols] = scr[pl.ds(at, block)].astype(dest.dtype)


def middle_kernel(
    n, seq, half, block, orders, me_ref, head_ref, gmi_own, gmi_got, resid, g_all, gain, w_out, ctx,
    grad_resid, gc_own, gc_oth, keep, send, sums, scr, cuts,
):
    unit, inv_std = centre(resid[...])
    gmi = gmi_own[...] + gmi_got[...].astype(f32)
    g_final = g_all[: gmi_own.shape[0]].astype(f32)
    total = g_final + norm_back(gmi, unit, inv_std, as_row(gain))
    grad_resid[...] = total
    low = total.astype(bf16)
    sums[...] = jnp.zeros_like(sums)
    sums[0:1] = col_sum(gmi * unit)
    sums[1:2] = col_sum(gmi)
    sums[2:3] = col_sum(low.astype(f32))
    sums[3:4] = col_sum(g_final)
    own = pl.multiple_of(head_ref[0] * half, LANES)
    oth = pl.multiple_of((1 - head_ref[0]) * half, LANES)
    for dest, at in ((gc_own, own), (gc_oth, oth)):
        part = dot(low, w_out[pl.ds(at, half)], 1, 1)
        for i in range(n):
            dest[i] = part[i * seq : (i + 1) * seq].astype(bf16)
    scr[pl.ds(own, half)] = dot(ctx[:, :half], low, 0, 0)
    scr[pl.ds(oth, half)] = dot(ctx[:, half:], low, 0, 0)
    if block % 16:
        keep[...] = scr[:half].astype(bf16)
        send[...] = scr[half:].astype(bf16)
        return
    part = block // 2
    for dest, core in ((keep, head_ref[0]), (send, 1 - head_ref[0])):
        for slot in range(len(orders[0])):
            at = pl.multiple_of(slot_row(orders, slot, core, me_ref, block) + core * part, 8)
            cuts[slot * block : slot * block + part] = scr[pl.ds(at, part), :half]
            cuts[slot * block + part : (slot + 1) * block] = scr[pl.ds(at, part), half:]
        dest[...] = cuts[...].astype(bf16)


def back_kernel(n, seq, half, block, orders, other, len_ref, head_ref, me_ref, qkv, gc, lse, normed, *refs):
    if other:
        wo, dqkv, d_qk, d_v, sums, grads, scr_qk, scr_v = refs
        at_v = 0
        if wo.shape[1] == half:
            d_v[:, half:] = wo[...]
    else:
        dqkv, d_qk, sums, grads, scr_qk, scr_v = refs
        d_v, at_v = d_qk, 2 * half
    scale = 1.0 / math.sqrt(HEAD_DIM)
    lane = lax.broadcasted_iota(jnp.int32, (seq, LANES), 1)
    key = lax.broadcasted_iota(jnp.int32, (WORDS, 1), 0)
    first = head_ref[0] * n

    def step(hp, carry):
        off = pl.multiple_of(hp * LANES, LANES)
        for i in range(n):
            q2 = qkv[i, :, pl.ds(off, LANES)]
            k2 = qkv[i, :, pl.ds(half + off, LANES)]
            v2 = qkv[i, :, pl.ds(2 * half + off, LANES)]
            g2 = gc[i, :, pl.ds(off, LANES)]
            kt = k2.T
            key_ok = key < len_ref[first + i]
            dq, dk, dv = [], [], []
            for e in range(2):
                qm = half_mask(q2, lane, e) * jnp.asarray(scale, bf16)
                s = mask_words(dot(k2, qm, 1, 1), key_ok)
                p = jnp.exp(s - lse[i, pl.ds(2 * hp + e, 1), :])
                dp = dot(v2, half_mask(g2, lane, e), 1, 1)
                inner = jnp.sum(p * dp, axis=0, keepdims=True)
                ds = (p * (dp - inner)).astype(bf16)
                dv.append(dot(p.astype(bf16), g2))
                dk.append(dot(ds, q2))
                dq.append(dot(kt[e * HEAD_DIM : (e + 1) * HEAD_DIM], ds))
            rows = pl.ds(i * seq, seq)
            grads[rows, pl.ds(off, LANES)] = jnp.concatenate(dq, axis=0).T * scale
            grads[rows, pl.ds(half + off, LANES)] = jnp.where(lane < HEAD_DIM, dk[0], dk[1]) * scale
            grads[rows, pl.ds(2 * half + off, LANES)] = jnp.where(lane < HEAD_DIM, dv[0], dv[1])
        return carry

    lax.fori_loop(0, half // LANES, step, 0)
    low = grads[...].astype(bf16)
    dqkv[...] = low
    sums[...] = jnp.zeros_like(sums)
    sums[0:1] = col_sum(low[:, :half].astype(f32))
    sums[1:2] = col_sum(low[:, 2 * half :].astype(f32))
    core = 1 - head_ref[0] if other else head_ref[0]
    rows = normed[...]
    ordered(dot(rows, low[:, : 2 * half], 0, 0), scr_qk, (d_qk,), 0, orders, block, me_ref, core)
    ordered(dot(rows, low[:, 2 * half :], 0, 0), scr_v, (d_v,), at_v, orders, block, me_ref, core)


def last_kernel(
    half, head_ref, dq_own, dq_oth, w_own, w_oth, tok, gain, grad_resid, sums_mid, sums_own, sums_oth, up_first, up_second,
    grad_tokens, vecs,
):
    grad_tokens[...] = jnp.zeros_like(grad_tokens)

    def step(t, carry):
        at = pl.ds(pl.multiple_of(t * half, LANES), half)
        grad_tokens[...] += dot(dq_own[:, at], w_own[t], 1, 1) + dot(dq_oth[:, at], w_oth[t], 1, 1)
        return carry

    lax.fori_loop(0, 3, step, 0)
    grad = grad_tokens[...]
    unit, inv_std = centre(tok[...].astype(f32))
    width = 2 * half
    grad_tokens[...] = grad_resid[...] + norm_back(grad, unit, inv_std, as_row(gain))
    width = 2 * half
    vecs[...] = jnp.zeros_like(vecs)
    vecs[0:1, :width], vecs[0:1, width:] = col_sum(grad * unit), col_sum(grad)
    vecs[1:2, :width], vecs[1:2, width:] = sums_mid[0:1], sums_mid[1:2]
    vecs[2:3, :width], vecs[2:3, width:] = sums_mid[2:3], sums_mid[3:4]
    first = head_ref[0] == 0
    for i in range(2):
        own, oth = sums_own[i : i + 1], sums_oth[i : i + 1]
        vecs[3:4, i * width : i * width + half] = jnp.where(first, own, oth)
        vecs[3:4, i * width + half : (i + 1) * width] = jnp.where(first, oth, own)
    for place, sums in enumerate((up_first, up_second)):
        up = as_row(sums)
        cut = up.shape[1]
        for i in range(2):
            at = place * cut
            vecs[4 + i : 5 + i, at : at + cut] = jnp.where(head_ref[0] == i, up, jnp.zeros_like(up))


def by_rows(count, step, *bases):
    size = next((v for v in (48, 80) if count % v == 0), count)

    def body(i, carry):
        step(*[pl.ds(pl.multiple_of(base + i * size, 16), size) for base in (0, *bases)])
        return carry

    lax.fori_loop(0, count // size, body, 0)


def layer_kernel(resid, out_own, out_got, down_bias, layer_out):
    def step(at):
        total = resid[at] + (out_own[at] + out_got[at].astype(f32) + as_row(down_bias))
        layer_out[at] = total.astype(bf16)

    by_rows(resid.shape[0], step)


def spread_vectors(count, width, hidden, index, total, outs):
    lanes = total.shape[1]
    part = width // count // 2
    rolled = pltpu.roll(total, lanes - index * part, 1)
    for i in range(6):
        at = (i % 2) * width
        outs[i][...] = rolled[i // 2 : i // 2 + 1, at : at + part].reshape(part)
    for i in range(2):
        outs[6][i : i + 1] = rolled[3:4, i * width : i * width + part]
    part = hidden // count
    up = jnp.where(index < count, total[4:5], total[5:6])
    up = pltpu.roll(jnp.concatenate([up] * 8, axis=0), lanes - (index % count) * part, 1)
    outs[7][...] = up[0:1, :part].reshape(part)


def spread_kernel(count, width, hidden, index_ref, vec, vec_got, *outs):
    spread_vectors(count, width, hidden, index_ref[0], vec[...] + vec_got[...], outs)


def pack(vec):
    high = vec.astype(bf16).astype(f32)
    return jnp.concatenate([high, vec - high], axis=0).astype(bf16)


def unpack(rows):
    rows = rows.astype(f32)
    return rows[:8] + rows[8:]


def halve(have, got, keep, send):
    half = keep.shape[0]

    def step(at, low):
        keep[at] = have[at].astype(f32) + got[at].astype(f32)
        send[at] = (have[low].astype(f32) + got[low].astype(f32)).astype(bf16)

    by_rows(half, step, half)


def halve_kernel(have, got, keep, send):
    halve(have, got, keep, send)


def merge_kernel(have, got, own, oth_qk, oth_v, wo, keep, send, at_keep, at_a, at_b):
    halve(have, got, keep, send)
    half, cols, at = at_keep.shape[0], own.shape[1], oth_qk.shape[1]

    def step(here, low):
        at_keep[here, :at] = own[here, :at] + oth_qk[here].astype(f32)
        at_keep[here, at:cols] = own[here, at:] + oth_v[here, : cols - at].astype(f32)
        at_keep[here, cols:] = wo[here].astype(f32) + oth_v[here, cols - at :].astype(f32)
        at_a[here] = (own[low, :at] + oth_qk[low].astype(f32)).astype(bf16)
        at_b[here, : cols - at] = (own[low, at:] + oth_v[low, : cols - at].astype(f32)).astype(bf16)
        at_b[here, cols - at :] = (wo[low].astype(f32) + oth_v[low, cols - at :].astype(f32)).astype(bf16)

    by_rows(half, step, half)


def fan_kernel(have, got, *refs):
    vec, (keep, *sends) = (refs[0], refs[1:]) if len(refs) == 6 else (None, refs)
    block = keep.shape[0]
    keep[...] = have[:block] + got[:block].astype(f32)
    if vec is not None:
        vec_keep = sends.pop()
        total = vec[...] + unpack(got[4 * block : 4 * block + 16])
        vec_keep[...] = total
    for i, send in enumerate(sends):
        at = pl.ds((i + 1) * block, block)
        send[:block] = (have[at] + got[at].astype(f32)).astype(bf16)
        if vec is not None:
            send[block : block + 16] = pack(total)


def fourth_kernel(at_have, at_a, at_b, vec, vec_got, have, got, at_keep, at_send, vec_keep, keep, send):
    total = vec[...] + vec_got[...]
    vec_keep[...] = total
    half, cols = at_keep.shape[0], at_a.shape[1]

    def step(at, low):
        for part, here in ((at_a, pl.ds(0, cols)), (at_b, pl.ds(cols, cols))):
            at_keep[at, here] = at_have[at, here] + part[at].astype(f32)
            at_send[at, here] = (at_have[low, here] + part[low].astype(f32)).astype(bf16)

    by_rows(half, step, half)
    at_send[half : half + 16] = pack(total)
    halve(have, got, keep, send)


def wide_kernel(first, got1, second, got2, up, down):
    cut = first.shape[1] // 2
    one, two = first[...] + got1[...].astype(f32), second[...] + got2[...].astype(f32)
    up[:, :cut], up[:, cut:] = one[:, :cut], two[:, :cut]
    down[:, :cut], down[:, cut:] = one[:, cut:], two[:, cut:]


def finish_kernel(count, width, hidden, index_ref, have, vec, *refs):
    gots, (w_qkv, w_out, *outs) = refs[:3], refs[3:]
    block, half = have.shape[0], width // 2
    total = have[...] + sum(g[:block].astype(f32) for g in gots)
    for t in range(3):
        w_qkv[t] = total[:, t * half : (t + 1) * half]
    part = block // 2
    w_out[:, :half], w_out[:, half:] = total[:part, 3 * half :], total[part:, 3 * half :]
    vec = vec[...] + sum(unpack(g[block : block + 16]) for g in gots)
    spread_vectors(count, width, hidden, index_ref[0], vec, outs)


SMEM = pl.BlockSpec(memory_space=pltpu.SMEM)
HBM, VMEM = pltpu.HBM, pltpu.VMEM


def params(limit):
    return dict(
        compiler_params=pltpu.CompilerParams(vmem_limit_bytes=limit * MIB),
        cost_estimate=pl.CostEstimate(flops=0, bytes_accessed=MIB, transcendentals=0),
    )


def scratch_of(what):
    if what == 0:
        return pltpu.SemaphoreType.DMA
    if isinstance(what, int):
        return pltpu.SemaphoreType.DMA((what,))
    return (what[2] if len(what) > 2 else VMEM)(*what[:2])


def call(body, name, outs, scratch, scalars, args, limit):
    place = lambda where: pl.BlockSpec(memory_space=pltpu.HBM if where is HBM else pltpu.VMEM)
    outs = [(*o, None)[:3] for o in outs]
    args = [a if isinstance(a, tuple) else (a, None) for a in args]
    arrays = [pltpu.with_memory_space_constraint(a, pltpu.HBM) if w is HBM else a for a, w in args]
    return pl.pallas_call(
        body,
        name=name,
        out_shape=[jax.ShapeDtypeStruct(s, d) if w is None else w(s, d) for s, d, w in outs],
        in_specs=[SMEM] * len(scalars) + [place(w) for _, w in args],
        out_specs=[place(w) for *_, w in outs],
        scratch_shapes=[scratch_of(v) for v in scratch],
        **params(limit),
    )(*scalars, *arrays)


def slots(masks):
    offsets = [0]
    for mask in reversed(masks):
        offsets = offsets + [o ^ mask for o in offsets]
    return offsets


def arrange(blocks, places):
    return jnp.concatenate([lax.dynamic_slice_in_dim(blocks, at, 1, axis=0) for at in places], axis=0)


def per_device(
    tokens, cotangent, text_len, word_mask, attn_gain, attn_shift, w_qkv, qv_bias, w_out, out_bias,
    mlp_gain, mlp_shift, w_up, up_bias, w_down, down_bias,
):
    n, seq, width = tokens.shape
    half = w_qkv.shape[2]
    hidden = w_up.shape[1]
    rows = n * seq
    count = lax.axis_size("pairs")
    block = width // count
    head = lax.axis_index("heads")
    me = lax.axis_index("pairs")
    head_s, me_s = head.reshape(1), me.reshape(1)
    bits = count.bit_length() - 1
    order_a = [1 << b for b in range(bits)]
    order_b = order_a[1::-1] + order_a[2:]
    orders = (slots(order_a), slots(order_b))
    direct = bits == 4 and block % 16 == 0

    def exchange(send, stage, mask=None, swap=False):
        masks = [order[stage] if mask is None else mask for order in (order_a, order_b)]
        masks = masks[::-1] if swap else masks
        pairs = [(p * 2 + h, (p ^ masks[h]) * 2 + h) for p in range(count) for h in range(2)]
        return lax.ppermute(send, ("pairs", "heads"), pairs)

    tie = lax.optimization_barrier
    tok = tokens.reshape(rows, width)

    w_oth = lax.ppermute(w_qkv, "heads", SWAP)
    bias_oth = lax.ppermute(qv_bias, "heads", SWAP)
    words_oth = lax.ppermute(word_mask, "heads", SWAP)
    cot_oth = lax.ppermute(cotangent, "heads", SWAP)

    qkv_shape = ((n, seq, 3 * half), bf16)
    lse_shape = ((n, 8, seq), f32, VMEM)
    low_rows, high_rows = ((rows, width), bf16), ((rows, width), f32)
    vector = ((width,), f32)
    weights = ((3, width, half), bf16)
    bias = ((2, half), f32)
    lens = (text_len.shape, jnp.int32, pltpu.SMEM)
    attn_scratch = [qkv_shape, ((rows, 3 * half), f32), ((rows, half), f32)]
    normed, qkv_own, ctx_own, lse_own = call(
        functools.partial(first_kernel, n, seq, half),
        "attend_own",
        [(*low_rows, VMEM), (*qkv_shape, HBM), ((rows, half), bf16, VMEM), lse_shape],
        [lens, low_rows, vector, vector, bias, weights, *attn_scratch, 9],
        [head_s],
        [(v, HBM) for v in (text_len, tok, attn_gain, attn_shift, qv_bias, w_qkv)],
        40,
    )
    w_oth, bias_oth, words_oth, cot_oth, normed = tie((w_oth, bias_oth, words_oth, cot_oth, normed))
    qkv_oth, ctx, lse_oth, resid, mlp_low, g_all = call(
        functools.partial(second_kernel, n, seq, half),
        "attend_other",
        [
            (*qkv_shape, HBM),
            (*low_rows, HBM),
            lse_shape,
            (*high_rows, HBM),
            (*low_rows, VMEM),
            ((2 * rows, width), bf16, VMEM),
        ],
        [
            lens, bias, weights, *[((n, seq, width), bf16)] * 2, *[(word_mask.shape, jnp.int32)] * 2, low_rows,
            ((width, width), bf16), vector, vector, vector, low_rows, high_rows, *attn_scratch,
            ((2 * rows, width), f32), 17,
        ],
        [head_s],
        [normed, ctx_own]
        + [
            (v, HBM)
            for v in (
                bias_oth, w_oth, text_len, cotangent, cot_oth, word_mask, words_oth, tok, w_out, out_bias, mlp_gain,
                mlp_shift,
            )
        ],
        26,
    )
    mlp_oth = lax.ppermute(mlp_low, "heads", SWAP)

    cut = hidden // 2

    def mlp(name, start, outs, args):
        return call(
            functools.partial(mlp_kernel, start, orders, block),
            name,
            outs + [((width // 2, 2 * cut), bf16, VMEM)] * 2 + [((cut,), f32, VMEM)],
            [((width, cut), bf16)] * 2 + ([((width, cut), bf16), ((cut, width), bf16), 4] if start == 0 else []),
            [me_s, head_s],
            args,
            20,
        )

    a_all, up_later, down_later, out_part, gmi_part, c1, c1_send, up_first = mlp(
        "mlp_first",
        0,
        [((2 * rows, width), bf16, VMEM), ((width, cut), bf16, VMEM), ((cut, width), bf16, VMEM)]
        + [((2 * rows, width), f32, VMEM)] * 2,
        [mlp_low, mlp_oth, g_all, up_bias, (w_up, HBM), (w_down, HBM)],
    )
    c1_got = exchange(c1_send, 0) if direct else None
    out_send, gmi_send, out_own, gmi_own, c2, c2_send, up_second = mlp(
        "mlp_second",
        cut,
        [((rows, width), bf16)] * 2 + [((rows, width), f32)] * 2,
        [a_all, g_all, out_part, gmi_part, up_later, up_bias, down_later],
    )
    if direct:
        c2_got = exchange(c2_send, 0)
        add = lambda name, body, outs, args, scalars=(): call(body, name, outs, [], list(scalars), args, 4)
        unit = lambda size, kind: ((size * block, 2 * width), kind, VMEM)
    gmi_got = lax.ppermute(gmi_send, "heads", SWAP)
    out_got = lax.ppermute(out_send, "heads", SWAP)

    grad_resid, gc_own, gc_oth, wo_keep, wo_send, sums_mid = call(
        functools.partial(middle_kernel, n, seq, half, block, orders[::-1]),
        "middle",
        [
            (*high_rows, VMEM),
            ((n, seq, half), bf16, VMEM),
            ((n, seq, half), bf16, VMEM),
            *[((width, half) if block % 16 == 0 else (half, width), bf16, VMEM)] * 2,
            ((8, width), f32, VMEM),
        ],
        [((width, width), f32), ((width, half), f32)],
        [me_s, head_s],
        [gmi_own, gmi_got, resid, g_all, mlp_gain, w_out, ctx],
        8,
    )
    if direct:
        c1_got, gc_oth = tie((c1_got, gc_oth))
        c1, c1_send = add("add_1", halve_kernel, [unit(4, f32), unit(4, bf16)], [c1, c1_got])
        qkv_oth, c1_send = tie((qkv_oth, c1_send))
        c1_got = exchange(c1_send, 1)

    def back(name, qkv, gc, lse, other, kind, sizes, more):
        return call(
            functools.partial(back_kernel, n, seq, half, block, orders[::-1], other),
            name,
            [((rows, 3 * half), bf16, VMEM), *[((width, v), kind, VMEM) for v in sizes], ((8, half), f32, VMEM)],
            [((rows, 3 * half), f32), ((width, 2 * half), kind), ((width, half), kind)],
            [text_len, head_s, me_s],
            [qkv, gc, lse, normed, *more],
            12,
        )

    dq_oth, *d_oth, sums_oth = back("back_other", qkv_oth, gc_oth, lse_oth, True, bf16, (width, width), [wo_send])
    d_got = [lax.ppermute(d, "heads", SWAP) for d in d_oth]
    dq_own, d_own, sums_own = back("back_own", qkv_own, gc_own, lse_own, False, f32, (3 * half,), [])
    if direct:
        c1_got, c2_got, d_own, dq_own = tie((c1_got, c2_got, d_own, dq_own))
        c1, c1_send = add("add_z", halve_kernel, [unit(2, f32), unit(2, bf16)], [c1, c1_got])
        d_own, c1_send, *d_got = tie((d_own, c1_send, *d_got))
        c2, c2_send, at_sum, *at_sends = add(
            "add_2",
            merge_kernel,
            [unit(4, f32), unit(4, bf16), unit(8, f32)] + [((8 * block, width), bf16, VMEM)] * 2,
            [c2, c2_got, d_own, *d_got, wo_keep],
        )
        dq_own, c2_send, c1_send, *at_sends = tie((dq_own, c2_send, c1_send, *at_sends))
        c2_got, at_gots = exchange(c2_send, 1), [exchange(v, 0, swap=True) for v in at_sends]
        c1_got = exchange(c1_send, 2)
    grad_tok, vecs = call(
        functools.partial(last_kernel, half),
        "last",
        [high_rows, ((8, 2 * width), f32, VMEM)],
        [],
        [head_s],
        [
            dq_own, dq_oth, w_qkv, w_oth, tok, attn_gain, grad_resid, sums_mid, sums_own, sums_oth, up_first, up_second,
        ],
        16,
    )
    if direct:
        c2_got, c1_got, vecs = tie((c2_got, c1_got, vecs))
        c2, c2_send = add("add_3", halve_kernel, [unit(2, f32), unit(2, bf16)], [c2, c2_got])
        c1, c1_send = add("add_y", halve_kernel, [unit(1, f32), unit(1, bf16)], [c1, c1_got])
        c2_got, c1_got = exchange(c2_send, 2), exchange(c1_send, 3)
        out_own, c2_send, c1_send, vecs = tie((out_own, c2_send, c1_send, vecs))
    vecs = vecs + lax.ppermute(vecs, "heads", SWAP)
    vecs_got = exchange(vecs, 0, swap=True)
    (layer_out,) = call(layer_kernel, "layer_out", [low_rows], [], [], [resid, out_own, out_got, down_bias], 8)
    part, up_part = width // count // 2, hidden // count
    index = (me * 2 + head).reshape(1)
    shares = [((part,), f32)] * 6 + [((2, part), f32), ((up_part,), f32)]
    if direct:
        c2_got, layer_out, vecs_got, c1_got, *at_gots = tie((c2_got, layer_out, vecs_got, c1_got, *at_gots))
        along = (order_a[3], order_a[2], order_a[2] ^ order_a[3])
        vec_shape = (vecs.shape, f32, VMEM)
        tall = lambda size: ((size * block + 16, 2 * width), bf16, VMEM)
        at_sum, at_send, vecs, c2, c2_send = add(
            "add_4",
            fourth_kernel,
            [unit(4, f32), tall(4), vec_shape, unit(1, f32), unit(1, bf16)],
            [at_sum, *at_gots, vecs, vecs_got, c2, c2_got],
        )
        at_got, c2_got = tie((exchange(at_send, 1, swap=True), exchange(c2_send, 3)))
        at_sum, *sends, vecs = add(
            "add_5", fan_kernel, [unit(1, f32)] + [tall(1)] * 3 + [vec_shape], [at_sum, at_got, vecs]
        )
        gots = [exchange(sends[i], 2, along[i]) for i in (0, 2, 1)]
        grad_w_up, grad_w_down = add(
            "add_wide", wide_kernel, [((block, hidden), f32)] * 2, [c1, c1_got, c2, c2_got]
        )
        grad_w_up, grad_w_down, *gots = tie((grad_w_up, grad_w_down, *gots))
        grad_w_qkv, grad_w_out, *piece = add(
            "finish",
            functools.partial(finish_kernel, count, width, hidden),
            [((3, block, half), f32), ((block // 2, width), f32)] + shares,
            [at_sum, vecs, *gots],
            [index],
        )
        grad_w_down = grad_w_down.T
    else:
        places = [me ^ jnp.where(head == 0, a, b) for a, b in zip(*orders)]
        here = lambda v: arrange(v.reshape(count, block, -1), places)

        def pair_sum(total):
            for stage in range(bits):
                at = total.shape[0] // 2
                total = total[:at].astype(f32) + exchange(total[at:].astype(bf16), stage).astype(f32)
            return total[0]

        c1, c2 = [pair_sum(here(jnp.concatenate(c))) for c in ((c1, c1_send), (c2, c2_send))]
        grad_w_up = jnp.concatenate([c1[:, :cut], c2[:, :cut]], axis=1)
        grad_w_down = jnp.concatenate([c1[:, cut:], c2[:, cut:]], axis=1).T
        grad_qkv = pair_sum(here(d_own + jnp.concatenate(d_got, axis=1)[:, : 3 * half].astype(f32)))
        grad_w_qkv = jnp.stack([grad_qkv[:, t * half : (t + 1) * half] for t in range(3)])
        wo = jnp.concatenate([wo_keep, wo_send], axis=0).reshape(count, 2, block // 2, width)
        mine, theirs = [lax.dynamic_index_in_dim(wo, c, 1, keepdims=False) for c in (head, 1 - head)]
        wo = mine.astype(f32) + lax.ppermute(theirs, "heads", SWAP).astype(f32)
        grad_w_out = pair_sum(arrange(wo, places))
        for stage in range(1, bits):
            vecs = vecs + vecs_got
            vecs_got = exchange(vecs, stage, swap=True)
        piece = call(
            functools.partial(spread_kernel, count, width, hidden), "spread", shares, [], [index], [vecs, vecs_got], 4
        )
    return (
        layer_out.reshape(n, seq, width),
        grad_tok.reshape(n, seq, width),
        piece[0],
        piece[1],
        grad_w_qkv,
        piece[6],
        grad_w_out,
        piece[4],
        piece[2],
        piece[3],
        grad_w_up,
        piece[7],
        grad_w_down,
        piece[5],
    )


def solution(mesh):
    in_specs = (
        P(("pairs", "heads"), None, None),
        P(("pairs", "heads"), None, None),
        P("pairs"),
        P(("pairs", "heads"), None),
        P(),
        P(),
        P(None, None, "heads"),
        P(None, "heads"),
        P(),
        P(),
        P(),
        P(),
        P(None, "heads"),
        P("heads"),
        P("heads", None),
        P(),
    )
    out_specs = (
        P(("pairs", "heads"), None, None),
        P(("pairs", "heads"), None, None),
        P(("pairs", "heads")),
        P(("pairs", "heads")),
        P(None, "pairs", "heads"),
        P(None, ("pairs", "heads")),
        P(("pairs", "heads"), None),
        P(("pairs", "heads")),
        P(("pairs", "heads")),
        P(("pairs", "heads")),
        P("pairs", "heads"),
        P(("pairs", "heads")),
        P("heads", "pairs"),
        P(("pairs", "heads")),
    )
    return jax.shard_map(
        per_device, mesh=mesh, in_specs=in_specs, out_specs=out_specs, check_vma=False
    )
```
